32 devices in a mesh: rep: 2 (over y), own: 4 (over z), tp: 2 (over x), sub: 2 (over core).
Axes of the slice: x: 2, y: 2, z: 4, core: 2. Of those that a mesh axis runs over, the one named last changes fastest.
Arguments:
- tokens: bfloat16 [8192, 5120], P(('rep', 'own', 'sub'), 'tp'), parts along dimension 0, may hold values from -6 to 6
- grad_output: bfloat16 [8192, 1024], P(('rep', 'own', 'sub'), 'tp'), parts along dimension 0, may hold values from -6 to 6
- frozen_value: bfloat16 [5120, 1024], P('tp', 'sub'), may hold values from -0.078125 to 0.078125
- shared_down: bfloat16 [5120, 64], P('tp'), may hold values from -0.078125 to 0.078125
- head_up: bfloat16 [64, 64, 1024], P('own', None, 'tp'), may hold values from -0.1875 to 0.1875
- adapter_ids: int32 [16], P('rep'), parts along dimension 0, may hold values from 0 to 63
- lengths: int32 [16], P(('rep', 'own', 'sub')), parts along dimension 0, may hold values from 1 to 512, 3072 in all
Outputs:
- input_gradient: bfloat16 [8192, 5120], P(('rep', 'own', 'sub'), 'tp'), parts along dimension 0
- shared_down_gradient: float32 [10240, 64], P(('rep', 'tp')), parts along dimension 0
- grad_heads: float32 [128, 64, 1024], P(('rep', 'own'), None, 'tp'), parts along dimension 0
The draws below stay inside these ranges and needn't reach their ends.
There are 2 independent parts, one for each index of `rep`. The reference program is written for one: setup_inputs(seed, part) draws one part's arguments, and reference() takes and returns one part's arrays. A program takes and returns all parts, laid end to end along the dimension named above; an argument that names none is the same for every part. Nothing has to cross between parts.
All inputs are finite; a program needn't handle non-finite values. No bound on the sum of `lengths` on one device may be relied on, other than what follows from the above.
Results may differ from the reference program's by a relative error of at most 0.0034.
Values may be sent and summed in bfloat16 or wider, within the bound.
No kernel may reach another device: no remote copies, remote signals or barrier semaphores. Data moves between devices by JAX's collectives and lax.ppermute only.
A program may use at most 64 MiB of HBM per device.

```python
import math
import jax
import jax.numpy as jnp
import numpy as np
from jax import lax

D = 5120
KV = 1024
R = 64
PAIR_LENGTH = 512
ADAPTERS = 64
PAIRS = 8
TOKENS = 4096


def with_ends(array, key, low, high):
    longest = array.shape.index(max(array.shape))
    spots = []
    for shift in (0, 1):
        where = [jax.random.randint(jax.random.fold_in(key, axis), (), 0, length) for axis, length in enumerate(array.shape)]
        where[longest] = (where[longest] + shift) % array.shape[longest]
        spots.append(tuple(where))
    return array.at[spots[0]].set(low).at[spots[1]].set(high)


def levels(own_key, dims, cuts, low, largest):
    def one(position, shards_of):
        steps = jax.random.uniform(jax.random.fold_in(jax.random.fold_in(own_key, 6), position), (shards_of,), jnp.float32, low / len(cuts), largest / len(cuts))
        return jnp.repeat(jnp.exp(steps), dims[position] // shards_of).reshape((-1,) + (1,) * (len(dims) - position - 1))

    level = one(*cuts[0])
    for cut in cuts[1:]:
        level = level * one(*cut)
    return level


def rank_table(number_of, skew):
    portions = [(1 << 20) // math.isqrt(standing ** skew) + 1 for standing in range(1, number_of + 1)]
    spread = 1 + sum(portions) // (1 << 30)
    return np.cumsum(np.array([max(1, weight // spread) for weight in portions]))


def ranked(rng, dims, amount, lean):
    grid = rank_table(amount, lean)
    lot = jax.random.randint(jax.random.fold_in(rng, 1), dims, 0, int(grid[amount - 1]))
    grade = jnp.searchsorted(jnp.asarray(grid, jnp.int32), lot, side="right")
    return jax.random.permutation(jax.random.fold_in(rng, 2), amount)[grade].astype(jnp.int32)


def profile(count, total, limit, lean):
    portions = [(1 << 20) // math.isqrt(standing ** lean) + 1 for standing in range(2, count + 1)]
    rest, holding = total - limit - (count - 1), [1] * (count - 1)
    while rest > 0:
        movable = [i for i in range(count - 1) if holding[i] < limit]
        whole, budget = sum([portions[i] for i in movable]), rest
        for i in movable:
            extra = min(limit - holding[i], max(1, budget * portions[i] // whole), rest)
            holding[i] = holding[i] + extra
            rest = rest - extra
    return np.array([limit] + holding)


def uneven_parts(own_key, number_of, total, most, slope):
    if number_of == 2:
        one = jax.random.randint(own_key, (), max(1, total - most), min(most, total - 1) + 1)
        return jnp.stack([one, total - one])
    sizes = jnp.asarray(profile(number_of, total, most, slope), jnp.int32)
    pairs = (number_of - 1) // 2
    giver, receiver = sizes[1:1 + 2 * pairs:2], sizes[2:2 + 2 * pairs:2]
    slack = jnp.minimum(giver - 1, most - receiver)
    shifted = jax.random.randint(jax.random.fold_in(own_key, 1), (pairs,), 0, 1 << 20) % (slack + 1)
    sizes = sizes.at[1:1 + 2 * pairs:2].set(giver - shifted).at[2:2 + 2 * pairs:2].set(receiver + shifted)
    return sizes[jax.random.permutation(jax.random.fold_in(own_key, 2), number_of)]


def normal_values(own_key, dims, deviation, reach, shards=(), kind=jnp.bfloat16):
    values = deviation * jax.random.normal(own_key, dims, jnp.float32)
    if shards:
        values = values * levels(own_key, dims, shards, -0.22, 0.18)
    return jnp.clip(values, -reach, reach).astype(kind)


def setup_inputs(seed: int = 0, part: int = 0) -> dict:
    key_list = jax.random.split(jax.random.key(seed), 8)
    own_keys = jax.random.split(jax.random.fold_in(key_list[7], part), 8)
    return {
        "tokens": normal_values(own_keys[0], (TOKENS, D), 1.0, 6.0, ((0, 8), (1, 2))),
        "grad_output": normal_values(own_keys[1], (TOKENS, KV), 1.0, 6.0, ((0, 8), (1, 2))),
        "frozen_value": normal_values(key_list[2], (D, KV), D ** -0.5, 0.078125, ((0, 2), (1, 2))),
        "shared_down": normal_values(key_list[3], (D, R), D ** -0.5, 0.078125, ((0, 2),)),
        "head_up": normal_values(key_list[4], (ADAPTERS, R, KV), KV ** -0.5, 0.1875, ((0, 4), (2, 2))),
        "adapter_ids": with_ends(ranked(own_keys[5], (PAIRS,), ADAPTERS, 2), jax.random.fold_in(own_keys[5], 3), 0, ADAPTERS - 1).astype(jnp.int32),
        "lengths": uneven_parts(own_keys[6], PAIRS, PAIRS * PAIR_LENGTH * 3 // 4, PAIR_LENGTH, 2).astype(jnp.int32),
    }


adapter_scale = 2.0


def reference(tokens, grad_output, frozen_value, shared_down, head_up, adapter_ids, lengths):
    pair_count = lengths.shape[0]
    positions = jnp.arange(PAIR_LENGTH, dtype=jnp.int32)
    keep_rows = (positions[None, :] < lengths[:, None]).reshape(pair_count * PAIR_LENGTH)
    kept_grad = jnp.where(keep_rows[:, None], grad_output, jnp.zeros_like(grad_output))
    low_rank = jnp.dot(tokens, shared_down, preferred_element_type=jnp.float32).astype(jnp.bfloat16)
    chosen = jnp.take(head_up, adapter_ids, axis=0).astype(jnp.float32)
    retained_pairs = kept_grad.reshape(pair_count, PAIR_LENGTH, KV).astype(jnp.float32)
    rank_backward = jnp.einsum("plc,prc->plr", retained_pairs, chosen).reshape(pair_count * PAIR_LENGTH, R).astype(jnp.bfloat16)
    frozen_value_term = jnp.dot(kept_grad, frozen_value.T, preferred_element_type=jnp.float32)
    adapter_side_term = jnp.dot(rank_backward, shared_down.T, preferred_element_type=jnp.float32)
    input_gradient = (frozen_value_term + adapter_scale * adapter_side_term).astype(jnp.bfloat16)
    shared_down_gradient = (adapter_scale / PAIR_LENGTH) * jnp.dot(tokens.T, rank_backward, preferred_element_type=jnp.float32)
    rank_pair_rows = low_rank.reshape(pair_count, PAIR_LENGTH, R).astype(jnp.float32)
    head_partials = (adapter_scale / PAIR_LENGTH) * jnp.einsum("mxy,mxb->myb", rank_pair_rows, retained_pairs)
    owners = (adapter_ids[None, :] == jnp.arange(ADAPTERS, dtype=jnp.int32)[:, None]).astype(jnp.float32)
    grad_heads = jnp.einsum("ap,prc->arc", owners, head_partials, precision=lax.Precision.HIGHEST)
    return (input_gradient, shared_down_gradient, grad_heads)
```

```python
import functools

import jax
import jax.numpy as jnp
from jax import lax
from jax.experimental import pallas as pl
from jax.experimental.pallas import tpu as pltpu
from jax.sharding import PartitionSpec as P

adapter_scale = 2.0
f32 = jnp.float32
bf16 = jnp.bfloat16

OWN, SUB, TP, LENGTH, IDS = 0, 1, 2, 3, 4


def shift(x, axis, step):
    count = lax.axis_size(axis)
    return lax.ppermute(x, axis, [(i, (i + step) % count) for i in range(count)])


def width_of(whole):
    for width in (512, 256, 128):
        if whole % width == 0:
            return width
    return whole


def whole(shape):
    return pl.BlockSpec(shape, lambda i, info: (0,) * len(shape))


def call(body, info, operands, in_specs, out_specs, out_shape, grid, scratch=(), flops=0):
    moved = sum(x.size * x.dtype.itemsize for x in list(operands) + list(out_shape))
    return pl.pallas_call(
        body,
        out_shape=out_shape,
        grid_spec=pltpu.PrefetchScalarGridSpec(
            num_scalar_prefetch=1,
            grid=grid,
            in_specs=in_specs,
            out_specs=out_specs,
            scratch_shapes=scratch,
        ),
        compiler_params=pltpu.CompilerParams(vmem_limit_bytes=40 * 1024 * 1024),
        cost_estimate=pl.CostEstimate(flops=flops, bytes_accessed=moved, transcendentals=0),
    )(info, *operands)


def shape_of(dims, kind):
    return jax.ShapeDtypeStruct(dims, kind)


def pick_heads(info, head_up, own_count, sub_count):
    per_owner, rank, width = head_up.shape

    def place(step):
        def index(i, info):
            target = lax.rem(info[OWN] + step, own_count) * sub_count + info[SUB]
            local = info[IDS + target] - info[OWN] * per_owner
            return jnp.clip(local, 0, per_owner - 1), 0, 0

        return index

    def body(info, *refs):
        for source, target in zip(refs[:own_count], refs[own_count:]):
            target[...] = source[0]

    return call(
        body,
        info,
        [head_up] * own_count,
        [pl.BlockSpec((1, rank, width), place(step)) for step in range(own_count)],
        [whole((rank, width))] * own_count,
        [shape_of((rank, width), bf16)] * own_count,
        (1,),
    )


def project_low(info, tokens, down):
    rows, features = tokens.shape
    rank = down.shape[0]
    width = width_of(features)

    def body(info, tokens, down, low):
        part = lax.dot_general(
            down[...], tokens[...], (((1,), (1,)), ((), ())), preferred_element_type=f32
        )

        @pl.when(pl.program_id(0) == 0)
        def _():
            low[...] = part

        @pl.when(pl.program_id(0) > 0)
        def _():
            low[...] += part

    return call(
        body,
        info,
        [tokens, down],
        [
            pl.BlockSpec((rows, width), lambda i, info: (0, i)),
            pl.BlockSpec((rank, width), lambda i, info: (0, i)),
        ],
        [whole((rank, rows))],
        [shape_of((rank, rows), f32)],
        (features // width,),
        flops=2 * rows * rank * features,
    )[0]


def head_term(info, lows, grad, scale):
    rank, rows = lows[0].shape
    columns = grad.shape[1]

    def body(info, *refs):
        *lows, grad, term = refs
        total = lows[0][...]
        for low in lows[1:]:
            total = total + low[...]
        live = lax.broadcasted_iota(jnp.int32, total.shape, 1) < info[LENGTH]
        kept = jnp.where(live, total, 0.0).astype(bf16)
        term[...] = (scale * jnp.dot(kept, grad[...], preferred_element_type=f32)).astype(bf16)

    return call(
        body,
        info,
        list(lows) + [grad],
        [whole((rank, rows))] * len(lows) + [whole((rows, columns))],
        [whole((rank, columns))],
        [shape_of((rank, columns), bf16)],
        (1,),
        flops=2 * rows * rank * columns,
    )[0]


def back_and_shared(info, grads, heads, tokens, scale, sub_count):
    rows, features = tokens.shape
    rank, columns = heads[0].shape
    parts = len(grads)
    width = width_of(features)
    share = rank // sub_count

    def body(info, *refs):
        grads, heads = refs[:parts], refs[parts : 2 * parts]
        tokens, back, keep, send, total = refs[2 * parts :]

        @pl.when(pl.program_id(0) == 0)
        def _():
            both = None
            for grad, head in zip(grads, heads):
                part = lax.dot_general(
                    head[...], grad[...], (((1,), (1,)), ((), ())), preferred_element_type=f32
                )
                both = part if both is None else both + part
            live = lax.broadcasted_iota(jnp.int32, both.shape, 1) < info[LENGTH]
            back[...] = jnp.where(live, both, 0.0).astype(bf16)

        total[...] = scale * jnp.dot(back[...], tokens[...], preferred_element_type=f32)
        mine = pl.multiple_of(info[SUB] * share, share)
        other = pl.multiple_of((1 - info[SUB]) * share, share)
        keep[...] = total[pl.ds(mine, share), :]
        send[...] = total[pl.ds(other, share), :]

    return call(
        body,
        info,
        list(grads) + list(heads) + [tokens],
        [whole((rows, columns))] * parts
        + [whole((rank, columns))] * parts
        + [pl.BlockSpec((rows, width), lambda i, info: (0, i))],
        [whole((rank, rows))] + [pl.BlockSpec((share, width), lambda i, info: (0, i))] * 2,
        [shape_of((rank, rows), bf16)] + [shape_of((share, features), f32)] * 2,
        (features // width,),
        scratch=[pltpu.VMEM((rank, width), f32)],
        flops=2 * rows * rank * (features + parts * columns),
    )


def cut_shares(info, keep, arrived, own_count):
    share, features = keep.shape
    per = share // own_count

    def body(info, keep, arrived, mine, *rest):
        sends, total = rest[:-1], rest[-1]
        total[...] = keep[...] + arrived[...]
        for step in range(own_count):
            place = lax.rem(info[OWN] + step, own_count) * per
            if per % 8 == 0:
                place = pl.multiple_of(place, 8)
            piece = total[pl.ds(place, per), :]
            if step == 0:
                mine[...] = piece
            else:
                sends[step - 1][...] = piece.astype(bf16)

    return call(
        body,
        info,
        [keep, arrived],
        [whole((share, features))] * 2,
        [whole((per, features))] * own_count,
        [shape_of((per, features), f32)] + [shape_of((per, features), bf16)] * (own_count - 1),
        (1,),
        scratch=[pltpu.VMEM((share, features), f32)],
    )


def add_shares(info, mine, arrived):
    def body(info, mine, *refs):
        total = mine[...]
        for piece in refs[:-1]:
            total = total + piece[...].astype(f32)
        refs[-1][...] = total.astype(bf16)

    return call(
        body,
        info,
        [mine] + list(arrived),
        [whole(mine.shape)] * (1 + len(arrived)),
        [whole(mine.shape)],
        [shape_of(mine.shape, bf16)],
        (1,),
    )[0]


def join_shares(info, near, far, own_count):
    per, features = near[0].shape
    share = per * own_count

    def body(info, *refs):
        out = refs[-1]
        for step in range(own_count):
            owner = lax.rem(info[OWN] + own_count - step, own_count)
            for side, piece in ((info[SUB], refs[step]), (1 - info[SUB], refs[own_count + step])):
                place = side * share + owner * per
                if per % 8 == 0:
                    place = pl.multiple_of(place, 8)
                out[pl.ds(place, per), :] = piece[...].astype(f32)

    return call(
        body,
        info,
        list(near) + list(far),
        [whole((per, features))] * (2 * own_count),
        [whole((2 * share, features))],
        [shape_of((2 * share, features), f32)],
        (1,),
    )[0]


def place_terms(info, near, far, per_owner, own_count, sub_count):
    rank, columns = near[0].shape
    group = 4 if per_owner % 4 == 0 else 1

    def body(info, *refs):
        out = refs[-1]
        for at in range(group):
            tenant = info[OWN] * per_owner + pl.program_id(0) * group + at
            total = jnp.zeros((rank, columns), f32)
            for step in range(own_count):
                first = lax.rem(info[OWN] + own_count - step, own_count) * sub_count
                one = info[IDS + first + info[SUB]] == tenant
                two = info[IDS + first + 1 - info[SUB]] == tenant
                total = total + (
                    jnp.where(one, refs[step][...].astype(f32), 0.0)
                    + jnp.where(two, refs[own_count + step][...].astype(f32), 0.0)
                )
            out[at] = total

    return call(
        body,
        info,
        list(near) + list(far),
        [whole((rank, columns))] * (2 * own_count),
        [pl.BlockSpec((group, rank, columns), lambda i, info: (i, 0, 0))],
        [shape_of((per_owner, rank, columns), f32)],
        (per_owner // group,),
    )[0]


def input_side(info, grads, frozen, frozen_other, back, down):
    rows, columns = grads[0].shape
    features, half = frozen.shape
    rank = back.shape[0]
    parts = len(grads)
    width = width_of(features)

    def body(info, *refs):
        grads = refs[:parts]
        frozen, frozen_other, back, down, out, kept = refs[parts:]

        @pl.when(pl.program_id(0) == 0)
        def _():
            live = lax.broadcasted_iota(jnp.int32, (rows, columns), 0) < info[LENGTH]
            for step, grad in enumerate(grads):
                place = lax.rem(info[TP] + parts - step, parts) * columns
                kept[:, pl.ds(pl.multiple_of(place, 128), columns)] = jnp.where(
                    live, grad[...], jnp.zeros((rows, columns), bf16)
                )

        both = (((1,), (1,)), ((), ()))
        mine = pl.multiple_of(info[SUB] * half, 128)
        other = pl.multiple_of((1 - info[SUB]) * half, 128)
        total = lax.dot_general(
            kept[:, pl.ds(mine, half)], frozen[...], both, preferred_element_type=f32
        )
        total += lax.dot_general(
            kept[:, pl.ds(other, half)], frozen_other[...], both, preferred_element_type=f32
        )
        total += lax.dot_general(
            adapter_scale * back[...], down[...], (((0,), (0,)), ((), ())),
            preferred_element_type=f32,
        )
        out[...] = total.astype(bf16)

    return call(
        body,
        info,
        list(grads) + [frozen, frozen_other, back, down],
        [whole((rows, columns))] * parts
        + [pl.BlockSpec((width, half), lambda i, info: (i, 0))] * 2
        + [whole((rank, rows)), pl.BlockSpec((rank, width), lambda i, info: (0, i))],
        [pl.BlockSpec((rows, width), lambda i, info: (0, i))],
        [shape_of((rows, features), bf16)],
        (features // width,),
        scratch=[pltpu.VMEM((rows, parts * columns), bf16)],
        flops=2 * rows * features * (2 * half + rank),
    )[0]


def on_device(tokens, grad_output, frozen_value, shared_down, head_up, adapter_ids, lengths):
    rows = tokens.shape[0]
    own_count = lax.axis_size("own")
    sub_count = lax.axis_size("sub")
    tp_count = lax.axis_size("tp")
    per_owner = head_up.shape[0]
    scale = adapter_scale / rows

    frozen_other = shift(frozen_value, "sub", 1)
    grads = [grad_output] + [shift(grad_output, "tp", step) for step in range(1, tp_count)]

    own_at = lax.axis_index("own")
    place = jnp.stack([own_at, lax.axis_index("sub"), lax.axis_index("tp"), lengths[0]])
    info = jnp.concatenate([place.astype(jnp.int32), adapter_ids])
    down = shared_down.T

    picked = pick_heads(info, head_up, own_count, sub_count)
    offered = [picked[0]] + [shift(picked[step], "own", step) for step in range(1, own_count)]
    my_adapter = lax.dynamic_index_in_dim(
        adapter_ids, own_at * sub_count + lax.axis_index("sub"), 0, keepdims=False
    )
    away = lax.rem(own_at + own_count - my_adapter // per_owner, own_count)
    head = offered[0]
    for step in range(1, own_count):
        head = jnp.where(away == step, offered[step], head)
    heads = [head] + [shift(head, "tp", step) for step in range(1, tp_count)]

    low = project_low(info, tokens, down)
    lows = [low] + [shift(low, "tp", step) for step in range(1, tp_count)]
    term = head_term(info, lows, grad_output, scale)
    near = [term] + [shift(term, "own", step) for step in range(1, own_count)]
    far = [shift(piece, "sub", 1) for piece in near]

    back, keep, send = back_and_shared(info, grads, heads, tokens, scale, sub_count)
    arrived = shift(send, "sub", 1)
    mine, *sends = cut_shares(info, keep, arrived, own_count)
    pieces = [shift(piece, "own", step + 1) for step, piece in enumerate(sends)]
    share = add_shares(info, mine, pieces)
    near_shares = [share] + [shift(share, "own", step) for step in range(1, own_count)]
    far_shares = [shift(piece, "sub", 1) for piece in near_shares]

    input_gradient = input_side(info, grads, frozen_value, frozen_other, back, down)
    grad_heads = place_terms(info, near, far, per_owner, own_count, sub_count)
    shared_down_gradient = join_shares(info, near_shares, far_shares, own_count).T
    return (input_gradient, shared_down_gradient, grad_heads)


def solution(mesh):
    placed = (
        P(("rep", "own", "sub"), "tp"),
        P(("rep", "own", "sub"), "tp"),
        P("tp", "sub"),
        P("tp", None),
        P("own", None, "tp"),
        P("rep"),
        P(("rep", "own", "sub")),
    )
    return jax.shard_map(
        on_device,
        mesh=mesh,
        in_specs=placed,
        out_specs=(
            P(("rep", "own", "sub"), "tp"),
            P(("rep", "tp"), None),
            P(("rep", "own"), None, "tp"),
        ),
        check_vma=False,
    )
```

```python
import jax
import jax.numpy as jnp
from jax import lax
from jax.experimental import pallas as pl
from jax.experimental.pallas import tpu as pltpu
from jax.sharding import PartitionSpec as P

adapter_scale = 2.0
f32 = jnp.float32
bf16 = jnp.bfloat16

anywhere = pl.BlockSpec(memory_space=pl.ANY)
in_vmem = pl.BlockSpec(memory_space=pltpu.VMEM)
in_smem = pl.BlockSpec(memory_space=pltpu.SMEM)


def shift(x, axis, step):
    count = lax.axis_size(axis)
    return lax.ppermute(x, axis, [(i, (i + step) % count) for i in range(count)])


def swap(x, own_bit, sub_bit):
    subs = lax.axis_size("sub")
    whole = lax.axis_size("own") * subs
    other = own_bit * subs + sub_bit
    return lax.ppermute(x, ("own", "sub"), [(i, i ^ other) for i in range(whole)])


def shape_of(dims, kind):
    return jax.ShapeDtypeStruct(dims, kind)


def call(body, operands, specs, outs, out_specs=None, after=(), flops=0, **more):
    count = len(operands)

    def kernel(*refs):
        body(*refs[:count], *refs[count + len(after) :])

    moved = sum(x.size * x.dtype.itemsize for x in list(operands) + list(outs))
    return pl.pallas_call(
        kernel,
        out_shape=outs,
        in_specs=list(specs) + [anywhere] * len(after),
        out_specs=[in_vmem] * len(outs) if out_specs is None else out_specs,
        compiler_params=pltpu.CompilerParams(vmem_limit_bytes=24 * 1024 * 1024),
        cost_estimate=pl.CostEstimate(flops=flops, bytes_accessed=moved, transcendentals=0),
        **more,
    )(*operands, *after)


def pick_heads(adapter_ids, head_up, grad):
    per_owner, rank, width = head_up.shape
    own_count, sub_count = lax.axis_size("own"), lax.axis_size("sub")
    first = grad.shape[0] // 2

    def body(ids, head_up, grad, *refs):
        outs, early, sems = refs[:own_count], refs[own_count], refs[own_count + 1]
        own, sub = lax.axis_index("own"), lax.axis_index("sub")
        copies = []
        for step in range(own_count):
            target = lax.rem(own + step, own_count) * sub_count + sub
            local = jnp.clip(ids[target] - own * per_owner, 0, per_owner - 1)
            copies.append(pltpu.make_async_copy(head_up.at[local], outs[step], sems.at[step]))
        copies.append(
            pltpu.make_async_copy(grad.at[pl.ds(0, first)], early, sems.at[own_count])
        )
        for copy in copies:
            copy.start()
        for copy in copies:
            copy.wait()

    *picked, early = call(
        body,
        [adapter_ids, head_up, grad],
        [in_smem, anywhere, anywhere],
        [shape_of((rank, width), bf16)] * own_count + [shape_of((first, grad.shape[1]), bf16)],
        scratch_shapes=[pltpu.SemaphoreType.DMA((own_count + 1,))],
    )
    return picked, early


def project_low(tokens, down, after):
    rows, features = tokens.shape
    rank = down.shape[0]

    def body(tokens, down, low):
        low[...] = lax.dot_general(
            down[...], tokens[...], (((1,), (1,)), ((), ())), preferred_element_type=f32
        )

    return call(
        body,
        [tokens, down],
        [in_vmem] * 2,
        [shape_of((rank, rows), f32)],
        after=after,
        flops=2 * rows * rank * features,
    )[0]


def project_back(adapter_ids, offered, grad, per_owner, after):
    rank, columns = offered[0].shape
    rows = grad.shape[0]
    own_count, sub_count = lax.axis_size("own"), lax.axis_size("sub")
    first = rows // 2

    def body(ids, *refs):
        offered, grad, part, late, head = refs[:own_count], *refs[own_count:]
        own, sub = lax.axis_index("own"), lax.axis_index("sub")
        owner = lax.div(ids[own * sub_count + sub], per_owner)
        away = lax.rem(own + own_count - owner, own_count)
        for step in range(own_count):

            @pl.when(away == step)
            def _():
                head[...] = offered[step][...]

        part[...] = lax.dot_general(
            head[...], grad[...], (((1,), (1,)), ((), ())), preferred_element_type=f32
        )
        late[...] = grad[first:, :]

    return call(
        body,
        [adapter_ids, *offered, grad],
        [in_smem] + [in_vmem] * (own_count + 1),
        [shape_of((rank, rows), f32), shape_of((rows - first, columns), bf16)],
        after=after,
        scratch_shapes=[pltpu.VMEM((rank, columns), bf16)],
        flops=2 * rows * rank * columns,
    )


def head_term(lengths, lows, grad, scale, after):
    rank, rows = lows[0].shape
    columns = grad.shape[1]

    def body(lengths, *refs):
        *lows, grad, term = refs
        total = lows[0][...]
        for low in lows[1:]:
            total = total + low[...]
        live = lax.broadcasted_iota(jnp.int32, total.shape, 1) < lengths[0]
        kept = jnp.where(live, total, 0.0).astype(bf16)
        term[...] = (scale * jnp.dot(kept, grad[...], preferred_element_type=f32)).astype(bf16)

    return call(
        body,
        [lengths, *lows, grad],
        [in_smem] + [in_vmem] * (len(lows) + 1),
        [shape_of((rank, columns), bf16)],
        after=after,
        flops=2 * rows * rank * columns,
    )[0]


def share_of(own, sub):
    return sub * 2 + lax.rem(own, 2)


def shared_terms(lengths, parts, tokens, scale, after):
    rows, features = tokens.shape
    rank = parts[0].shape[0]
    share = rank // 4

    def body(lengths, *refs):
        parts, (tokens, back, mine, *sends, total) = refs[:count], refs[count:]
        own, sub = lax.axis_index("own"), lax.axis_index("sub")
        both = parts[0][...]
        for part in parts[1:]:
            both = both + part[...]
        live = lax.broadcasted_iota(jnp.int32, both.shape, 1) < lengths[0]
        back[...] = jnp.where(live, both, 0.0).astype(bf16)
        total[...] = scale * jnp.dot(back[...], tokens[...], preferred_element_type=f32)
        at = share_of(own, sub)

        def piece(flip):
            return total[pl.ds(pl.multiple_of((at ^ flip) * share, share), share), :]

        mine[...] = piece(0)
        for flip, send in zip((1, 2, 3), sends):
            send[...] = piece(flip).astype(bf16)

    count = len(parts)
    return call(
        body,
        [lengths, *parts, tokens],
        [in_smem] + [in_vmem] * (count + 1),
        [shape_of((rank, rows), bf16), shape_of((share, features), f32)]
        + [shape_of((share, features), bf16)] * 3,
        after=after,
        scratch_shapes=[pltpu.VMEM((rank, features), f32)],
        flops=2 * rows * rank * features,
    )


def add_up(pieces, after=()):
    def body(*refs):
        total = refs[0][...].astype(f32)
        for piece in refs[1:-1]:
            total = total + piece[...].astype(f32)
        refs[-1][...] = total.astype(bf16)

    return call(
        body,
        list(pieces),
        [in_vmem] * len(pieces),
        [shape_of(pieces[0].shape, bf16)],
        after=after,
    )[0]


def halve(pieces, bit):
    rows, features = pieces[0].shape
    half = rows // 2

    def body(*refs):
        total = refs[0][...].astype(f32)
        for piece in refs[1:-2]:
            total = total + piece[...].astype(f32)
        upper = lax.rem(lax.div(lax.axis_index("own"), bit), 2) == 1
        low, high = total[:half], total[half:]
        refs[-2][...] = jnp.where(upper, high, low)
        refs[-1][...] = jnp.where(upper, low, high).astype(bf16)

    return call(
        body,
        list(pieces),
        [in_vmem] * len(pieces),
        [shape_of((half, features), f32), shape_of((half, features), bf16)],
    )


def rejoin(mine, arrived, bit):
    rows, features = mine.shape

    def body(mine, arrived, out):
        upper = lax.rem(lax.div(lax.axis_index("own"), bit), 2) == 1
        one, two = mine[...].astype(f32), arrived[...].astype(f32)
        out[:rows] = jnp.where(upper, two, one).astype(bf16)
        out[rows:] = jnp.where(upper, one, two).astype(bf16)

    return call(
        body, [mine, arrived], [in_vmem] * 2, [shape_of((2 * rows, features), bf16)]
    )[0]


def join_shares(quarters, after):
    share, features = quarters[0].shape

    def body(*refs):
        out = refs[-1]
        at = share_of(lax.axis_index("own"), lax.axis_index("sub"))
        for flip in range(4):
            place = pl.multiple_of((at ^ flip) * share, share)
            out[pl.ds(place, share), :] = refs[flip][...].astype(f32)

    return call(
        body,
        quarters,
        [in_vmem] * 4,
        [shape_of((4 * share, features), f32)],
        after=after,
    )[0]


def pack_terms(near, after):
    def body(*refs):
        for at, piece in enumerate(refs[:-1]):
            refs[-1][at] = piece[...]

    return call(
        body,
        near,
        [in_vmem] * len(near),
        [shape_of((len(near),) + near[0].shape, bf16)],
        after=after,
    )[0]


def place_terms(adapter_ids, near, far, per_owner, after):
    own_count, rank, columns = near.shape
    sub_count = lax.axis_size("sub")
    group = 4 if per_owner % 4 == 0 else 1

    def body(ids, near, far, out):
        own, sub = lax.axis_index("own"), lax.axis_index("sub")
        for at in range(group):
            tenant = own * per_owner + pl.program_id(0) * group + at
            out[at] = jnp.zeros((rank, columns), f32)
            for step in range(own_count):
                first = lax.rem(own + own_count - step, own_count) * sub_count
                one = ids[first + sub] == tenant
                two = ids[first + 1 - sub] == tenant

                @pl.when(jnp.logical_or(one, two))
                def _():
                    out[at] += jnp.where(one, near[step].astype(f32), 0.0) + jnp.where(
                        two, far[step].astype(f32), 0.0
                    )

    every = pl.BlockSpec((own_count, rank, columns), lambda i: (0, 0, 0))
    return call(
        body,
        [adapter_ids, near, far],
        [in_smem, every, every],
        [shape_of((per_owner, rank, columns), f32)],
        out_specs=[pl.BlockSpec((group, rank, columns), lambda i: (i, 0, 0))],
        after=after,
        grid=(per_owner // group,),
    )[0]


def arrange(lengths, grad, others):
    rows, columns = grad.shape
    count = 1 + len(others) // 2
    first = rows // 2

    def body(lengths, grad, *refs):
        others, kept = refs[:-1], refs[-1]
        at = lax.axis_index("tp")
        live = lax.broadcasted_iota(jnp.int32, (rows, columns), 0) < lengths[0]
        zero = jnp.zeros((rows, columns), bf16)
        place = pl.multiple_of(at * columns, 128)
        kept[:, pl.ds(place, columns)] = jnp.where(live, grad[...], zero)
        for step in range(1, count):
            place = pl.multiple_of(lax.rem(at + count - step, count) * columns, 128)
            for base, piece in ((0, others[step - 1]), (first, others[count - 2 + step])):
                size = piece.shape[0]
                kept[base : base + size, pl.ds(place, columns)] = jnp.where(
                    live[base : base + size], piece[...], zero[base : base + size]
                )

    return call(
        body,
        [lengths, grad, *others],
        [in_smem] + [in_vmem] * (1 + len(others)),
        [shape_of((rows, count * columns), bf16)],
    )[0]


def input_side(kept, frozen, frozen_other, back, down, width, begin, count, before, after):
    rows, whole = kept.shape
    features, half = frozen.shape
    rank = back.shape[0]

    def body(*refs):
        kept, frozen, frozen_other, back, down = refs[:5]
        out = refs[-1]
        sub = lax.axis_index("sub")
        both = (((1,), (1,)), ((), ()))
        mine = pl.multiple_of(sub * half, 128)
        other = pl.multiple_of((1 - sub) * half, 128)
        total = lax.dot_general(
            kept[:, pl.ds(mine, half)], frozen[...], both, preferred_element_type=f32
        )
        total += lax.dot_general(
            kept[:, pl.ds(other, half)], frozen_other[...], both, preferred_element_type=f32
        )
        total += lax.dot_general(
            adapter_scale * back[...],
            down[...],
            (((0,), (0,)), ((), ())),
            preferred_element_type=f32,
        )
        out[...] = total.astype(bf16)

    held = [] if before is None else [before]
    return call(
        body,
        [kept, frozen, frozen_other, back, down] + held,
        [pl.BlockSpec((rows, whole), lambda i: (0, 0))]
        + [pl.BlockSpec((width, half), lambda i: (i + begin, 0))] * 2
        + [
            pl.BlockSpec((rank, rows), lambda i: (0, 0)),
            pl.BlockSpec((rank, width), lambda i: (0, i + begin)),
        ]
        + [anywhere] * len(held),
        [shape_of((rows, features), bf16)],
        out_specs=[pl.BlockSpec((rows, width), lambda i: (0, i + begin))],
        after=after,
        grid=(count,),
        input_output_aliases={5: 0} if held else {},
        flops=2 * rows * width * count * (2 * half + rank),
    )[0]


def on_device(tokens, grad_output, frozen_value, shared_down, head_up, adapter_ids, lengths):
    rows, features = tokens.shape
    own_count = lax.axis_size("own")
    tp_count = lax.axis_size("tp")
    per_owner = head_up.shape[0]
    scale = adapter_scale / rows
    down = shared_down.T
    tp_steps, own_steps = range(1, tp_count), range(1, own_count)

    frozen_other = shift(frozen_value, "sub", 1)
    picked, early = pick_heads(adapter_ids, head_up, grad_output)
    offered = [picked[0]] + [shift(picked[step], "own", step) for step in own_steps]
    early_grads = [shift(early, "tp", step) for step in tp_steps]

    low = project_low(tokens, down, [picked[0]])
    lows = [low] + [shift(low, "tp", step) for step in tp_steps]

    part, late = project_back(adapter_ids, offered, grad_output, per_owner, [low])
    parts = [part] + [shift(part, "tp", step) for step in tp_steps]
    late_grads = [shift(late, "tp", step) for step in tp_steps]

    term = head_term(lengths, lows, grad_output, scale, [part])
    near = [term] + [shift(term, "own", step) for step in own_steps]

    back, mine, *sends = shared_terms(lengths, parts, tokens, scale, [term])
    flips = ((1, 0), (0, 1), (1, 1))
    pieces = [mine] + [swap(send, *flip) for send, flip in zip(sends, flips)]

    near = pack_terms(near, [back])
    far = shift(near, "sub", 1)
    kept = arrange(lengths, grad_output, early_grads + late_grads)

    width = next(w for w in (512, 256, 128) if features % w == 0)
    blocks = features // width
    cut = max(1, blocks * 3 // 5)

    bits = [1 << i for i in range(1, own_count.bit_length() - 1)]
    for bit in bits[:-1]:
        stays, leaves = halve(pieces, bit)
        pieces = [stays, swap(leaves, bit, 0)]
    total = add_up(pieces, [near])
    input_gradient = input_side(
        kept, frozen_value, frozen_other, back, down, width, 0, cut, None, [total]
    )
    if bits:
        total = add_up([total, swap(total, bits[-1], 0)], [input_gradient])
    for bit in reversed(bits[:-1]):
        total = rejoin(total, swap(total, bit, 0), bit)
    quarters = [total] + [swap(total, *flip) for flip in flips]
    if cut < blocks:
        input_gradient = input_side(
            kept, frozen_value, frozen_other, back, down, width, cut, blocks - cut,
            input_gradient, [total],
        )
    grad_heads = place_terms(adapter_ids, near, far, per_owner, [total])
    shared_down_gradient = join_shares(quarters, [grad_heads]).T
    return (input_gradient, shared_down_gradient, grad_heads)


def solution(mesh):
    placed = (
        P(("rep", "own", "sub"), "tp"),
        P(("rep", "own", "sub"), "tp"),
        P("tp", "sub"),
        P("tp", None),
        P("own", None, "tp"),
        P("rep"),
        P(("rep", "own", "sub")),
    )
    return jax.shard_map(
        on_device,
        mesh=mesh,
        in_specs=placed,
        out_specs=(
            P(("rep", "own", "sub"), "tp"),
            P(("rep", "tp"), None),
            P(("rep", "own"), None, "tp"),
        ),
        check_vma=False,
    )
```

```python
import jax
import jax.numpy as jnp
from jax import lax
from jax.experimental import pallas as pl
from jax.experimental.pallas import tpu as pltpu
from jax.sharding import PartitionSpec as P

adapter_scale = 2.0
f32 = jnp.float32
bf16 = jnp.bfloat16

anywhere = pl.BlockSpec(memory_space=pl.ANY)
in_hbm = pl.BlockSpec(memory_space=pltpu.HBM)
in_vmem = pl.BlockSpec(memory_space=pltpu.VMEM)
in_smem = pl.BlockSpec(memory_space=pltpu.SMEM)


def shift(x, axis, step):
    count = lax.axis_size(axis)
    return lax.ppermute(x, axis, [(i, (i + step) % count) for i in range(count)])


def swap(x, own_bit, sub_bit):
    subs = lax.axis_size("sub")
    whole = lax.axis_size("own") * subs
    other = own_bit * subs + sub_bit
    return lax.ppermute(x, ("own", "sub"), [(i, i ^ other) for i in range(whole)])


def width_of(features):
    return next(width for width in (512, 256, 128) if features % width == 0)


def stay(x):
    return pltpu.with_memory_space_constraint(x, pltpu.HBM)


def shape_of(dims, kind):
    return jax.ShapeDtypeStruct(dims, kind)


def call(body, operands, specs, outs, out_specs=None, after=(), flops=0, **more):
    count, idle = len(operands), len(after)

    def kernel(*refs):
        body(*refs[:count], *refs[count + idle :])

    moved = sum(x.size * x.dtype.itemsize for x in list(operands) + list(outs))
    return pl.pallas_call(
        kernel,
        out_shape=outs,
        in_specs=list(specs) + [anywhere] * len(after),
        out_specs=[in_vmem] * len(outs) if out_specs is None else out_specs,
        compiler_params=pltpu.CompilerParams(vmem_limit_bytes=24 * 1024 * 1024),
        cost_estimate=pl.CostEstimate(flops=flops, bytes_accessed=moved, transcendentals=0),
        **more,
    )(*operands, *after)


def pick_heads(adapter_ids, head_up):
    per_owner, rank, width = head_up.shape
    own_count, sub_count = lax.axis_size("own"), lax.axis_size("sub")

    def body(ids_far, head_up, *refs):
        outs, ids, sems = refs[:own_count], refs[own_count], refs[own_count + 1]
        own, sub = lax.axis_index("own"), lax.axis_index("sub")
        fetch = pltpu.make_async_copy(ids_far, ids, sems.at[own_count])
        fetch.start()
        fetch.wait()
        copies = []
        for step in range(own_count):
            target = (own ^ step) * sub_count + sub
            local = jnp.clip(ids[target] - own * per_owner, 0, per_owner - 1)
            copies.append(pltpu.make_async_copy(head_up.at[local], outs[step], sems.at[step]))
        for copy in copies:
            copy.start()
        for copy in copies:
            copy.wait()

    return call(
        body,
        [stay(adapter_ids), stay(head_up)],
        [in_hbm] * 2,
        [shape_of((rank, width), bf16)] * own_count,
        scratch_shapes=[
            pltpu.SMEM(adapter_ids.shape, jnp.int32),
            pltpu.SemaphoreType.DMA((own_count + 1,)),
        ],
    )


def project_low(tokens, down, after):
    rows, features = tokens.shape
    rank = down.shape[0]
    width = width_of(features)
    blocks = features // width

    def body(tokens, down, low, near_tokens, near_down, sems):
        copies = [pltpu.make_async_copy(down, near_down, sems.at[blocks])]
        for at in range(blocks):
            here = pl.ds(at * width, width)
            copies.append(
                pltpu.make_async_copy(tokens.at[:, here], near_tokens.at[:, here], sems.at[at])
            )
        for copy in copies:
            copy.start()
        copies[0].wait()
        total = None
        for at in range(blocks):
            copies[at + 1].wait()
            here = slice(at * width, (at + 1) * width)
            part = lax.dot_general(
                near_down[:, here], near_tokens[:, here], (((1,), (1,)), ((), ())),
                preferred_element_type=f32,
            )
            total = part if total is None else total + part
        low[...] = total

    return call(
        body,
        [stay(tokens), stay(down)],
        [in_hbm] * 2,
        [shape_of((rank, rows), f32), shape_of(tokens.shape, bf16), shape_of(down.shape, bf16)],
        after=after,
        flops=2 * rows * rank * features,
        scratch_shapes=[pltpu.SemaphoreType.DMA((blocks + 1,))],
    )


def project_back(adapter_ids, offered, grad, per_owner, after):
    rank, columns = offered[0].shape
    rows = grad.shape[0]
    own_count, sub_count = lax.axis_size("own"), lax.axis_size("sub")

    def body(ids, *refs):
        offered, grad, part, head = refs[:own_count], *refs[own_count:]
        own, sub = lax.axis_index("own"), lax.axis_index("sub")
        away = lax.div(ids[own * sub_count + sub], per_owner) ^ own
        for step in range(own_count):

            @pl.when(away == step)
            def _():
                head[...] = offered[step][...]

        part[...] = lax.dot_general(
            head[...], grad[...], (((1,), (1,)), ((), ())), preferred_element_type=f32
        )

    return call(
        body,
        [adapter_ids, *offered, grad],
        [in_smem] + [in_vmem] * (own_count + 1),
        [shape_of((rank, rows), f32)],
        after=after,
        scratch_shapes=[pltpu.VMEM((rank, columns), bf16)],
        flops=2 * rows * rank * columns,
    )[0]


def head_term(lengths, lows, grad, scale, after):
    rank, rows = lows[0].shape
    columns = grad.shape[1]

    def body(lengths, *refs):
        *lows, grad, term = refs
        total = lows[0][...]
        for low in lows[1:]:
            total = total + low[...]
        live = lax.broadcasted_iota(jnp.int32, total.shape, 1) < lengths[0]
        kept = jnp.where(live, total, 0.0).astype(bf16)
        term[0] = (scale * jnp.dot(kept, grad[...], preferred_element_type=f32)).astype(bf16)

    return call(
        body,
        [lengths, *lows, grad],
        [in_smem] + [in_vmem] * (len(lows) + 1),
        [shape_of((1, rank, columns), bf16)],
        after=after,
        flops=2 * rows * rank * columns,
    )[0]


def share_of(own, sub):
    return sub * 2 + lax.rem(own, 2)


def shared_terms(lengths, parts, tokens, grad, scale, after):
    rows, features = tokens.shape
    rank = parts[0].shape[0]
    share = rank // 4

    def body(lengths, *refs):
        parts, (tokens, grad, back, mine, *sends, again, total) = refs[:count], refs[count:]
        own, sub = lax.axis_index("own"), lax.axis_index("sub")
        both = parts[0][...]
        for part in parts[1:]:
            both = both + part[...]
        live = lax.broadcasted_iota(jnp.int32, both.shape, 1) < lengths[0]
        back[...] = jnp.where(live, both, 0.0).astype(bf16)
        total[...] = scale * jnp.dot(back[...], tokens[...], preferred_element_type=f32)
        at = share_of(own, sub)

        def piece(flip):
            return total[pl.ds(pl.multiple_of((at ^ flip) * share, share), share), :]

        mine[...] = piece(0)
        for flip, send in zip((1, 2, 3), sends):
            send[...] = piece(flip).astype(bf16)
        again[...] = grad[...]

    count = len(parts)
    return call(
        body,
        [lengths, *parts, tokens, grad],
        [in_smem] + [in_vmem] * (count + 2),
        [shape_of((rank, rows), bf16), shape_of((share, features), f32)]
        + [shape_of((share, features), bf16)] * 3
        + [shape_of(grad.shape, bf16)],
        after=after,
        scratch_shapes=[pltpu.VMEM((rank, features), f32)],
        flops=2 * rows * rank * features,
    )


def add_up(pieces, after=()):
    def body(*refs):
        total = refs[0][...].astype(f32)
        for piece in refs[1:-1]:
            total = total + piece[...].astype(f32)
        refs[-1][...] = total.astype(bf16)

    return call(
        body,
        list(pieces),
        [in_vmem] * len(pieces),
        [shape_of(pieces[0].shape, bf16)],
        after=after,
    )[0]


def halve(pieces, bit):
    rows, features = pieces[0].shape
    half = rows // 2

    def body(*refs):
        total = refs[0][...].astype(f32)
        for piece in refs[1:-2]:
            total = total + piece[...].astype(f32)
        upper = lax.rem(lax.div(lax.axis_index("own"), bit), 2) == 1
        low, high = total[:half], total[half:]
        refs[-2][...] = jnp.where(upper, high, low)
        refs[-1][...] = jnp.where(upper, low, high).astype(bf16)

    return call(
        body,
        list(pieces),
        [in_vmem] * len(pieces),
        [shape_of((half, features), f32), shape_of((half, features), bf16)],
    )


def rejoin(mine, arrived, bit):
    rows, features = mine.shape

    def body(mine, arrived, out):
        upper = lax.rem(lax.div(lax.axis_index("own"), bit), 2) == 1
        one, two = mine[...].astype(f32), arrived[...].astype(f32)
        out[:rows] = jnp.where(upper, two, one).astype(bf16)
        out[rows:] = jnp.where(upper, one, two).astype(bf16)

    return call(
        body, [mine, arrived], [in_vmem] * 2, [shape_of((2 * rows, features), bf16)]
    )[0]


def join_shares(quarters, after):
    share, features = quarters[0].shape

    def body(*refs):
        out = refs[-1]
        at = share_of(lax.axis_index("own"), lax.axis_index("sub"))
        for flip in range(4):
            place = pl.multiple_of((at ^ flip) * share, share)
            out[pl.ds(place, share), :] = refs[flip][...].astype(f32)

    return call(
        body,
        quarters,
        [in_vmem] * 4,
        [shape_of((4 * share, features), f32)],
        after=after,
    )[0]


def stack(pieces, after=()):
    depths = [piece.shape[0] for piece in pieces]

    def body(*refs):
        at = 0
        for depth, piece in zip(depths, refs[:-1]):
            refs[-1][at : at + depth] = piece[...]
            at += depth

    return call(
        body,
        list(pieces),
        [in_vmem] * len(pieces),
        [shape_of((sum(depths),) + pieces[0].shape[1:], bf16)],
        after=after,
    )[0]


def place_terms(adapter_ids, near, far, pattern, per_owner, after):
    _, rank, columns = near.shape
    sub_count = lax.axis_size("sub")

    def body(ids, near, far, out, mark, held, sem):
        own, sub = lax.axis_index("own"), lax.axis_index("sub")
        held[...] = jnp.zeros(held.shape, f32)
        mark[...] = jnp.zeros(mark.shape, f32)
        for at, step in enumerate(pattern):
            for side in range(sub_count):
                local = ids[(own ^ step) * sub_count + side] - own * per_owner

                @pl.when(jnp.logical_and(local >= 0, local < per_owner))
                def _():
                    term = jnp.where(sub == side, near[at], far[at])
                    held[pl.ds(local, 1)] += term.astype(f32)[None]

        copy = pltpu.make_async_copy(held, out, sem)
        copy.start()
        copy.wait()

    return call(
        body,
        [adapter_ids, near, far],
        [in_smem, in_vmem, in_vmem],
        [shape_of((per_owner, rank, columns), f32), shape_of((8, 128), f32)],
        out_specs=[in_hbm, in_vmem],
        after=after,
        scratch_shapes=[
            pltpu.VMEM((per_owner, rank, columns), f32),
            pltpu.SemaphoreType.DMA,
        ],
    )


def arrange(lengths, grads):
    rows, columns = grads[0].shape
    count = len(grads)

    def body(lengths, *refs):
        grads, kept = refs[:-1], refs[-1]
        at = lax.axis_index("tp")
        live = lax.broadcasted_iota(jnp.int32, (rows, columns), 0) < lengths[0]
        for step in range(count):
            place = pl.multiple_of(lax.rem(at + count - step, count) * columns, 128)
            kept[:, pl.ds(place, columns)] = jnp.where(
                live, grads[step][...], jnp.zeros((rows, columns), bf16)
            )

    return call(
        body,
        [lengths, *grads],
        [in_smem] + [in_vmem] * count,
        [shape_of((rows, count * columns), bf16)],
    )[0]


def input_side(kept, frozen, frozen_other, back, down, after):
    rows, whole = kept.shape
    features, half = frozen.shape
    rank = back.shape[0]
    width = width_of(features)
    blocks = features // width

    def body(kept, frozen, frozen_other, back, down, out, mark, held, sems):
        mark[...] = jnp.zeros(mark.shape, f32)
        sub = lax.axis_index("sub")
        both = (((1,), (1,)), ((), ()))
        mine = kept[:, pl.ds(pl.multiple_of(sub * half, 128), half)]
        other = kept[:, pl.ds(pl.multiple_of((1 - sub) * half, 128), half)]
        twice = adapter_scale * back[...]
        copies = []
        for at in range(blocks):
            here = slice(at * width, (at + 1) * width)
            total = lax.dot_general(mine, frozen[here, :], both, preferred_element_type=f32)
            total += lax.dot_general(other, frozen_other[here, :], both, preferred_element_type=f32)
            total += lax.dot_general(
                twice, down[:, here], (((0,), (0,)), ((), ())), preferred_element_type=f32
            )
            held[:, here] = total.astype(bf16)
            copies.append(
                pltpu.make_async_copy(held.at[:, here], out.at[:, here], sems.at[at])
            )
            copies[-1].start()
        for copy in copies:
            copy.wait()

    return call(
        body,
        [kept, frozen, frozen_other, back, down],
        [in_vmem] * 5,
        [shape_of((rows, features), bf16), shape_of((8, 128), f32)],
        out_specs=[in_hbm, in_vmem],
        after=after,
        scratch_shapes=[
            pltpu.VMEM((rows, features), bf16),
            pltpu.SemaphoreType.DMA((blocks,)),
        ],
        flops=2 * rows * features * (2 * half + rank),
    )


def on_device(tokens, grad_output, frozen_value, shared_down, head_up, adapter_ids, lengths):
    rows = tokens.shape[0]
    own_count = lax.axis_size("own")
    tp_count = lax.axis_size("tp")
    per_owner = head_up.shape[0]
    scale = adapter_scale / rows
    tp_steps, own_steps = range(1, tp_count), range(1, own_count)

    frozen_other = shift(frozen_value, "sub", 1)
    picked = pick_heads(adapter_ids, head_up)
    offered = [picked[0]] + [swap(picked[step], step, 0) for step in own_steps]

    low, tokens, down = project_low(tokens, shared_down.T, offered[1:2] or picked[:1])
    lows = [low] + [shift(low, "tp", step) for step in tp_steps]

    part = project_back(adapter_ids, offered, grad_output, per_owner, [low, frozen_other])
    parts = [part] + [shift(part, "tp", step) for step in tp_steps]

    near = head_term(lengths, lows, grad_output, scale, [part])
    far_bits = [1 << i for i in reversed(range(1, own_count.bit_length() - 1))]
    pattern = [0]
    for bit in far_bits[:1]:
        near_arrived = swap(near, bit, 0)

    back, mine, *sends, again = shared_terms(lengths, parts, tokens, grad_output, scale, [near])
    grads = [grad_output] + [shift(again, "tp", step) for step in tp_steps]
    flips = ((1, 0), (0, 1), (1, 1))
    pieces = [mine] + [swap(send, *flip) for send, flip in zip(sends, flips)]

    bits = far_bits[::-1]
    for bit in bits[:-1]:
        stays, leaves = halve(pieces, bit)
        pieces = [stays, swap(leaves, bit, 0)]
    total = add_up(pieces)

    for bit in far_bits + [1] * (own_count > 1):
        arrived = near_arrived if bit == far_bits[0] else swap(near, bit, 0)
        near = stack([near, arrived], [total])
        pattern = pattern + [step ^ bit for step in pattern]
    far = shift(near, "sub", 1)

    if bits:
        total = add_up([total, swap(total, bits[-1], 0)])
    for bit in reversed(bits[:-1]):
        total = rejoin(total, swap(total, bit, 0), bit)
    quarters = [total] + [swap(total, *flip) for flip in flips]
    kept = arrange(lengths, grads)
    input_gradient, mark = input_side(kept, frozen_value, frozen_other, back, down, [total])
    grad_heads, mark = place_terms(adapter_ids, near, far, pattern, per_owner, [mark])
    shared_down_gradient = join_shares(quarters, [mark]).T
    return (input_gradient, shared_down_gradient, grad_heads)


def solution(mesh):
    placed = (
        P(("rep", "own", "sub"), "tp"),
        P(("rep", "own", "sub"), "tp"),
        P("tp", "sub"),
        P("tp", None),
        P("own", None, "tp"),
        P("rep"),
        P(("rep", "own", "sub")),
    )
    return jax.shard_map(
        on_device,
        mesh=mesh,
        in_specs=placed,
        out_specs=(
            P(("rep", "own", "sub"), "tp"),
            P(("rep", "tp"), None),
            P(("rep", "own"), None, "tp"),
        ),
        check_vma=False,
    )
```

```python
import jax
import jax.numpy as jnp
from jax import lax
from jax.experimental import pallas as pl
from jax.experimental.pallas import tpu as pltpu
from jax.sharding import PartitionSpec as P

adapter_scale = 2.0
f32 = jnp.float32
bf16 = jnp.bfloat16

anywhere = pl.BlockSpec(memory_space=pl.ANY)
in_hbm = pl.BlockSpec(memory_space=pltpu.HBM)
in_vmem = pl.BlockSpec(memory_space=pltpu.VMEM)
in_smem = pl.BlockSpec(memory_space=pltpu.SMEM)


def shift(x, axis, step):
    count = lax.axis_size(axis)
    return lax.ppermute(x, axis, [(i, (i + step) % count) for i in range(count)])


def swap(x, own_bit, sub_bit):
    subs = lax.axis_size("sub")
    whole = lax.axis_size("own") * subs
    other = own_bit * subs + sub_bit
    return lax.ppermute(x, ("own", "sub"), [(i, i ^ other) for i in range(whole)])


def width_of(features):
    return next(width for width in (512, 256, 128) if features % width == 0)


def stay(x):
    return pltpu.with_memory_space_constraint(x, pltpu.HBM)


def shape_of(dims, kind):
    return jax.ShapeDtypeStruct(dims, kind)


def call(body, operands, specs, outs, out_specs=None, after=(), flops=0, **more):
    count, idle = len(operands), len(after)

    def kernel(*refs):
        body(*refs[:count], *refs[count + idle :])

    moved = sum(x.size * x.dtype.itemsize for x in list(operands) + list(outs))
    return pl.pallas_call(
        kernel,
        out_shape=outs,
        in_specs=list(specs) + [anywhere] * len(after),
        out_specs=[in_vmem] * len(outs) if out_specs is None else out_specs,
        compiler_params=pltpu.CompilerParams(vmem_limit_bytes=24 * 1024 * 1024),
        cost_estimate=pl.CostEstimate(flops=flops, bytes_accessed=moved, transcendentals=0),
        **more,
    )(*operands, *after)


def pick_heads(adapter_ids, head_up, grad):
    per_owner, rank, width = head_up.shape
    own_count, sub_count = lax.axis_size("own"), lax.axis_size("sub")
    first = grad.shape[0] // 2

    def body(ids_far, head_up, grad, *refs):
        outs, early, away, ids, maps, sems = refs[:own_count], *refs[own_count:]
        own, sub = lax.axis_index("own"), lax.axis_index("sub")
        copies = [
            pltpu.make_async_copy(ids_far, ids, sems.at[0]),
            pltpu.make_async_copy(head_up, maps, sems.at[1]),
            pltpu.make_async_copy(grad.at[pl.ds(0, first)], early, sems.at[2]),
        ]
        for copy in copies:
            copy.start()
        copies[0].wait()
        copies[1].wait()
        for step in range(own_count):
            local = ids[(own ^ step) * sub_count + sub] - own * per_owner
            outs[step][...] = maps[jnp.clip(local, 0, per_owner - 1)]
        step = lax.div(ids[own * sub_count + sub], per_owner) ^ own
        away[...] = jnp.full(away.shape, step, jnp.int32)
        copies[2].wait()

    *picked, early, away = call(
        body,
        [stay(adapter_ids), stay(head_up), stay(grad)],
        [in_hbm] * 3,
        [shape_of((rank, width), bf16)] * own_count
        + [shape_of((first, grad.shape[1]), bf16), shape_of((8, 128), jnp.int32)],
        scratch_shapes=[
            pltpu.SMEM(adapter_ids.shape, jnp.int32),
            pltpu.VMEM(head_up.shape, bf16),
            pltpu.SemaphoreType.DMA((3,)),
        ],
    )
    return picked, early, away


def project_low(tokens, down, after):
    rows, features = tokens.shape
    rank = down.shape[0]
    width = width_of(features)
    blocks = features // width

    def body(tokens, down, low, near_tokens, near_down, sems):
        copies = [pltpu.make_async_copy(down, near_down, sems.at[blocks])]
        for at in range(blocks):
            here = pl.ds(at * width, width)
            copies.append(
                pltpu.make_async_copy(tokens.at[:, here], near_tokens.at[:, here], sems.at[at])
            )
        for copy in copies:
            copy.start()
        copies[0].wait()
        total = None
        for at in range(blocks):
            copies[at + 1].wait()
            here = slice(at * width, (at + 1) * width)
            part = lax.dot_general(
                near_down[:, here], near_tokens[:, here], (((1,), (1,)), ((), ())),
                preferred_element_type=f32,
            )
            total = part if total is None else total + part
        low[...] = total

    return call(
        body,
        [stay(tokens), stay(down)],
        [in_hbm] * 2,
        [shape_of((rank, rows), f32), shape_of(tokens.shape, bf16), shape_of(down.shape, bf16)],
        after=after,
        flops=2 * rows * rank * features,
        scratch_shapes=[pltpu.SemaphoreType.DMA((blocks + 1,))],
    )


def project_back(away, offered, grad, after):
    rank, columns = offered[0].shape
    rows = grad.shape[0]

    def body(away, *refs):
        *offered, grad, part = refs
        step = jnp.broadcast_to(away[:1, :1], (rank, columns))
        head = offered[0][...].astype(f32)
        for at in range(1, len(offered)):
            head = jnp.where(step == at, offered[at][...].astype(f32), head)
        part[...] = lax.dot_general(
            head.astype(bf16), grad[...], (((1,), (1,)), ((), ())), preferred_element_type=f32
        )

    return call(
        body,
        [away, *offered, grad],
        [in_vmem] * (len(offered) + 2),
        [shape_of((rank, rows), f32)],
        after=after,
        flops=2 * rows * rank * columns,
    )[0]


def head_term(lengths, lows, grad, scale, after):
    rank, rows = lows[0].shape
    columns = grad.shape[1]
    first = rows // 2

    def body(lengths, *refs):
        *lows, grad, term, late = refs
        total = lows[0][...]
        for low in lows[1:]:
            total = total + low[...]
        live = lax.broadcasted_iota(jnp.int32, total.shape, 1) < lengths[0]
        kept = jnp.where(live, total, 0.0).astype(bf16)
        term[0] = (scale * jnp.dot(kept, grad[...], preferred_element_type=f32)).astype(bf16)
        late[...] = grad[first:, :]

    return call(
        body,
        [lengths, *lows, grad],
        [in_smem] + [in_vmem] * (len(lows) + 1),
        [shape_of((1, rank, columns), bf16), shape_of((rows - first, columns), bf16)],
        after=after,
        flops=2 * rows * rank * columns,
    )


def shared_terms(lengths, parts, tokens, scale, after):
    rows, features = tokens.shape
    rank = parts[0].shape[0]
    share = rank // 2

    def body(lengths, *refs):
        parts, (tokens, back, keep, send, total) = refs[:count], refs[count:]
        sub = lax.axis_index("sub")
        both = parts[0][...]
        for part in parts[1:]:
            both = both + part[...]
        live = lax.broadcasted_iota(jnp.int32, both.shape, 1) < lengths[0]
        back[...] = jnp.where(live, both, 0.0).astype(bf16)
        total[...] = scale * jnp.dot(back[...], tokens[...], preferred_element_type=f32)
        keep[...] = total[pl.ds(pl.multiple_of(sub * share, share), share), :]
        send[...] = total[pl.ds(pl.multiple_of((1 - sub) * share, share), share), :]

    count = len(parts)
    return call(
        body,
        [lengths, *parts, tokens],
        [in_smem] + [in_vmem] * (count + 1),
        [shape_of((rank, rows), bf16)] + [shape_of((share, features), f32)] * 2,
        after=after,
        scratch_shapes=[pltpu.VMEM((rank, features), f32)],
        flops=2 * rows * rank * features,
    )


def add_up(pieces, after=()):
    def body(*refs):
        total = refs[0][...].astype(f32)
        for piece in refs[1:-1]:
            total = total + piece[...].astype(f32)
        refs[-1][...] = total.astype(bf16)

    return call(
        body,
        list(pieces),
        [in_vmem] * len(pieces),
        [shape_of(pieces[0].shape, bf16)],
        after=after,
    )[0]


def halve(pieces, bit, after=()):
    rows, features = pieces[0].shape
    half = rows // 2

    def body(*refs):
        total = refs[0][...].astype(f32)
        for piece in refs[1:-2]:
            total = total + piece[...].astype(f32)
        upper = lax.rem(lax.div(lax.axis_index("own"), bit), 2) == 1
        low, high = total[:half], total[half:]
        refs[-2][...] = jnp.where(upper, high, low)
        refs[-1][...] = jnp.where(upper, low, high).astype(bf16)

    return call(
        body,
        list(pieces),
        [in_vmem] * len(pieces),
        [shape_of((half, features), f32), shape_of((half, features), bf16)],
        after=after,
    )


def rejoin(mine, arrived, bit):
    rows, features = mine.shape

    def body(mine, arrived, out):
        upper = lax.rem(lax.div(lax.axis_index("own"), bit), 2) == 1
        one, two = mine[...].astype(f32), arrived[...].astype(f32)
        out[:rows] = jnp.where(upper, two, one).astype(bf16)
        out[rows:] = jnp.where(upper, one, two).astype(bf16)

    return call(
        body, [mine, arrived], [in_vmem] * 2, [shape_of((2 * rows, features), bf16)]
    )[0]


def join_shares(mine, other, after):
    share, features = mine.shape

    def body(mine, other, out):
        sub = lax.axis_index("sub")
        for side, piece in ((sub, mine), (1 - sub, other)):
            out[pl.ds(pl.multiple_of(side * share, share), share), :] = piece[...].astype(f32)

    return call(
        body,
        [mine, other],
        [in_vmem] * 2,
        [shape_of((2 * share, features), f32)],
        after=after,
    )[0]


def stack(pieces, after=()):
    depths = [piece.shape[0] for piece in pieces]

    def body(*refs):
        at = 0
        for depth, piece in zip(depths, refs[:-1]):
            refs[-1][at : at + depth] = piece[...]
            at += depth

    return call(
        body,
        list(pieces),
        [in_vmem] * len(pieces),
        [shape_of((sum(depths),) + pieces[0].shape[1:], bf16)],
        after=after,
    )[0]


def clean(dims, after):
    def body(out, mark, held, sem):
        held[...] = jnp.zeros(held.shape, f32)
        mark[...] = jnp.zeros(mark.shape, f32)
        copies = [pltpu.make_async_copy(held, out.at[at], sem.at[at]) for at in range(dims[0])]
        for copy in copies:
            copy.start()
        for copy in copies:
            copy.wait()

    return call(
        body,
        [],
        [],
        [shape_of(dims, f32), shape_of((8, 128), f32)],
        out_specs=[in_hbm, in_vmem],
        after=after,
        scratch_shapes=[pltpu.VMEM(dims[1:], f32), pltpu.SemaphoreType.DMA((dims[0],))],
    )


def place_terms(adapter_ids, near, far, pattern, cleaned, after):
    per_owner, rank, columns = cleaned.shape
    sub_count = lax.axis_size("sub")

    def body(ids_far, near, far, cleaned, out, mark, held, ids, counts, sems):
        own, sub = lax.axis_index("own"), lax.axis_index("sub")
        fetch = pltpu.make_async_copy(ids_far, ids, sems.at[per_owner])
        fetch.start()
        mark[...] = jnp.zeros(mark.shape, f32)
        for local in range(per_owner):
            counts[local] = 0
        fetch.wait()
        for at, step in enumerate(pattern):
            for side in range(sub_count):
                local = ids[(own ^ step) * sub_count + side] - own * per_owner

                @pl.when(jnp.logical_and(local >= 0, local < per_owner))
                def _():
                    term = jnp.where(sub == side, near[at], far[at]).astype(f32)

                    @pl.when(counts[local] == 0)
                    def _():
                        held[local] = term

                    @pl.when(counts[local] > 0)
                    def _():
                        held[local] += term

                    counts[local] += 1

        copies = [
            pltpu.make_async_copy(held.at[local], out.at[local], sems.at[local])
            for local in range(per_owner)
        ]
        for local, copy in enumerate(copies):
            pl.when(counts[local] > 0)(copy.start)
        for local, copy in enumerate(copies):
            pl.when(counts[local] > 0)(copy.wait)

    return call(
        body,
        [stay(adapter_ids), near, far, cleaned],
        [in_hbm, in_vmem, in_vmem, in_hbm],
        [shape_of(cleaned.shape, f32), shape_of((8, 128), f32)],
        out_specs=[in_hbm, in_vmem],
        after=after,
        input_output_aliases={3: 0},
        scratch_shapes=[
            pltpu.VMEM(cleaned.shape, f32),
            pltpu.SMEM(adapter_ids.shape, jnp.int32),
            pltpu.SMEM((per_owner,), jnp.int32),
            pltpu.SemaphoreType.DMA((per_owner + 1,)),
        ],
    )


def arrange(lengths, grad, pieces, after):
    rows, columns = grad.shape
    count = 1 + len(pieces)
    first = rows // 2

    def body(lengths, grad, *refs):
        pieces, kept = refs[:-1], refs[-1]
        at = lax.axis_index("tp")
        live = lax.broadcasted_iota(jnp.int32, (rows, columns), 0) < lengths[0]
        zero = jnp.zeros((rows, columns), bf16)
        place = pl.multiple_of(at * columns, 128)
        kept[:, pl.ds(place, columns)] = jnp.where(live, grad[...], zero)
        for step in range(1, count):
            place = pl.multiple_of(lax.rem(at + count - step, count) * columns, 128)
            early, late = pieces[2 * step - 2 : 2 * step]
            kept[:first, pl.ds(place, columns)] = jnp.where(live[:first], early[...], zero[:first])
            kept[first:, pl.ds(place, columns)] = jnp.where(live[first:], late[...], zero[first:])

    flat = [x for pair in pieces for x in pair]
    return call(
        body,
        [lengths, grad, *flat],
        [in_smem] + [in_vmem] * (1 + len(flat)),
        [shape_of((rows, count * columns), bf16)],
        after=after,
    )[0]


def input_side(kept, frozen, frozen_other, back, down, after):
    rows, whole = kept.shape
    features, half = frozen.shape
    rank = back.shape[0]
    width = width_of(features)
    blocks = features // width

    def body(kept, frozen, frozen_other, back, down, out, mark, held, sems):
        mark[...] = jnp.zeros(mark.shape, f32)
        sub = lax.axis_index("sub")
        both = (((1,), (1,)), ((), ()))
        mine = kept[:, pl.ds(pl.multiple_of(sub * half, 128), half)]
        other = kept[:, pl.ds(pl.multiple_of((1 - sub) * half, 128), half)]
        twice = adapter_scale * back[...]
        copies = []
        for at in range(blocks):
            here = slice(at * width, (at + 1) * width)
            total = lax.dot_general(mine, frozen[here, :], both, preferred_element_type=f32)
            total += lax.dot_general(other, frozen_other[here, :], both, preferred_element_type=f32)
            total += lax.dot_general(
                twice, down[:, here], (((0,), (0,)), ((), ())), preferred_element_type=f32
            )
            held[:, here] = total.astype(bf16)
            copies.append(
                pltpu.make_async_copy(held.at[:, here], out.at[:, here], sems.at[at])
            )
            copies[-1].start()
        for copy in copies:
            copy.wait()

    return call(
        body,
        [kept, frozen, frozen_other, back, down],
        [in_vmem] * 5,
        [shape_of((rows, features), bf16), shape_of((8, 128), f32)],
        out_specs=[in_hbm, in_vmem],
        after=after,
        scratch_shapes=[
            pltpu.VMEM((rows, features), bf16),
            pltpu.SemaphoreType.DMA((blocks,)),
        ],
        flops=2 * rows * features * (2 * half + rank),
    )


def on_device(tokens, grad_output, frozen_value, shared_down, head_up, adapter_ids, lengths):
    rows = tokens.shape[0]
    own_count = lax.axis_size("own")
    tp_count = lax.axis_size("tp")
    per_owner = head_up.shape[0]
    scale = adapter_scale / rows
    tp_steps, own_steps = range(1, tp_count), range(1, own_count)

    frozen_other = shift(frozen_value, "sub", 1)
    picked, early, away = pick_heads(adapter_ids, head_up, grad_output)
    offered = [picked[0]] + [swap(picked[step], step, 0) for step in own_steps]
    early_grads = [shift(early, "tp", step) for step in tp_steps]

    low, tokens, down = project_low(tokens, shared_down.T, offered[1:2] or picked[:1])
    lows = [low] + [shift(low, "tp", step) for step in tp_steps]

    part = project_back(away, offered, grad_output, [low, frozen_other, *early_grads])
    parts = [part] + [shift(part, "tp", step) for step in tp_steps]

    near, late = head_term(lengths, lows, grad_output, scale, [part])
    late_grads = [shift(late, "tp", step) for step in tp_steps]
    bits = [1 << i for i in range(own_count.bit_length() - 1)]
    terms, pattern = [near], [0]
    for bit in reversed(bits):
        terms = terms + [swap(term, bit, 0) for term in terms]
        pattern = pattern + [step ^ bit for step in pattern]

    back, keep, send = shared_terms(lengths, parts, tokens, scale, [near])
    pieces = [keep, shift(send, "sub", 1)]

    mark = keep
    for bit in bits[:-1]:
        stays, leaves = halve(pieces, bit)
        pieces = [stays, swap(leaves, bit, 0)]
        mark = leaves
    cleaned, mark = clean((per_owner,) + near.shape[1:], [mark])
    total = add_up(pieces, [mark])
    kept = arrange(lengths, grad_output, list(zip(early_grads, late_grads)), [total])
    input_gradient, mark = input_side(kept, frozen_value, frozen_other, back, down, [total])
    near = stack(terms, [total])
    far = shift(near, "sub", 1)
    if bits:
        total = add_up([total, swap(total, bits[-1], 0)], [mark])
    grad_heads, mark = place_terms(adapter_ids, near, far, pattern, cleaned, [total])
    for bit in reversed(bits[:-1]):
        total = rejoin(total, swap(total, bit, 0), bit)
    shared_down_gradient = join_shares(total, shift(total, "sub", 1), [mark]).T
    return (input_gradient, shared_down_gradient, grad_heads)


def solution(mesh):
    placed = (
        P(("rep", "own", "sub"), "tp"),
        P(("rep", "own", "sub"), "tp"),
        P("tp", "sub"),
        P("tp", None),
        P("own", None, "tp"),
        P("rep"),
        P(("rep", "own", "sub")),
    )
    return jax.shard_map(
        on_device,
        mesh=mesh,
        in_specs=placed,
        out_specs=(
            P(("rep", "own", "sub"), "tp"),
            P(("rep", "tp"), None),
            P(("rep", "own"), None, "tp"),
        ),
        check_vma=False,
    )
```

```python
import jax
import jax.numpy as jnp
from jax import lax
from jax.experimental import pallas as pl
from jax.experimental.pallas import tpu as pltpu
from jax.sharding import PartitionSpec as P

adapter_scale = 2.0
f32 = jnp.float32
bf16 = jnp.bfloat16

anywhere = pl.BlockSpec(memory_space=pl.ANY)
in_hbm = pl.BlockSpec(memory_space=pltpu.HBM)
in_vmem = pl.BlockSpec(memory_space=pltpu.VMEM)
in_smem = pl.BlockSpec(memory_space=pltpu.SMEM)


def shift(x, axis, step):
    count = lax.axis_size(axis)
    return lax.ppermute(x, axis, [(i, (i + step) % count) for i in range(count)])


def swap(x, own_bit, sub_bit):
    subs = lax.axis_size("sub")
    whole = lax.axis_size("own") * subs
    other = own_bit * subs + sub_bit
    return lax.ppermute(x, ("own", "sub"), [(i, i ^ other) for i in range(whole)])


def width_of(features):
    return next(width for width in (512, 256, 128) if features % width == 0)


def stay(x):
    return pltpu.with_memory_space_constraint(x, pltpu.HBM)


def shape_of(dims, kind):
    return jax.ShapeDtypeStruct(dims, kind)


def call(body, operands, specs, outs, out_specs=None, after=(), flops=0, **more):
    count, idle = len(operands), len(after)

    def kernel(*refs):
        body(*refs[:count], *refs[count + idle :])

    moved = sum(x.size * x.dtype.itemsize for x in list(operands) + list(outs))
    return pl.pallas_call(
        kernel,
        out_shape=outs,
        in_specs=list(specs) + [anywhere] * len(after),
        out_specs=[in_vmem] * len(outs) if out_specs is None else out_specs,
        compiler_params=pltpu.CompilerParams(vmem_limit_bytes=24 * 1024 * 1024),
        cost_estimate=pl.CostEstimate(flops=flops, bytes_accessed=moved, transcendentals=0),
        **more,
    )(*operands, *after)


def pick_heads(adapter_ids, head_up, grad):
    per_owner, rank, width = head_up.shape
    own_count, sub_count = lax.axis_size("own"), lax.axis_size("sub")
    first = grad.shape[0] // 2

    def body(ids_far, head_up, grad, *refs):
        outs, early, away, ids, maps, sems = refs[:own_count], *refs[own_count:]
        own, sub = lax.axis_index("own"), lax.axis_index("sub")
        copies = [
            pltpu.make_async_copy(ids_far, ids, sems.at[0]),
            pltpu.make_async_copy(head_up, maps, sems.at[1]),
            pltpu.make_async_copy(grad.at[pl.ds(0, first)], early, sems.at[2]),
        ]
        for copy in copies:
            copy.start()
        copies[0].wait()
        copies[1].wait()
        for step in range(own_count):
            local = ids[(own ^ step) * sub_count + sub] - own * per_owner
            outs[step][...] = maps[jnp.clip(local, 0, per_owner - 1)]
        step = lax.div(ids[own * sub_count + sub], per_owner) ^ own
        away[...] = jnp.full(away.shape, step, jnp.int32)
        copies[2].wait()

    *picked, early, away = call(
        body,
        [stay(adapter_ids), stay(head_up), stay(grad)],
        [in_hbm] * 3,
        [shape_of((rank, width), bf16)] * own_count
        + [shape_of((first, grad.shape[1]), bf16), shape_of((8, 128), jnp.int32)],
        scratch_shapes=[
            pltpu.SMEM(adapter_ids.shape, jnp.int32),
            pltpu.VMEM(head_up.shape, bf16),
            pltpu.SemaphoreType.DMA((3,)),
        ],
    )
    return picked, early, away


def project_low(tokens, down, after):
    rows, features = tokens.shape
    rank = down.shape[0]
    width = width_of(features)
    blocks = features // width

    def body(tokens, down, low, near_tokens, near_down, sems):
        copies = [pltpu.make_async_copy(down, near_down, sems.at[blocks])]
        for at in range(blocks):
            here = pl.ds(at * width, width)
            copies.append(
                pltpu.make_async_copy(tokens.at[:, here], near_tokens.at[:, here], sems.at[at])
            )
        for copy in copies:
            copy.start()
        copies[0].wait()
        total = None
        for at in range(blocks):
            copies[at + 1].wait()
            here = slice(at * width, (at + 1) * width)
            part = lax.dot_general(
                near_down[:, here], near_tokens[:, here], (((1,), (1,)), ((), ())),
                preferred_element_type=f32,
            )
            total = part if total is None else total + part
        low[...] = total

    return call(
        body,
        [stay(tokens), stay(down)],
        [in_hbm] * 2,
        [shape_of((rank, rows), f32), shape_of(tokens.shape, bf16), shape_of(down.shape, bf16)],
        after=after,
        flops=2 * rows * rank * features,
        scratch_shapes=[pltpu.SemaphoreType.DMA((blocks + 1,))],
    )


def project_back(away, offered, grad, after):
    rank, columns = offered[0].shape
    rows = grad.shape[0]

    def body(away, *refs):
        *offered, grad, part = refs
        step = jnp.broadcast_to(away[:1, :1], (rank, columns))
        head = offered[0][...].astype(f32)
        for at in range(1, len(offered)):
            head = jnp.where(step == at, offered[at][...].astype(f32), head)
        part[...] = lax.dot_general(
            head.astype(bf16), grad[...], (((1,), (1,)), ((), ())), preferred_element_type=f32
        )

    return call(
        body,
        [away, *offered, grad],
        [in_vmem] * (len(offered) + 2),
        [shape_of((rank, rows), f32)],
        after=after,
        flops=2 * rows * rank * columns,
    )[0]


def head_term(lengths, lows, grad, scale, after):
    rank, rows = lows[0].shape
    columns = grad.shape[1]
    first = rows // 2

    def body(lengths, *refs):
        *lows, grad, term, late = refs
        total = lows[0][...]
        for low in lows[1:]:
            total = total + low[...]
        live = lax.broadcasted_iota(jnp.int32, total.shape, 1) < lengths[0]
        kept = jnp.where(live, total, 0.0).astype(bf16)
        term[0] = (scale * jnp.dot(kept, grad[...], preferred_element_type=f32)).astype(bf16)
        late[...] = grad[first:, :]

    return call(
        body,
        [lengths, *lows, grad],
        [in_smem] + [in_vmem] * (len(lows) + 1),
        [shape_of((1, rank, columns), bf16), shape_of((rows - first, columns), bf16)],
        after=after,
        flops=2 * rows * rank * columns,
    )


def shared_terms(lengths, parts, tokens, scale, after):
    rows, features = tokens.shape
    rank = parts[0].shape[0]
    share = rank // 2

    def body(lengths, *refs):
        parts, (tokens, back, keep, send, total) = refs[:count], refs[count:]
        sub = lax.axis_index("sub")
        both = parts[0][...]
        for part in parts[1:]:
            both = both + part[...]
        live = lax.broadcasted_iota(jnp.int32, both.shape, 1) < lengths[0]
        back[...] = jnp.where(live, both, 0.0).astype(bf16)
        total[...] = scale * jnp.dot(back[...], tokens[...], preferred_element_type=f32)
        keep[...] = total[pl.ds(pl.multiple_of(sub * share, share), share), :]
        send[...] = total[pl.ds(pl.multiple_of((1 - sub) * share, share), share), :]

    count = len(parts)
    return call(
        body,
        [lengths, *parts, tokens],
        [in_smem] + [in_vmem] * (count + 1),
        [shape_of((rank, rows), bf16)] + [shape_of((share, features), f32)] * 2,
        after=after,
        scratch_shapes=[pltpu.VMEM((rank, features), f32)],
        flops=2 * rows * rank * features,
    )


def add_up(pieces, after=()):
    def body(*refs):
        total = refs[0][...].astype(f32)
        for piece in refs[1:-1]:
            total = total + piece[...].astype(f32)
        refs[-1][...] = total.astype(bf16)

    return call(
        body,
        list(pieces),
        [in_vmem] * len(pieces),
        [shape_of(pieces[0].shape, bf16)],
        after=after,
    )[0]


def halve(pieces, bit, after=()):
    rows, features = pieces[0].shape
    half = rows // 2

    def body(*refs):
        total = refs[0][...].astype(f32)
        for piece in refs[1:-2]:
            total = total + piece[...].astype(f32)
        upper = lax.rem(lax.div(lax.axis_index("own"), bit), 2) == 1
        low, high = total[:half], total[half:]
        refs[-2][...] = jnp.where(upper, high, low)
        refs[-1][...] = jnp.where(upper, low, high).astype(bf16)

    return call(
        body,
        list(pieces),
        [in_vmem] * len(pieces),
        [shape_of((half, features), f32), shape_of((half, features), bf16)],
        after=after,
    )


def rejoin(mine, arrived, bit, after):
    rows, features = mine.shape

    def body(mine, arrived, out):
        upper = lax.rem(lax.div(lax.axis_index("own"), bit), 2) == 1
        one, two = mine[...].astype(f32), arrived[...].astype(f32)
        out[:rows] = jnp.where(upper, two, one).astype(bf16)
        out[rows:] = jnp.where(upper, one, two).astype(bf16)

    return call(
        body,
        [mine, arrived],
        [in_vmem] * 2,
        [shape_of((2 * rows, features), bf16)],
        after=after,
    )[0]


def join_shares(mine, other, after):
    share, features = mine.shape

    def body(mine, other, out):
        sub = lax.axis_index("sub")
        for side, piece in ((sub, mine), (1 - sub, other)):
            out[pl.ds(pl.multiple_of(side * share, share), share), :] = piece[...].astype(f32)

    return call(
        body,
        [mine, other],
        [in_vmem] * 2,
        [shape_of((2 * share, features), f32)],
        after=after,
    )[0]


def stack(pieces, after=()):
    depths = [piece.shape[0] for piece in pieces]

    def body(*refs):
        at = 0
        for depth, piece in zip(depths, refs[:-1]):
            refs[-1][at : at + depth] = piece[...]
            at += depth

    return call(
        body,
        list(pieces),
        [in_vmem] * len(pieces),
        [shape_of((sum(depths),) + pieces[0].shape[1:], bf16)],
        after=after,
    )[0]


def clean(dims, after):
    def body(out, mark, held, sem):
        held[...] = jnp.zeros(held.shape, f32)
        mark[...] = jnp.zeros(mark.shape, f32)
        copies = [pltpu.make_async_copy(held, out.at[at], sem.at[at]) for at in range(dims[0])]
        for copy in copies:
            copy.start()
        for copy in copies:
            copy.wait()

    return call(
        body,
        [],
        [],
        [shape_of(dims, f32), shape_of((8, 128), f32)],
        out_specs=[in_hbm, in_vmem],
        after=after,
        scratch_shapes=[pltpu.VMEM(dims[1:], f32), pltpu.SemaphoreType.DMA((dims[0],))],
    )


def place_terms(adapter_ids, near, far, pattern, cleaned, after):
    per_owner, rank, columns = cleaned.shape
    sub_count = lax.axis_size("sub")

    def body(ids_far, near, far, cleaned, out, mark, held, ids, counts, sems):
        own, sub = lax.axis_index("own"), lax.axis_index("sub")
        fetch = pltpu.make_async_copy(ids_far, ids, sems.at[per_owner])
        fetch.start()
        mark[...] = jnp.zeros(mark.shape, f32)
        for local in range(per_owner):
            counts[local] = 0
        fetch.wait()
        for at, step in enumerate(pattern):
            for side in range(sub_count):
                local = ids[(own ^ step) * sub_count + side] - own * per_owner

                @pl.when(jnp.logical_and(local >= 0, local < per_owner))
                def _():
                    term = jnp.where(sub == side, near[at], far[at]).astype(f32)

                    @pl.when(counts[local] == 0)
                    def _():
                        held[local] = term

                    @pl.when(counts[local] > 0)
                    def _():
                        held[local] += term

                    counts[local] += 1

        copies = [
            pltpu.make_async_copy(held.at[local], out.at[local], sems.at[local])
            for local in range(per_owner)
        ]
        for local, copy in enumerate(copies):
            pl.when(counts[local] > 0)(copy.start)
        for local, copy in enumerate(copies):
            pl.when(counts[local] > 0)(copy.wait)

    return call(
        body,
        [stay(adapter_ids), near, far, cleaned],
        [in_hbm, in_vmem, in_vmem, in_hbm],
        [shape_of(cleaned.shape, f32), shape_of((8, 128), f32)],
        out_specs=[in_hbm, in_vmem],
        after=after,
        input_output_aliases={3: 0},
        scratch_shapes=[
            pltpu.VMEM(cleaned.shape, f32),
            pltpu.SMEM(adapter_ids.shape, jnp.int32),
            pltpu.SMEM((per_owner,), jnp.int32),
            pltpu.SemaphoreType.DMA((per_owner + 1,)),
        ],
    )


def arrange(lengths, grad, pieces, after):
    rows, columns = grad.shape
    count = 1 + len(pieces)
    first = rows // 2

    def body(lengths, grad, *refs):
        pieces, kept = refs[:-1], refs[-1]
        at = lax.axis_index("tp")
        live = lax.broadcasted_iota(jnp.int32, (rows, columns), 0) < lengths[0]
        zero = jnp.zeros((rows, columns), bf16)
        place = pl.multiple_of(at * columns, 128)
        kept[:, pl.ds(place, columns)] = jnp.where(live, grad[...], zero)
        for step in range(1, count):
            place = pl.multiple_of(lax.rem(at + count - step, count) * columns, 128)
            early, late = pieces[2 * step - 2 : 2 * step]
            kept[:first, pl.ds(place, columns)] = jnp.where(live[:first], early[...], zero[:first])
            kept[first:, pl.ds(place, columns)] = jnp.where(live[first:], late[...], zero[first:])

    flat = [x for pair in pieces for x in pair]
    return call(
        body,
        [lengths, grad, *flat],
        [in_smem] + [in_vmem] * (1 + len(flat)),
        [shape_of((rows, count * columns), bf16)],
        after=after,
    )[0]


def input_side(kept, frozen, frozen_other, back, down, after):
    rows, whole = kept.shape
    features, half = frozen.shape
    rank = back.shape[0]
    width = width_of(features)
    blocks = features // width

    def body(kept, frozen, frozen_other, back, down, out, mark, held, sems):
        mark[...] = jnp.zeros(mark.shape, f32)
        sub = lax.axis_index("sub")
        both = (((1,), (1,)), ((), ()))
        mine = kept[:, pl.ds(pl.multiple_of(sub * half, 128), half)]
        other = kept[:, pl.ds(pl.multiple_of((1 - sub) * half, 128), half)]
        twice = adapter_scale * back[...]
        copies = []
        for at in range(blocks):
            here = slice(at * width, (at + 1) * width)
            total = lax.dot_general(mine, frozen[here, :], both, preferred_element_type=f32)
            total += lax.dot_general(other, frozen_other[here, :], both, preferred_element_type=f32)
            total += lax.dot_general(
                twice, down[:, here], (((0,), (0,)), ((), ())), preferred_element_type=f32
            )
            held[:, here] = total.astype(bf16)
            copies.append(
                pltpu.make_async_copy(held.at[:, here], out.at[:, here], sems.at[at])
            )
            copies[-1].start()
        for copy in copies:
            copy.wait()

    return call(
        body,
        [kept, frozen, frozen_other, back, down],
        [in_vmem] * 5,
        [shape_of((rows, features), bf16), shape_of((8, 128), f32)],
        out_specs=[in_hbm, in_vmem],
        after=after,
        scratch_shapes=[
            pltpu.VMEM((rows, features), bf16),
            pltpu.SemaphoreType.DMA((blocks,)),
        ],
        flops=2 * rows * features * (2 * half + rank),
    )


def on_device(tokens, grad_output, frozen_value, shared_down, head_up, adapter_ids, lengths):
    rows = tokens.shape[0]
    own_count = lax.axis_size("own")
    tp_count = lax.axis_size("tp")
    per_owner = head_up.shape[0]
    scale = adapter_scale / rows
    tp_steps, own_steps = range(1, tp_count), range(1, own_count)

    frozen_other = shift(frozen_value, "sub", 1)
    picked, early, away = pick_heads(adapter_ids, head_up, grad_output)
    offered = [picked[0]] + [swap(picked[step], step, 0) for step in own_steps]
    early_grads = [shift(early, "tp", step) for step in tp_steps]

    low, tokens, down = project_low(tokens, shared_down.T, offered[1:2] or picked[:1])
    lows = [low] + [shift(low, "tp", step) for step in tp_steps]

    part = project_back(away, offered, grad_output, [low, frozen_other, *early_grads])
    parts = [part] + [shift(part, "tp", step) for step in tp_steps]

    near, late = head_term(lengths, lows, grad_output, scale, [part])
    late_grads = [shift(late, "tp", step) for step in tp_steps]
    bits = [1 << i for i in range(own_count.bit_length() - 1)]
    terms, pattern = [near], [0]
    for bit in reversed(bits):
        terms = terms + [swap(term, bit, 0) for term in terms]
        pattern = pattern + [step ^ bit for step in pattern]

    cleaned, mark = clean((per_owner,) + near.shape[1:], [near])
    back, keep, send = shared_terms(lengths, parts, tokens, scale, [mark])
    pieces = [keep, shift(send, "sub", 1)]

    for bit in bits[:-1]:
        stays, leaves = halve(pieces, bit)
        pieces = [stays, swap(leaves, bit, 0)]
    total = add_up(pieces)
    near = stack(terms, [total])
    far = shift(near, "sub", 1)
    kept = arrange(lengths, grad_output, list(zip(early_grads, late_grads)), [total])
    input_gradient, mark = input_side(kept, frozen_value, frozen_other, back, down, [total])
    if bits:
        total = add_up([total, swap(total, bits[-1], 0)], [mark])
    grad_heads, mark = place_terms(adapter_ids, near, far, pattern, cleaned, [total])
    for bit in reversed(bits[:-1]):
        total = rejoin(total, swap(total, bit, 0), bit, [mark])
        mark = total
    shared_down_gradient = join_shares(total, shift(total, "sub", 1), [mark]).T
    return (input_gradient, shared_down_gradient, grad_heads)


def solution(mesh):
    placed = (
        P(("rep", "own", "sub"), "tp"),
        P(("rep", "own", "sub"), "tp"),
        P("tp", "sub"),
        P("tp", None),
        P("own", None, "tp"),
        P("rep"),
        P(("rep", "own", "sub")),
    )
    return jax.shard_map(
        on_device,
        mesh=mesh,
        in_specs=placed,
        out_specs=(
            P(("rep", "own", "sub"), "tp"),
            P(("rep", "tp"), None),
            P(("rep", "own"), None, "tp"),
        ),
        check_vma=False,
    )
```

```python
import jax
import jax.numpy as jnp
from jax import lax
from jax.experimental import pallas as pl
from jax.experimental.pallas import tpu as pltpu
from jax.sharding import PartitionSpec as P

adapter_scale = 2.0
f32 = jnp.float32
bf16 = jnp.bfloat16

busy = 10**10
brief = 3 * 10**9

anywhere = pl.BlockSpec(memory_space=pl.ANY)
in_hbm = pl.BlockSpec(memory_space=pltpu.HBM)
in_vmem = pl.BlockSpec(memory_space=pltpu.VMEM)
in_smem = pl.BlockSpec(memory_space=pltpu.SMEM)


def shift(x, axis, step):
    count = lax.axis_size(axis)
    return lax.ppermute(x, axis, [(i, (i + step) % count) for i in range(count)])


def swap(x, own_bit, sub_bit):
    subs = lax.axis_size("sub")
    whole = lax.axis_size("own") * subs
    other = own_bit * subs + sub_bit
    return lax.ppermute(x, ("own", "sub"), [(i, i ^ other) for i in range(whole)])


def width_of(features):
    return next(width for width in (512, 256, 128) if features % width == 0)


def stay(x):
    return pltpu.with_memory_space_constraint(x, pltpu.HBM)


def shape_of(dims, kind):
    return jax.ShapeDtypeStruct(dims, kind)


def call(body, operands, specs, outs, out_specs=None, after=(), flops=0, **more):
    count, idle = len(operands), len(after)

    def kernel(*refs):
        body(*refs[:count], *refs[count + idle :])

    moved = sum(x.size * x.dtype.itemsize for x in list(operands) + list(outs))
    return pl.pallas_call(
        kernel,
        out_shape=outs,
        in_specs=list(specs) + [anywhere] * len(after),
        out_specs=[in_vmem] * len(outs) if out_specs is None else out_specs,
        compiler_params=pltpu.CompilerParams(vmem_limit_bytes=24 * 1024 * 1024),
        cost_estimate=pl.CostEstimate(flops=flops, bytes_accessed=moved, transcendentals=0),
        **more,
    )(*operands, *after)


def pick_heads(adapter_ids, head_up, grad):
    per_owner, rank, width = head_up.shape
    own_count, sub_count = lax.axis_size("own"), lax.axis_size("sub")
    first = grad.shape[0] // 2

    def body(ids_far, head_up, grad, *refs):
        outs, early, away, ids, maps, sems = refs[:own_count], *refs[own_count:]
        own, sub = lax.axis_index("own"), lax.axis_index("sub")
        copies = [
            pltpu.make_async_copy(ids_far, ids, sems.at[0]),
            pltpu.make_async_copy(head_up, maps, sems.at[1]),
            pltpu.make_async_copy(grad.at[pl.ds(0, first)], early, sems.at[2]),
        ]
        for copy in copies:
            copy.start()
        copies[0].wait()
        copies[1].wait()
        for step in range(own_count):
            local = ids[(own ^ step) * sub_count + sub] - own * per_owner
            outs[step][...] = maps[jnp.clip(local, 0, per_owner - 1)]
        step = lax.div(ids[own * sub_count + sub], per_owner) ^ own
        away[...] = jnp.full(away.shape, step, jnp.int32)
        copies[2].wait()

    *picked, early, away = call(
        body,
        [stay(adapter_ids), stay(head_up), stay(grad)],
        [in_hbm] * 3,
        [shape_of((rank, width), bf16)] * own_count
        + [shape_of((first, grad.shape[1]), bf16), shape_of((8, 128), jnp.int32)],
        scratch_shapes=[
            pltpu.SMEM(adapter_ids.shape, jnp.int32),
            pltpu.VMEM(head_up.shape, bf16),
            pltpu.SemaphoreType.DMA((3,)),
        ],
    )
    return picked, early, away


def project_low(tokens, down, after):
    rows, features = tokens.shape
    rank = down.shape[0]
    width = width_of(features)
    blocks = features // width

    def body(tokens, down, low, near_tokens, near_down, sems):
        copies = [pltpu.make_async_copy(down, near_down, sems.at[blocks])]
        for at in range(blocks):
            here = pl.ds(at * width, width)
            copies.append(
                pltpu.make_async_copy(tokens.at[:, here], near_tokens.at[:, here], sems.at[at])
            )
        for copy in copies:
            copy.start()
        copies[0].wait()
        total = None
        for at in range(blocks):
            copies[at + 1].wait()
            here = slice(at * width, (at + 1) * width)
            part = lax.dot_general(
                near_down[:, here], near_tokens[:, here], (((1,), (1,)), ((), ())),
                preferred_element_type=f32,
            )
            total = part if total is None else total + part
        low[...] = total

    return call(
        body,
        [stay(tokens), stay(down)],
        [in_hbm] * 2,
        [shape_of((rank, rows), f32), shape_of(tokens.shape, bf16), shape_of(down.shape, bf16)],
        after=after,
        flops=2 * rows * rank * features,
        scratch_shapes=[pltpu.SemaphoreType.DMA((blocks + 1,))],
    )


def project_back(away, offered, grad, after):
    rank, columns = offered[0].shape
    rows = grad.shape[0]

    def body(away, *refs):
        *offered, grad, part = refs
        step = jnp.broadcast_to(away[:1, :1], (rank, columns))
        head = offered[0][...].astype(f32)
        for at in range(1, len(offered)):
            head = jnp.where(step == at, offered[at][...].astype(f32), head)
        part[...] = lax.dot_general(
            head.astype(bf16), grad[...], (((1,), (1,)), ((), ())), preferred_element_type=f32
        )

    return call(
        body,
        [away, *offered, grad],
        [in_vmem] * (len(offered) + 2),
        [shape_of((rank, rows), f32)],
        after=after,
        flops=2 * rows * rank * columns,
    )[0]


def head_term(lengths, lows, grad, scale, after):
    rank, rows = lows[0].shape
    columns = grad.shape[1]
    first = rows // 2

    def body(lengths, *refs):
        *lows, grad, term, late = refs
        total = lows[0][...]
        for low in lows[1:]:
            total = total + low[...]
        live = lax.broadcasted_iota(jnp.int32, total.shape, 1) < lengths[0]
        kept = jnp.where(live, total, 0.0).astype(bf16)
        term[0] = (scale * jnp.dot(kept, grad[...], preferred_element_type=f32)).astype(bf16)
        late[...] = grad[first:, :]

    return call(
        body,
        [lengths, *lows, grad],
        [in_smem] + [in_vmem] * (len(lows) + 1),
        [shape_of((1, rank, columns), bf16), shape_of((rows - first, columns), bf16)],
        after=after,
        flops=2 * rows * rank * columns,
    )


def shared_terms(lengths, parts, tokens, scale, after):
    rows, features = tokens.shape
    rank = parts[0].shape[0]
    share = rank // 2

    def body(lengths, *refs):
        parts, (tokens, back, keep, send, total) = refs[:count], refs[count:]
        sub = lax.axis_index("sub")
        both = parts[0][...]
        for part in parts[1:]:
            both = both + part[...]
        live = lax.broadcasted_iota(jnp.int32, both.shape, 1) < lengths[0]
        back[...] = jnp.where(live, both, 0.0).astype(bf16)
        total[...] = scale * jnp.dot(back[...], tokens[...], preferred_element_type=f32)
        keep[...] = total[pl.ds(pl.multiple_of(sub * share, share), share), :]
        send[...] = total[pl.ds(pl.multiple_of((1 - sub) * share, share), share), :]

    count = len(parts)
    return call(
        body,
        [lengths, *parts, tokens],
        [in_smem] + [in_vmem] * (count + 1),
        [shape_of((rank, rows), bf16)] + [shape_of((share, features), f32)] * 2,
        after=after,
        scratch_shapes=[pltpu.VMEM((rank, features), f32)],
        flops=2 * rows * rank * features,
    )


def add_up(pieces, after=()):
    def body(*refs):
        total = refs[0][...].astype(f32)
        for piece in refs[1:-1]:
            total = total + piece[...].astype(f32)
        refs[-1][...] = total.astype(bf16)

    return call(
        body,
        list(pieces),
        [in_vmem] * len(pieces),
        [shape_of(pieces[0].shape, bf16)],
        after=after,
    )[0]


def halve(pieces, bit, after=()):
    rows, features = pieces[0].shape
    half = rows // 2

    def body(*refs):
        total = refs[0][...].astype(f32)
        for piece in refs[1:-2]:
            total = total + piece[...].astype(f32)
        upper = lax.rem(lax.div(lax.axis_index("own"), bit), 2) == 1
        low, high = total[:half], total[half:]
        refs[-2][...] = jnp.where(upper, high, low)
        refs[-1][...] = jnp.where(upper, low, high).astype(bf16)

    return call(
        body,
        list(pieces),
        [in_vmem] * len(pieces),
        [shape_of((half, features), f32), shape_of((half, features), bf16)],
        after=after,
    )


def rejoin(mine, arrived, bit):
    rows, features = mine.shape

    def body(mine, arrived, out):
        upper = lax.rem(lax.div(lax.axis_index("own"), bit), 2) == 1
        one, two = mine[...].astype(f32), arrived[...].astype(f32)
        out[:rows] = jnp.where(upper, two, one).astype(bf16)
        out[rows:] = jnp.where(upper, one, two).astype(bf16)

    return call(
        body,
        [mine, arrived],
        [in_vmem] * 2,
        [shape_of((2 * rows, features), bf16)],
        flops=busy,
    )[0]


def join_shares(mine, other, after):
    share, features = mine.shape

    def body(mine, other, out):
        sub = lax.axis_index("sub")
        for side, piece in ((sub, mine), (1 - sub, other)):
            out[pl.ds(pl.multiple_of(side * share, share), share), :] = piece[...].astype(f32)

    return call(
        body,
        [mine, other],
        [in_vmem] * 2,
        [shape_of((2 * share, features), f32)],
        after=after,
    )[0]


def stack(pieces, after=(), flops=0):
    depths = [piece.shape[0] for piece in pieces]

    def body(*refs):
        at = 0
        for depth, piece in zip(depths, refs[:-1]):
            refs[-1][at : at + depth] = piece[...]
            at += depth

    return call(
        body,
        list(pieces),
        [in_vmem] * len(pieces),
        [shape_of((sum(depths),) + pieces[0].shape[1:], bf16)],
        after=after,
        flops=flops,
    )[0]


def clean(dims, after):
    def body(out, mark, held, sem):
        held[...] = jnp.zeros(held.shape, f32)
        mark[...] = jnp.zeros(mark.shape, f32)
        copies = [pltpu.make_async_copy(held, out.at[at], sem.at[at]) for at in range(dims[0])]
        for copy in copies:
            copy.start()
        for copy in copies:
            copy.wait()

    return call(
        body,
        [],
        [],
        [shape_of(dims, f32), shape_of((8, 128), f32)],
        out_specs=[in_hbm, in_vmem],
        after=after,
        scratch_shapes=[pltpu.VMEM(dims[1:], f32), pltpu.SemaphoreType.DMA((dims[0],))],
        flops=busy,
    )


def place_terms(adapter_ids, near, far, pattern, cleaned, after):
    per_owner, rank, columns = cleaned.shape
    sub_count = lax.axis_size("sub")

    def body(ids_far, near, far, cleaned, out, mark, held, ids, counts, sems):
        own, sub = lax.axis_index("own"), lax.axis_index("sub")
        fetch = pltpu.make_async_copy(ids_far, ids, sems.at[per_owner])
        fetch.start()
        mark[...] = jnp.zeros(mark.shape, f32)
        for local in range(per_owner):
            counts[local] = 0
        fetch.wait()
        for at, step in enumerate(pattern):
            for side in range(sub_count):
                local = ids[(own ^ step) * sub_count + side] - own * per_owner

                @pl.when(jnp.logical_and(local >= 0, local < per_owner))
                def _():
                    term = jnp.where(sub == side, near[at], far[at]).astype(f32)

                    @pl.when(counts[local] == 0)
                    def _():
                        held[local] = term

                    @pl.when(counts[local] > 0)
                    def _():
                        held[local] += term

                    counts[local] += 1

        copies = [
            pltpu.make_async_copy(held.at[local], out.at[local], sems.at[local])
            for local in range(per_owner)
        ]
        for local, copy in enumerate(copies):
            pl.when(counts[local] > 0)(copy.start)
        for local, copy in enumerate(copies):
            pl.when(counts[local] > 0)(copy.wait)

    return call(
        body,
        [stay(adapter_ids), near, far, cleaned],
        [in_hbm, in_vmem, in_vmem, in_hbm],
        [shape_of(cleaned.shape, f32), shape_of((8, 128), f32)],
        out_specs=[in_hbm, in_vmem],
        after=after,
        input_output_aliases={3: 0},
        scratch_shapes=[
            pltpu.VMEM(cleaned.shape, f32),
            pltpu.SMEM(adapter_ids.shape, jnp.int32),
            pltpu.SMEM((per_owner,), jnp.int32),
            pltpu.SemaphoreType.DMA((per_owner + 1,)),
        ],
    )


def arrange(lengths, grad, pieces, after):
    rows, columns = grad.shape
    count = 1 + len(pieces)
    first = rows // 2

    def body(lengths, grad, *refs):
        pieces, kept = refs[:-1], refs[-1]
        at = lax.axis_index("tp")
        live = lax.broadcasted_iota(jnp.int32, (rows, columns), 0) < lengths[0]
        zero = jnp.zeros((rows, columns), bf16)
        place = pl.multiple_of(at * columns, 128)
        kept[:, pl.ds(place, columns)] = jnp.where(live, grad[...], zero)
        for step in range(1, count):
            place = pl.multiple_of(lax.rem(at + count - step, count) * columns, 128)
            early, late = pieces[2 * step - 2 : 2 * step]
            kept[:first, pl.ds(place, columns)] = jnp.where(live[:first], early[...], zero[:first])
            kept[first:, pl.ds(place, columns)] = jnp.where(live[first:], late[...], zero[first:])

    flat = [x for pair in pieces for x in pair]
    return call(
        body,
        [lengths, grad, *flat],
        [in_smem] + [in_vmem] * (1 + len(flat)),
        [shape_of((rows, count * columns), bf16)],
        after=after,
    )[0]


def input_side(kept, frozen, frozen_other, back, down, after):
    rows, whole = kept.shape
    features, half = frozen.shape
    rank = back.shape[0]
    width = width_of(features)
    blocks = features // width

    def body(kept, frozen, frozen_other, back, down, out, mark, held, sems):
        mark[...] = jnp.zeros(mark.shape, f32)
        sub = lax.axis_index("sub")
        both = (((1,), (1,)), ((), ()))
        mine = kept[:, pl.ds(pl.multiple_of(sub * half, 128), half)]
        other = kept[:, pl.ds(pl.multiple_of((1 - sub) * half, 128), half)]
        twice = adapter_scale * back[...]
        copies = []
        for at in range(blocks):
            here = slice(at * width, (at + 1) * width)
            total = lax.dot_general(mine, frozen[here, :], both, preferred_element_type=f32)
            total += lax.dot_general(other, frozen_other[here, :], both, preferred_element_type=f32)
            total += lax.dot_general(
                twice, down[:, here], (((0,), (0,)), ((), ())), preferred_element_type=f32
            )
            held[:, here] = total.astype(bf16)
            copies.append(
                pltpu.make_async_copy(held.at[:, here], out.at[:, here], sems.at[at])
            )
            copies[-1].start()
        for copy in copies:
            copy.wait()

    return call(
        body,
        [kept, frozen, frozen_other, back, down],
        [in_vmem] * 5,
        [shape_of((rows, features), bf16), shape_of((8, 128), f32)],
        out_specs=[in_hbm, in_vmem],
        after=after,
        scratch_shapes=[
            pltpu.VMEM((rows, features), bf16),
            pltpu.SemaphoreType.DMA((blocks,)),
        ],
        flops=2 * rows * features * (2 * half + rank),
    )


def on_device(tokens, grad_output, frozen_value, shared_down, head_up, adapter_ids, lengths):
    rows = tokens.shape[0]
    own_count = lax.axis_size("own")
    tp_count = lax.axis_size("tp")
    per_owner = head_up.shape[0]
    scale = adapter_scale / rows
    tp_steps, own_steps = range(1, tp_count), range(1, own_count)

    frozen_other = shift(frozen_value, "sub", 1)
    picked, early, away = pick_heads(adapter_ids, head_up, grad_output)
    offered = [picked[0]] + [swap(picked[step], step, 0) for step in own_steps]
    early_grads = [shift(early, "tp", step) for step in tp_steps]

    low, tokens, down = project_low(tokens, shared_down.T, offered[1:2] or picked[:1])
    lows = [low] + [shift(low, "tp", step) for step in tp_steps]

    part = project_back(away, offered, grad_output, [low, frozen_other, *early_grads])
    parts = [part] + [shift(part, "tp", step) for step in tp_steps]

    near, late = head_term(lengths, lows, grad_output, scale, [part])
    late_grads = [shift(late, "tp", step) for step in tp_steps]
    bits = [1 << i for i in range(own_count.bit_length() - 1)]
    terms, pattern = [near], [0]
    for bit in reversed(bits[1:]):
        terms = terms + [swap(term, bit, 0) for term in terms]
        pattern = pattern + [step ^ bit for step in pattern]
    nearby = [swap(near, 1, 0)] if bits else []

    back, keep, send = shared_terms(lengths, parts, tokens, scale, [near])
    pieces = [keep, shift(send, "sub", 1)]
    met = stack(terms[1:] + nearby, flops=brief) if bits else near

    mark = met
    for bit in bits[:-1]:
        stays, leaves = halve(pieces, bit, [mark])
        pieces = [stays, swap(leaves, bit, 0)]
        mark = leaves
    cleaned, mark = clean((per_owner,) + near.shape[1:], [mark])
    total = add_up(pieces, [mark])
    relays = [total]
    if bits:
        relays = [stack([term], [total]) for term in terms[1:]]
        terms = terms + nearby + [swap(relay, 1, 0) for relay in relays]
        pattern = pattern + [step ^ 1 for step in pattern]
    kept = arrange(lengths, grad_output, list(zip(early_grads, late_grads)), [total])
    input_gradient, mark = input_side(kept, frozen_value, frozen_other, back, down, relays)
    near = stack(terms, [mark])
    if bits:
        total = add_up([total, swap(total, bits[-1], 0)], [near])
    far = shift(near, "sub", 1)
    for bit in reversed(bits[:-1]):
        total = rejoin(total, swap(total, bit, 0), bit)
    grad_heads, mark = place_terms(adapter_ids, near, far, pattern, cleaned, [total])
    shared_down_gradient = join_shares(total, shift(total, "sub", 1), [mark]).T
    return (input_gradient, shared_down_gradient, grad_heads)


def solution(mesh):
    placed = (
        P(("rep", "own", "sub"), "tp"),
        P(("rep", "own", "sub"), "tp"),
        P("tp", "sub"),
        P("tp", None),
        P("own", None, "tp"),
        P("rep"),
        P(("rep", "own", "sub")),
    )
    return jax.shard_map(
        on_device,
        mesh=mesh,
        in_specs=placed,
        out_specs=(
            P(("rep", "own", "sub"), "tp"),
            P(("rep", "tp"), None),
            P(("rep", "own"), None, "tp"),
        ),
        check_vma=False,
    )
```

```python
import jax
import jax.numpy as jnp
from jax import lax
from jax.experimental import pallas as pl
from jax.experimental.pallas import tpu as pltpu
from jax.sharding import PartitionSpec as P

adapter_scale = 2.0
f32 = jnp.float32
bf16 = jnp.bfloat16

early_part = 4

busy, middling, brief = 10**10, 5 * 10**9, 3 * 10**9

anywhere = pl.BlockSpec(memory_space=pl.ANY)
in_hbm = pl.BlockSpec(memory_space=pltpu.HBM)
in_vmem = pl.BlockSpec(memory_space=pltpu.VMEM)
in_smem = pl.BlockSpec(memory_space=pltpu.SMEM)


def shift(x, axis, step):
    count = lax.axis_size(axis)
    return lax.ppermute(x, axis, [(i, (i + step) % count) for i in range(count)])


def swap(x, own_bit, sub_bit):
    subs = lax.axis_size("sub")
    whole = lax.axis_size("own") * subs
    other = own_bit * subs + sub_bit
    return lax.ppermute(x, ("own", "sub"), [(i, i ^ other) for i in range(whole)])


def width_of(features):
    return next(width for width in (512, 256, 128) if features % width == 0)


def stay(x):
    return pltpu.with_memory_space_constraint(x, pltpu.HBM)


def shape_of(dims, kind):
    return jax.ShapeDtypeStruct(dims, kind)


def call(body, operands, specs, outs, out_specs=None, after=(), flops=0, **more):
    count, idle = len(operands), len(after)

    def kernel(*refs):
        body(*refs[:count], *refs[count + idle :])

    moved = sum(x.size * x.dtype.itemsize for x in list(operands) + list(outs))
    return pl.pallas_call(
        kernel,
        out_shape=outs,
        in_specs=list(specs) + [anywhere] * len(after),
        out_specs=[in_vmem] * len(outs) if out_specs is None else out_specs,
        compiler_params=pltpu.CompilerParams(vmem_limit_bytes=24 * 1024 * 1024),
        cost_estimate=pl.CostEstimate(flops=flops, bytes_accessed=moved, transcendentals=0),
        **more,
    )(*operands, *after)


def pick_heads(adapter_ids, head_up, grad):
    per_owner, rank, width = head_up.shape
    own_count, sub_count = lax.axis_size("own"), lax.axis_size("sub")
    first = grad.shape[0] // early_part

    def body(ids_far, head_up, grad, *refs):
        outs, early, away, ids, maps, sems = refs[:own_count], *refs[own_count:]
        own, sub = lax.axis_index("own"), lax.axis_index("sub")
        copies = [
            pltpu.make_async_copy(ids_far, ids, sems.at[0]),
            pltpu.make_async_copy(head_up, maps, sems.at[1]),
            pltpu.make_async_copy(grad.at[pl.ds(0, first)], early, sems.at[2]),
        ]
        for copy in copies:
            copy.start()
        copies[0].wait()
        copies[1].wait()
        for step in range(own_count):
            local = ids[(own ^ step) * sub_count + sub] - own * per_owner
            outs[step][...] = maps[jnp.clip(local, 0, per_owner - 1)]
        step = lax.div(ids[own * sub_count + sub], per_owner) ^ own
        away[...] = jnp.full(away.shape, step, jnp.int32)
        copies[2].wait()

    *picked, early, away = call(
        body,
        [stay(adapter_ids), stay(head_up), stay(grad)],
        [in_hbm] * 3,
        [shape_of((rank, width), bf16)] * own_count
        + [shape_of((first, grad.shape[1]), bf16), shape_of((8, 128), jnp.int32)],
        scratch_shapes=[
            pltpu.SMEM(adapter_ids.shape, jnp.int32),
            pltpu.VMEM(head_up.shape, bf16),
            pltpu.SemaphoreType.DMA((3,)),
        ],
    )
    return picked, early, away


def project_low(tokens, down, after):
    rows, features = tokens.shape
    rank = down.shape[0]
    width = width_of(features)
    blocks = features // width

    def body(tokens, down, low, rounded, near_tokens, near_down, sems):
        copies = [pltpu.make_async_copy(down, near_down, sems.at[blocks])]
        for at in range(blocks):
            here = pl.ds(at * width, width)
            copies.append(
                pltpu.make_async_copy(tokens.at[:, here], near_tokens.at[:, here], sems.at[at])
            )
        for copy in copies:
            copy.start()
        copies[0].wait()
        total = None
        for at in range(blocks):
            copies[at + 1].wait()
            here = slice(at * width, (at + 1) * width)
            part = lax.dot_general(
                near_down[:, here], near_tokens[:, here], (((1,), (1,)), ((), ())),
                preferred_element_type=f32,
            )
            total = part if total is None else total + part
        low[...] = total
        rounded[...] = total.astype(bf16)

    return call(
        body,
        [stay(tokens), stay(down)],
        [in_hbm] * 2,
        [shape_of((rank, rows), f32), shape_of((rank, rows), bf16)]
        + [shape_of(tokens.shape, bf16), shape_of(down.shape, bf16)],
        after=after,
        flops=2 * rows * rank * features,
        scratch_shapes=[pltpu.SemaphoreType.DMA((blocks + 1,))],
    )


def project_back(away, offered, grad, after):
    rank, columns = offered[0].shape
    rows = grad.shape[0]

    def body(away, *refs):
        *offered, grad, part = refs
        step = jnp.broadcast_to(away[:1, :1], (rank, columns))
        head = offered[0][...].astype(f32)
        for at in range(1, len(offered)):
            head = jnp.where(step == at, offered[at][...].astype(f32), head)
        part[...] = lax.dot_general(
            head.astype(bf16), grad[...], (((1,), (1,)), ((), ())), preferred_element_type=f32
        )

    return call(
        body,
        [away, *offered, grad],
        [in_vmem] * (len(offered) + 2),
        [shape_of((rank, rows), f32)],
        after=after,
        flops=2 * rows * rank * columns,
    )[0]


def head_term(lengths, lows, grad, scale, after):
    rank, rows = lows[0].shape
    columns = grad.shape[1]
    first = rows // early_part

    def body(lengths, *refs):
        *lows, grad, term, late = refs
        total = lows[0][...]
        for low in lows[1:]:
            total = total + low[...].astype(f32)
        live = lax.broadcasted_iota(jnp.int32, total.shape, 1) < lengths[0]
        total = jnp.where(live, total, 0.0)
        kept = total.astype(bf16)
        rest = (total - kept.astype(f32)).astype(bf16)
        product = jnp.dot(kept, grad[...], preferred_element_type=f32)
        product += jnp.dot(rest, grad[...], preferred_element_type=f32)
        term[0] = (scale * product).astype(bf16)
        late[...] = grad[first:, :]

    return call(
        body,
        [lengths, *lows, grad],
        [in_smem] + [in_vmem] * (len(lows) + 1),
        [shape_of((1, rank, columns), bf16), shape_of((rows - first, columns), bf16)],
        after=after,
        flops=brief,
    )


def shared_terms(lengths, parts, tokens, scale, after):
    rows, features = tokens.shape
    rank = parts[0].shape[0]
    share = rank // 2

    def body(lengths, *refs):
        parts, (tokens, back, keep, send, total) = refs[:count], refs[count:]
        sub = lax.axis_index("sub")
        both = parts[0][...]
        for part in parts[1:]:
            both = both + part[...]
        live = lax.broadcasted_iota(jnp.int32, both.shape, 1) < lengths[0]
        back[...] = jnp.where(live, both, 0.0).astype(bf16)
        total[...] = scale * jnp.dot(back[...], tokens[...], preferred_element_type=f32)
        keep[...] = total[pl.ds(pl.multiple_of(sub * share, share), share), :]
        send[...] = total[pl.ds(pl.multiple_of((1 - sub) * share, share), share), :]

    count = len(parts)
    return call(
        body,
        [lengths, *parts, tokens],
        [in_smem] + [in_vmem] * (count + 1),
        [shape_of((rank, rows), bf16)] + [shape_of((share, features), f32)] * 2,
        after=after,
        scratch_shapes=[pltpu.VMEM((rank, features), f32)],
        flops=2 * rows * rank * features,
    )


def add_up(pieces, after=()):
    def body(*refs):
        total = refs[0][...].astype(f32)
        for piece in refs[1:-1]:
            total = total + piece[...].astype(f32)
        refs[-1][...] = total.astype(bf16)

    return call(
        body,
        list(pieces),
        [in_vmem] * len(pieces),
        [shape_of(pieces[0].shape, bf16)],
        after=after,
    )[0]


def halve(pieces, bit, after=()):
    rows, features = pieces[0].shape
    half = rows // 2

    def body(*refs):
        total = refs[0][...].astype(f32)
        for piece in refs[1:-2]:
            total = total + piece[...].astype(f32)
        upper = lax.rem(lax.div(lax.axis_index("own"), bit), 2) == 1
        low, high = total[:half], total[half:]
        refs[-2][...] = jnp.where(upper, high, low)
        refs[-1][...] = jnp.where(upper, low, high).astype(bf16)

    return call(
        body,
        list(pieces),
        [in_vmem] * len(pieces),
        [shape_of((half, features), f32), shape_of((half, features), bf16)],
        after=after,
    )


def rejoin(mine, arrived, bit):
    rows, features = mine.shape

    def body(mine, arrived, out):
        upper = lax.rem(lax.div(lax.axis_index("own"), bit), 2) == 1
        one, two = mine[...].astype(f32), arrived[...].astype(f32)
        out[:rows] = jnp.where(upper, two, one).astype(bf16)
        out[rows:] = jnp.where(upper, one, two).astype(bf16)

    return call(
        body,
        [mine, arrived],
        [in_vmem] * 2,
        [shape_of((2 * rows, features), bf16)],
        flops=busy,
    )[0]


def join_shares(mine, other, after):
    share, features = mine.shape

    def body(mine, other, out):
        sub = lax.axis_index("sub")
        for side, piece in ((sub, mine), (1 - sub, other)):
            out[pl.ds(pl.multiple_of(side * share, share), share), :] = piece[...].astype(f32)

    return call(
        body,
        [mine, other],
        [in_vmem] * 2,
        [shape_of((2 * share, features), f32)],
        after=after,
    )[0]


def stack(pieces, after=(), flops=0):
    depths = [piece.shape[0] for piece in pieces]

    def body(*refs):
        at = 0
        for depth, piece in zip(depths, refs[:-1]):
            refs[-1][at : at + depth] = piece[...]
            at += depth

    return call(
        body,
        list(pieces),
        [in_vmem] * len(pieces),
        [shape_of((sum(depths),) + pieces[0].shape[1:], bf16)],
        after=after,
        flops=flops,
    )[0]


def clean(dims, after):
    def body(out, mark, held, sem):
        held[...] = jnp.zeros(held.shape, f32)
        mark[...] = jnp.zeros(mark.shape, f32)
        copies = [pltpu.make_async_copy(held, out.at[at], sem.at[at]) for at in range(dims[0])]
        for copy in copies:
            copy.start()
        for copy in copies:
            copy.wait()

    return call(
        body,
        [],
        [],
        [shape_of(dims, f32), shape_of((8, 128), f32)],
        out_specs=[in_hbm, in_vmem],
        after=after,
        scratch_shapes=[pltpu.VMEM(dims[1:], f32), pltpu.SemaphoreType.DMA((dims[0],))],
        flops=busy,
    )


def place_terms(adapter_ids, near, far, pattern, cleaned, after):
    per_owner, rank, columns = cleaned.shape
    sub_count = lax.axis_size("sub")

    def body(ids_far, near, far, cleaned, out, mark, held, ids, counts, sems):
        own, sub = lax.axis_index("own"), lax.axis_index("sub")
        fetch = pltpu.make_async_copy(ids_far, ids, sems.at[per_owner])
        fetch.start()
        mark[...] = jnp.zeros(mark.shape, f32)
        for local in range(per_owner):
            counts[local] = 0
        fetch.wait()
        for at, step in enumerate(pattern):
            for side in range(sub_count):
                local = ids[(own ^ step) * sub_count + side] - own * per_owner

                @pl.when(jnp.logical_and(local >= 0, local < per_owner))
                def _():
                    term = jnp.where(sub == side, near[at], far[at]).astype(f32)

                    @pl.when(counts[local] == 0)
                    def _():
                        held[local] = term

                    @pl.when(counts[local] > 0)
                    def _():
                        held[local] += term

                    counts[local] += 1

        copies = [
            pltpu.make_async_copy(held.at[local], out.at[local], sems.at[local])
            for local in range(per_owner)
        ]
        for local, copy in enumerate(copies):
            pl.when(counts[local] > 0)(copy.start)
        for local, copy in enumerate(copies):
            pl.when(counts[local] > 0)(copy.wait)

    return call(
        body,
        [stay(adapter_ids), near, far, cleaned],
        [in_hbm, in_vmem, in_vmem, in_hbm],
        [shape_of(cleaned.shape, f32), shape_of((8, 128), f32)],
        out_specs=[in_hbm, in_vmem],
        after=after,
        input_output_aliases={3: 0},
        scratch_shapes=[
            pltpu.VMEM(cleaned.shape, f32),
            pltpu.SMEM(adapter_ids.shape, jnp.int32),
            pltpu.SMEM((per_owner,), jnp.int32),
            pltpu.SemaphoreType.DMA((per_owner + 1,)),
        ],
    )


def arrange(lengths, grad, pieces, after):
    rows, columns = grad.shape
    count = 1 + len(pieces)
    first = rows // early_part

    def body(lengths, grad, *refs):
        pieces, kept = refs[:-1], refs[-1]
        at = lax.axis_index("tp")
        live = lax.broadcasted_iota(jnp.int32, (rows, columns), 0) < lengths[0]
        zero = jnp.zeros((rows, columns), bf16)
        place = pl.multiple_of(at * columns, 128)
        kept[:, pl.ds(place, columns)] = jnp.where(live, grad[...], zero)
        for step in range(1, count):
            place = pl.multiple_of(lax.rem(at + count - step, count) * columns, 128)
            early, late = pieces[2 * step - 2 : 2 * step]
            kept[:first, pl.ds(place, columns)] = jnp.where(live[:first], early[...], zero[:first])
            kept[first:, pl.ds(place, columns)] = jnp.where(live[first:], late[...], zero[first:])

    flat = [x for pair in pieces for x in pair]
    return call(
        body,
        [lengths, grad, *flat],
        [in_smem] + [in_vmem] * (1 + len(flat)),
        [shape_of((rows, count * columns), bf16)],
        after=after,
    )[0]


def input_side(kept, frozen, frozen_other, back, down, after):
    rows, whole = kept.shape
    features, half = frozen.shape
    rank = back.shape[0]
    width = width_of(features)
    blocks = features // width

    def body(kept, frozen, frozen_other, back, down, out, mark, held, sems):
        mark[...] = jnp.zeros(mark.shape, f32)
        sub = lax.axis_index("sub")
        both = (((1,), (1,)), ((), ()))
        mine = kept[:, pl.ds(pl.multiple_of(sub * half, 128), half)]
        other = kept[:, pl.ds(pl.multiple_of((1 - sub) * half, 128), half)]
        twice = adapter_scale * back[...]
        copies = []
        for at in range(blocks):
            here = slice(at * width, (at + 1) * width)
            total = lax.dot_general(mine, frozen[here, :], both, preferred_element_type=f32)
            total += lax.dot_general(other, frozen_other[here, :], both, preferred_element_type=f32)
            total += lax.dot_general(
                twice, down[:, here], (((0,), (0,)), ((), ())), preferred_element_type=f32
            )
            held[:, here] = total.astype(bf16)
            copies.append(
                pltpu.make_async_copy(held.at[:, here], out.at[:, here], sems.at[at])
            )
            copies[-1].start()
        for copy in copies:
            copy.wait()

    return call(
        body,
        [kept, frozen, frozen_other, back, down],
        [in_vmem] * 5,
        [shape_of((rows, features), bf16), shape_of((8, 128), f32)],
        out_specs=[in_hbm, in_vmem],
        after=after,
        scratch_shapes=[
            pltpu.VMEM((rows, features), bf16),
            pltpu.SemaphoreType.DMA((blocks,)),
        ],
        flops=2 * rows * features * (2 * half + rank),
    )


def on_device(tokens, grad_output, frozen_value, shared_down, head_up, adapter_ids, lengths):
    rows = tokens.shape[0]
    own_count = lax.axis_size("own")
    tp_count = lax.axis_size("tp")
    per_owner = head_up.shape[0]
    scale = adapter_scale / rows
    tp_steps, own_steps = range(1, tp_count), range(1, own_count)

    frozen_other = shift(frozen_value, "sub", 1)
    picked, early, away = pick_heads(adapter_ids, head_up, grad_output)
    offered = [picked[0]] + [swap(picked[step], step, 0) for step in own_steps]
    early_grads = [shift(early, "tp", step) for step in tp_steps]

    low, rounded, tokens, down = project_low(tokens, shared_down.T, offered[1:2] or picked[:1])
    lows = [low] + [shift(rounded, "tp", step) for step in tp_steps]

    part = project_back(away, offered, grad_output, [low, frozen_other, *early_grads])
    parts = [part] + [shift(part, "tp", step) for step in tp_steps]

    near, late = head_term(lengths, lows, grad_output, scale, [part])
    late_grads = [shift(late, "tp", step) for step in tp_steps]
    bits = [1 << i for i in range(own_count.bit_length() - 1)]
    terms, pattern = [near], [0]
    for bit in reversed(bits[1:]):
        terms = terms + [swap(term, bit, 0) for term in terms]
        pattern = pattern + [step ^ bit for step in pattern]
    nearby = [swap(near, 1, 0)] if bits else []

    back, keep, send = shared_terms(lengths, parts, tokens, scale, [near])
    pieces = [keep, shift(send, "sub", 1)]
    met = stack(terms[1:] + nearby, flops=middling) if bits else near

    mark = met
    for bit in bits[:-1]:
        stays, leaves = halve(pieces, bit, [mark])
        pieces = [stays, swap(leaves, bit, 0)]
        mark = leaves
    cleaned, mark = clean((per_owner,) + near.shape[1:], [mark])
    total = add_up(pieces, [mark])
    relays = [total]
    if bits:
        relays = [stack([term], [total]) for term in terms[1:]]
        terms = terms + nearby + [swap(relay, 1, 0) for relay in relays]
        pattern = pattern + [step ^ 1 for step in pattern]
    kept = arrange(lengths, grad_output, list(zip(early_grads, late_grads)), [total])
    input_gradient, mark = input_side(kept, frozen_value, frozen_other, back, down, relays)
    near = stack(terms, [mark])
    if bits:
        total = add_up([total, swap(total, bits[-1], 0)], [near])
    far = shift(near, "sub", 1)
    for bit in reversed(bits[:-1]):
        total = rejoin(total, swap(total, bit, 0), bit)
    grad_heads, mark = place_terms(adapter_ids, near, far, pattern, cleaned, [total])
    shared_down_gradient = join_shares(total, shift(total, "sub", 1), [mark]).T
    return (input_gradient, shared_down_gradient, grad_heads)


def solution(mesh):
    placed = (
        P(("rep", "own", "sub"), "tp"),
        P(("rep", "own", "sub"), "tp"),
        P("tp", "sub"),
        P("tp", None),
        P("own", None, "tp"),
        P("rep"),
        P(("rep", "own", "sub")),
    )
    return jax.shard_map(
        on_device,
        mesh=mesh,
        in_specs=placed,
        out_specs=(
            P(("rep", "own", "sub"), "tp"),
            P(("rep", "tp"), None),
            P(("rep", "own"), None, "tp"),
        ),
        check_vma=False,
    )
```

```python
import jax
import jax.numpy as jnp
from jax import lax
from jax.experimental import pallas as pl
from jax.experimental.pallas import tpu as pltpu
from jax.sharding import PartitionSpec as P

adapter_scale = 2.0
f32 = jnp.float32
bf16 = jnp.bfloat16

early_part = 4

busy, middling, brief, slight = 10**10, 5 * 10**9, 3 * 10**9, 15 * 10**8

anywhere = pl.BlockSpec(memory_space=pl.ANY)
in_hbm = pl.BlockSpec(memory_space=pltpu.HBM)
in_vmem = pl.BlockSpec(memory_space=pltpu.VMEM)
in_smem = pl.BlockSpec(memory_space=pltpu.SMEM)


def shift(x, axis, step):
    count = lax.axis_size(axis)
    return lax.ppermute(x, axis, [(i, (i + step) % count) for i in range(count)])


def swap(x, own_bit, sub_bit):
    subs = lax.axis_size("sub")
    whole = lax.axis_size("own") * subs
    other = own_bit * subs + sub_bit
    return lax.ppermute(x, ("own", "sub"), [(i, i ^ other) for i in range(whole)])


def width_of(features):
    return next(width for width in (512, 256, 128) if features % width == 0)


def stay(x):
    return pltpu.with_memory_space_constraint(x, pltpu.HBM)


def shape_of(dims, kind):
    return jax.ShapeDtypeStruct(dims, kind)


def call(body, operands, specs, outs, out_specs=None, after=(), flops=0, **more):
    count, idle = len(operands), len(after)

    def kernel(*refs):
        body(*refs[:count], *refs[count + idle :])

    moved = sum(x.size * x.dtype.itemsize for x in list(operands) + list(outs))
    return pl.pallas_call(
        kernel,
        out_shape=outs,
        in_specs=list(specs) + [anywhere] * len(after),
        out_specs=[in_vmem] * len(outs) if out_specs is None else out_specs,
        compiler_params=pltpu.CompilerParams(vmem_limit_bytes=24 * 1024 * 1024),
        cost_estimate=pl.CostEstimate(flops=flops, bytes_accessed=moved, transcendentals=0),
        **more,
    )(*operands, *after)


def pick_heads(adapter_ids, head_up, grad):
    per_owner, rank, width = head_up.shape
    own_count, sub_count = lax.axis_size("own"), lax.axis_size("sub")
    first = grad.shape[0] // early_part

    def body(ids_far, head_up, grad, *refs):
        outs, early, away, ids, maps, sems = refs[:own_count], *refs[own_count:]
        own, sub = lax.axis_index("own"), lax.axis_index("sub")
        copies = [
            pltpu.make_async_copy(ids_far, ids, sems.at[0]),
            pltpu.make_async_copy(head_up, maps, sems.at[1]),
            pltpu.make_async_copy(grad.at[pl.ds(0, first)], early, sems.at[2]),
        ]
        for copy in copies:
            copy.start()
        copies[0].wait()
        copies[1].wait()
        for step in range(own_count):
            local = ids[(own ^ step) * sub_count + sub] - own * per_owner
            outs[step][...] = maps[jnp.clip(local, 0, per_owner - 1)]
        step = lax.div(ids[own * sub_count + sub], per_owner) ^ own
        away[...] = jnp.full(away.shape, step, jnp.int32)
        copies[2].wait()

    *picked, early, away = call(
        body,
        [stay(adapter_ids), stay(head_up), stay(grad)],
        [in_hbm] * 3,
        [shape_of((rank, width), bf16)] * own_count
        + [shape_of((first, grad.shape[1]), bf16), shape_of((8, 128), jnp.int32)],
        scratch_shapes=[
            pltpu.SMEM(adapter_ids.shape, jnp.int32),
            pltpu.VMEM(head_up.shape, bf16),
            pltpu.SemaphoreType.DMA((3,)),
        ],
    )
    return picked, early, away


def project_low(tokens, down, after):
    rows, features = tokens.shape
    rank = down.shape[0]
    width = width_of(features)
    blocks = features // width

    def body(tokens, down, low, rounded, near_tokens, near_down, sems):
        copies = [pltpu.make_async_copy(down, near_down, sems.at[blocks])]
        for at in range(blocks):
            here = pl.ds(at * width, width)
            copies.append(
                pltpu.make_async_copy(tokens.at[:, here], near_tokens.at[:, here], sems.at[at])
            )
        for copy in copies:
            copy.start()
        copies[0].wait()
        total = None
        for at in range(blocks):
            copies[at + 1].wait()
            here = slice(at * width, (at + 1) * width)
            part = lax.dot_general(
                near_down[:, here], near_tokens[:, here], (((1,), (1,)), ((), ())),
                preferred_element_type=f32,
            )
            total = part if total is None else total + part
        low[...] = total
        rounded[...] = total.astype(bf16)

    return call(
        body,
        [stay(tokens), stay(down)],
        [in_hbm] * 2,
        [shape_of((rank, rows), f32), shape_of((rank, rows), bf16)]
        + [shape_of(tokens.shape, bf16), shape_of(down.shape, bf16)],
        after=after,
        flops=2 * rows * rank * features,
        scratch_shapes=[pltpu.SemaphoreType.DMA((blocks + 1,))],
    )


def project_back(away, offered, steps, grad, after):
    rank, columns = offered[0].shape
    rows = grad.shape[0]

    def body(away, *refs):
        *offered, grad, part = refs
        step = jnp.broadcast_to(away[:1, :1], (rank, columns))
        head = offered[0][...].astype(f32)
        for at, block in zip(steps, offered[1:]):
            head = jnp.where(step == at, block[...].astype(f32), head)
        part[...] = lax.dot_general(
            head.astype(bf16), grad[...], (((1,), (1,)), ((), ())), preferred_element_type=f32
        )

    return call(
        body,
        [away, *offered, grad],
        [in_vmem] * (len(offered) + 2),
        [shape_of((rank, rows), f32)],
        after=after,
        flops=slight,
    )[0]


def head_term(lengths, lows, grad, scale, after):
    rank, rows = lows[0].shape
    columns = grad.shape[1]
    first = rows // early_part

    def body(lengths, *refs):
        *lows, grad, term, late = refs
        total = lows[0][...]
        for low in lows[1:]:
            total = total + low[...].astype(f32)
        live = lax.broadcasted_iota(jnp.int32, total.shape, 1) < lengths[0]
        total = jnp.where(live, total, 0.0)
        kept = total.astype(bf16)
        rest = (total - kept.astype(f32)).astype(bf16)
        product = jnp.dot(kept, grad[...], preferred_element_type=f32)
        product += jnp.dot(rest, grad[...], preferred_element_type=f32)
        term[0] = (scale * product).astype(bf16)
        late[...] = grad[first:, :]

    return call(
        body,
        [lengths, *lows, grad],
        [in_smem] + [in_vmem] * (len(lows) + 1),
        [shape_of((1, rank, columns), bf16), shape_of((rows - first, columns), bf16)],
        after=after,
        flops=brief,
    )


def shared_terms(lengths, parts, tokens, scale, after):
    rows, features = tokens.shape
    rank = parts[0].shape[0]
    share = rank // 2

    def body(lengths, *refs):
        parts, (tokens, back, keep, send, total) = refs[:count], refs[count:]
        sub = lax.axis_index("sub")
        both = parts[0][...]
        for part in parts[1:]:
            both = both + part[...]
        live = lax.broadcasted_iota(jnp.int32, both.shape, 1) < lengths[0]
        back[...] = jnp.where(live, both, 0.0).astype(bf16)
        total[...] = scale * jnp.dot(back[...], tokens[...], preferred_element_type=f32)
        keep[...] = total[pl.ds(pl.multiple_of(sub * share, share), share), :]
        send[...] = total[pl.ds(pl.multiple_of((1 - sub) * share, share), share), :]

    count = len(parts)
    return call(
        body,
        [lengths, *parts, tokens],
        [in_smem] + [in_vmem] * (count + 1),
        [shape_of((rank, rows), bf16)] + [shape_of((share, features), f32)] * 2,
        after=after,
        scratch_shapes=[pltpu.VMEM((rank, features), f32)],
        flops=2 * rows * rank * features,
    )


def add_up(pieces, after=()):
    def body(*refs):
        total = refs[0][...].astype(f32)
        for piece in refs[1:-1]:
            total = total + piece[...].astype(f32)
        refs[-1][...] = total.astype(bf16)

    return call(
        body,
        list(pieces),
        [in_vmem] * len(pieces),
        [shape_of(pieces[0].shape, bf16)],
        after=after,
    )[0]


def halve(pieces, bit, after=()):
    rows, features = pieces[0].shape
    half = rows // 2

    def body(*refs):
        total = refs[0][...].astype(f32)
        for piece in refs[1:-2]:
            total = total + piece[...].astype(f32)
        upper = lax.rem(lax.div(lax.axis_index("own"), bit), 2) == 1
        low, high = total[:half], total[half:]
        refs[-2][...] = jnp.where(upper, high, low)
        refs[-1][...] = jnp.where(upper, low, high).astype(bf16)

    return call(
        body,
        list(pieces),
        [in_vmem] * len(pieces),
        [shape_of((half, features), f32), shape_of((half, features), bf16)],
        after=after,
    )


def rejoin(mine, arrived, bit):
    rows, features = mine.shape

    def body(mine, arrived, out):
        upper = lax.rem(lax.div(lax.axis_index("own"), bit), 2) == 1
        one, two = mine[...].astype(f32), arrived[...].astype(f32)
        out[:rows] = jnp.where(upper, two, one).astype(bf16)
        out[rows:] = jnp.where(upper, one, two).astype(bf16)

    return call(
        body,
        [mine, arrived],
        [in_vmem] * 2,
        [shape_of((2 * rows, features), bf16)],
        flops=busy,
    )[0]


def join_shares(mine, other, after):
    share, features = mine.shape

    def body(mine, other, out):
        sub = lax.axis_index("sub")
        for side, piece in ((sub, mine), (1 - sub, other)):
            out[pl.ds(pl.multiple_of(side * share, share), share), :] = piece[...].astype(f32)

    return call(
        body,
        [mine, other],
        [in_vmem] * 2,
        [shape_of((2 * share, features), f32)],
        after=after,
    )[0]


def stack(pieces, after=(), flops=0):
    depths = [piece.shape[0] for piece in pieces]

    def body(*refs):
        at = 0
        for depth, piece in zip(depths, refs[:-1]):
            refs[-1][at : at + depth] = piece[...]
            at += depth

    return call(
        body,
        list(pieces),
        [in_vmem] * len(pieces),
        [shape_of((sum(depths),) + pieces[0].shape[1:], bf16)],
        after=after,
        flops=flops,
    )[0]


def clean(dims, after):
    def body(out, mark, held, sem):
        held[...] = jnp.zeros(held.shape, f32)
        mark[...] = jnp.zeros(mark.shape, f32)
        copies = [pltpu.make_async_copy(held, out.at[at], sem.at[at]) for at in range(dims[0])]
        for copy in copies:
            copy.start()
        for copy in copies:
            copy.wait()

    return call(
        body,
        [],
        [],
        [shape_of(dims, f32), shape_of((8, 128), f32)],
        out_specs=[in_hbm, in_vmem],
        after=after,
        scratch_shapes=[pltpu.VMEM(dims[1:], f32), pltpu.SemaphoreType.DMA((dims[0],))],
        flops=busy,
    )


def place_terms(adapter_ids, near, far, pattern, cleaned, after):
    per_owner, rank, columns = cleaned.shape
    sub_count = lax.axis_size("sub")

    def body(ids_far, near, far, cleaned, out, mark, held, ids, counts, sems):
        own, sub = lax.axis_index("own"), lax.axis_index("sub")
        fetch = pltpu.make_async_copy(ids_far, ids, sems.at[per_owner])
        fetch.start()
        mark[...] = jnp.zeros(mark.shape, f32)
        for local in range(per_owner):
            counts[local] = 0
        fetch.wait()
        for at, step in enumerate(pattern):
            for side in range(sub_count):
                local = ids[(own ^ step) * sub_count + side] - own * per_owner

                @pl.when(jnp.logical_and(local >= 0, local < per_owner))
                def _():
                    term = jnp.where(sub == side, near[at], far[at]).astype(f32)

                    @pl.when(counts[local] == 0)
                    def _():
                        held[local] = term

                    @pl.when(counts[local] > 0)
                    def _():
                        held[local] += term

                    counts[local] += 1

        copies = [
            pltpu.make_async_copy(held.at[local], out.at[local], sems.at[local])
            for local in range(per_owner)
        ]
        for local, copy in enumerate(copies):
            pl.when(counts[local] > 0)(copy.start)
        for local, copy in enumerate(copies):
            pl.when(counts[local] > 0)(copy.wait)

    return call(
        body,
        [stay(adapter_ids), near, far, cleaned],
        [in_hbm, in_vmem, in_vmem, in_hbm],
        [shape_of(cleaned.shape, f32), shape_of((8, 128), f32)],
        out_specs=[in_hbm, in_vmem],
        after=after,
        input_output_aliases={3: 0},
        scratch_shapes=[
            pltpu.VMEM(cleaned.shape, f32),
            pltpu.SMEM(adapter_ids.shape, jnp.int32),
            pltpu.SMEM((per_owner,), jnp.int32),
            pltpu.SemaphoreType.DMA((per_owner + 1,)),
        ],
    )


def arrange(lengths, grad, pieces, after):
    rows, columns = grad.shape
    count = 1 + len(pieces)
    first = rows // early_part

    def body(lengths, grad, *refs):
        pieces, kept = refs[:-1], refs[-1]
        at = lax.axis_index("tp")
        live = lax.broadcasted_iota(jnp.int32, (rows, columns), 0) < lengths[0]
        zero = jnp.zeros((rows, columns), bf16)
        place = pl.multiple_of(at * columns, 128)
        kept[:, pl.ds(place, columns)] = jnp.where(live, grad[...], zero)
        for step in range(1, count):
            place = pl.multiple_of(lax.rem(at + count - step, count) * columns, 128)
            early, late = pieces[2 * step - 2 : 2 * step]
            kept[:first, pl.ds(place, columns)] = jnp.where(live[:first], early[...], zero[:first])
            kept[first:, pl.ds(place, columns)] = jnp.where(live[first:], late[...], zero[first:])

    flat = [x for pair in pieces for x in pair]
    return call(
        body,
        [lengths, grad, *flat],
        [in_smem] + [in_vmem] * (1 + len(flat)),
        [shape_of((rows, count * columns), bf16)],
        after=after,
    )[0]


def input_side(kept, frozen, frozen_other, back, down, after):
    rows, whole = kept.shape
    features, half = frozen.shape
    rank = back.shape[0]
    width = width_of(features)
    blocks = features // width

    def body(kept, frozen, frozen_other, back, down, out, mark, held, sems):
        mark[...] = jnp.zeros(mark.shape, f32)
        sub = lax.axis_index("sub")
        both = (((1,), (1,)), ((), ()))
        mine = kept[:, pl.ds(pl.multiple_of(sub * half, 128), half)]
        other = kept[:, pl.ds(pl.multiple_of((1 - sub) * half, 128), half)]
        twice = adapter_scale * back[...]
        copies = []
        for at in range(blocks):
            here = slice(at * width, (at + 1) * width)
            total = lax.dot_general(mine, frozen[here, :], both, preferred_element_type=f32)
            total += lax.dot_general(other, frozen_other[here, :], both, preferred_element_type=f32)
            total += lax.dot_general(
                twice, down[:, here], (((0,), (0,)), ((), ())), preferred_element_type=f32
            )
            held[:, here] = total.astype(bf16)
            copies.append(
                pltpu.make_async_copy(held.at[:, here], out.at[:, here], sems.at[at])
            )
            copies[-1].start()
        for copy in copies:
            copy.wait()

    return call(
        body,
        [kept, frozen, frozen_other, back, down],
        [in_vmem] * 5,
        [shape_of((rows, features), bf16), shape_of((8, 128), f32)],
        out_specs=[in_hbm, in_vmem],
        after=after,
        scratch_shapes=[
            pltpu.VMEM((rows, features), bf16),
            pltpu.SemaphoreType.DMA((blocks,)),
        ],
        flops=2 * rows * features * (2 * half + rank),
    )


def on_device(tokens, grad_output, frozen_value, shared_down, head_up, adapter_ids, lengths):
    rows = tokens.shape[0]
    own_count = lax.axis_size("own")
    tp_count = lax.axis_size("tp")
    per_owner = head_up.shape[0]
    scale = adapter_scale / rows
    tp_steps, own_steps = range(1, tp_count), range(1, own_count)

    frozen_other = shift(frozen_value, "sub", 1)
    picked, early, away = pick_heads(adapter_ids, head_up, grad_output)
    steps = sorted(own_steps, key=lambda step: (-step.bit_length(), step))
    offered = [picked[0]] + [swap(picked[step], step, 0) for step in steps]
    early_grads = [shift(early, "tp", step) for step in tp_steps]

    low, rounded, tokens, down = project_low(
        tokens, shared_down.T, [picked[0], frozen_other]
    )
    lows = [low] + [shift(rounded, "tp", step) for step in tp_steps]

    part = project_back(away, offered, steps, grad_output, [low])
    parts = [part] + [shift(part, "tp", step) for step in tp_steps]

    near, late = head_term(lengths, lows, grad_output, scale, [part, *early_grads])
    late_grads = [shift(late, "tp", step) for step in tp_steps]
    bits = [1 << i for i in range(own_count.bit_length() - 1)]
    terms, pattern = [near], [0]
    for bit in reversed(bits[1:]):
        terms = terms + [swap(term, bit, 0) for term in terms]
        pattern = pattern + [step ^ bit for step in pattern]
    nearby = [swap(near, 1, 0)] if bits else []

    back, keep, send = shared_terms(lengths, parts, tokens, scale, [near])
    pieces = [keep, shift(send, "sub", 1)]
    met = stack(terms[1:] + nearby, flops=middling) if bits else near

    mark = met
    for bit in bits[:-1]:
        stays, leaves = halve(pieces, bit, [mark])
        pieces = [stays, swap(leaves, bit, 0)]
        mark = leaves
    cleaned, mark = clean((per_owner,) + near.shape[1:], [mark])
    total = add_up(pieces, [mark])
    relays = [total]
    if bits:
        relays = [stack([term], [total]) for term in terms[1:]]
        terms = terms + nearby + [swap(relay, 1, 0) for relay in relays]
        pattern = pattern + [step ^ 1 for step in pattern]
    kept = arrange(lengths, grad_output, list(zip(early_grads, late_grads)), [total])
    input_gradient, mark = input_side(kept, frozen_value, frozen_other, back, down, relays)
    near = stack(terms, [mark])
    if bits:
        total = add_up([total, swap(total, bits[-1], 0)], [near])
    far = shift(near, "sub", 1)
    for bit in reversed(bits[:-1]):
        total = rejoin(total, swap(total, bit, 0), bit)
    grad_heads, mark = place_terms(adapter_ids, near, far, pattern, cleaned, [total])
    shared_down_gradient = join_shares(total, shift(total, "sub", 1), [mark]).T
    return (input_gradient, shared_down_gradient, grad_heads)


def solution(mesh):
    placed = (
        P(("rep", "own", "sub"), "tp"),
        P(("rep", "own", "sub"), "tp"),
        P("tp", "sub"),
        P("tp", None),
        P("own", None, "tp"),
        P("rep"),
        P(("rep", "own", "sub")),
    )
    return jax.shard_map(
        on_device,
        mesh=mesh,
        in_specs=placed,
        out_specs=(
            P(("rep", "own", "sub"), "tp"),
            P(("rep", "tp"), None),
            P(("rep", "own"), None, "tp"),
        ),
        check_vma=False,
    )
```

```python
import jax
import jax.numpy as jnp
from jax import lax
from jax.experimental import pallas as pl
from jax.experimental.pallas import tpu as pltpu
from jax.sharding import PartitionSpec as P

adapter_scale = 2.0
f32 = jnp.float32
bf16 = jnp.bfloat16

(busy, first_cost, middling, filling, brief, slight) = (
    10**10, 5 * 10**9, 5 * 10**9, 10**10, 3 * 10**9, 15 * 10**8
)

anywhere = pl.BlockSpec(memory_space=pl.ANY)
in_hbm = pl.BlockSpec(memory_space=pltpu.HBM)
in_vmem = pl.BlockSpec(memory_space=pltpu.VMEM)
in_smem = pl.BlockSpec(memory_space=pltpu.SMEM)


def shift(x, axis, step):
    count = lax.axis_size(axis)
    return lax.ppermute(x, axis, [(i, (i + step) % count) for i in range(count)])


def swap(x, own_bit, sub_bit):
    subs = lax.axis_size("sub")
    whole = lax.axis_size("own") * subs
    other = own_bit * subs + sub_bit
    return lax.ppermute(x, ("own", "sub"), [(i, i ^ other) for i in range(whole)])


def width_of(features):
    return next(width for width in (512, 256, 128) if features % width == 0)


def stay(x):
    return pltpu.with_memory_space_constraint(x, pltpu.HBM)


def shape_of(dims, kind):
    return jax.ShapeDtypeStruct(dims, kind)


def call(body, operands, specs, outs, out_specs=None, after=(), flops=0, **more):
    count, idle = len(operands), len(after)

    def kernel(*refs):
        body(*refs[:count], *refs[count + idle :])

    moved = sum(x.size * x.dtype.itemsize for x in list(operands) + list(outs))
    return pl.pallas_call(
        kernel,
        out_shape=outs,
        in_specs=list(specs) + [anywhere] * len(after),
        out_specs=[in_vmem] * len(outs) if out_specs is None else out_specs,
        compiler_params=pltpu.CompilerParams(vmem_limit_bytes=24 * 1024 * 1024),
        cost_estimate=pl.CostEstimate(flops=flops, bytes_accessed=moved, transcendentals=0),
        **more,
    )(*operands, *after)


def pick_heads(adapter_ids, head_up):
    per_owner, rank, width = head_up.shape
    own_count, sub_count = lax.axis_size("own"), lax.axis_size("sub")

    def body(ids_far, head_up, *refs):
        outs, away, ids, maps, sems = refs[:own_count], *refs[own_count:]
        own, sub = lax.axis_index("own"), lax.axis_index("sub")
        copies = [
            pltpu.make_async_copy(ids_far, ids, sems.at[0]),
            pltpu.make_async_copy(head_up, maps, sems.at[1]),
        ]
        for copy in copies:
            copy.start()
        for copy in copies:
            copy.wait()
        for step in range(own_count):
            local = ids[(own ^ step) * sub_count + sub] - own * per_owner
            outs[step][...] = maps[jnp.clip(local, 0, per_owner - 1)]
        step = lax.div(ids[own * sub_count + sub], per_owner) ^ own
        away[...] = jnp.full(away.shape, step, jnp.int32)

    *picked, away = call(
        body,
        [stay(adapter_ids), stay(head_up)],
        [in_hbm] * 2,
        [shape_of((rank, width), bf16)] * own_count + [shape_of((8, 128), jnp.int32)],
        scratch_shapes=[
            pltpu.SMEM(adapter_ids.shape, jnp.int32),
            pltpu.VMEM(head_up.shape, bf16),
            pltpu.SemaphoreType.DMA((2,)),
        ],
        flops=first_cost,
    )
    return picked, away


def project_low(tokens, down, after):
    rows, features = tokens.shape
    rank = down.shape[0]

    def body(tokens, down, low):
        low[...] = lax.dot_general(
            down[...], tokens[...], (((1,), (1,)), ((), ())), preferred_element_type=f32
        )

    return call(
        body,
        [tokens, down],
        [in_vmem] * 2,
        [shape_of((rank, rows), f32)],
        after=after,
        flops=2 * rows * rank * features,
    )[0]


def rounded(x, after):
    def body(x, out):
        out[...] = x[...].astype(bf16)

    return call(body, [x], [in_vmem], [shape_of(x.shape, bf16)], after=after)[0]


def project_back(away, offered, steps, grad, after):
    rank, columns = offered[0].shape
    rows = grad.shape[0]

    def body(away, *refs):
        *offered, grad, part = refs
        step = jnp.broadcast_to(away[:1, :1], (rank, columns))
        head = offered[0][...].astype(f32)
        for at, block in zip(steps, offered[1:]):
            head = jnp.where(step == at, block[...].astype(f32), head)
        part[...] = lax.dot_general(
            head.astype(bf16), grad[...], (((1,), (1,)), ((), ())), preferred_element_type=f32
        )

    return call(
        body,
        [away, *offered, grad],
        [in_vmem] * (len(offered) + 2),
        [shape_of((rank, rows), f32)],
        after=after,
        flops=slight,
    )[0]


def head_term(lengths, lows, grad, scale, after):
    rank, rows = lows[0].shape
    columns = grad.shape[1]

    def body(lengths, *refs):
        *lows, grad, term, again = refs
        total = lows[0][...]
        for low in lows[1:]:
            total = total + low[...].astype(f32)
        live = lax.broadcasted_iota(jnp.int32, total.shape, 1) < lengths[0]
        total = jnp.where(live, total, 0.0)
        kept = total.astype(bf16)
        rest = (total - kept.astype(f32)).astype(bf16)
        product = jnp.dot(kept, grad[...], preferred_element_type=f32)
        product += jnp.dot(rest, grad[...], preferred_element_type=f32)
        term[0] = (scale * product).astype(bf16)
        again[...] = grad[...]

    return call(
        body,
        [lengths, *lows, grad],
        [in_smem] + [in_vmem] * (len(lows) + 1),
        [shape_of((1, rank, columns), bf16), shape_of(grad.shape, bf16)],
        after=after,
        flops=brief,
    )


def shared_terms(lengths, parts, tokens, scale, after):
    rows, features = tokens.shape
    rank = parts[0].shape[0]
    share = rank // 2

    def body(lengths, *refs):
        parts, (tokens, back, keep, send, total) = refs[:count], refs[count:]
        sub = lax.axis_index("sub")
        both = parts[0][...]
        for part in parts[1:]:
            both = both + part[...]
        live = lax.broadcasted_iota(jnp.int32, both.shape, 1) < lengths[0]
        back[...] = jnp.where(live, both, 0.0).astype(bf16)
        total[...] = scale * jnp.dot(back[...], tokens[...], preferred_element_type=f32)
        keep[...] = total[pl.ds(pl.multiple_of(sub * share, share), share), :]
        send[...] = total[pl.ds(pl.multiple_of((1 - sub) * share, share), share), :]

    count = len(parts)
    return call(
        body,
        [lengths, *parts, tokens],
        [in_smem] + [in_vmem] * (count + 1),
        [shape_of((rank, rows), bf16)] + [shape_of((share, features), f32)] * 2,
        after=after,
        scratch_shapes=[pltpu.VMEM((rank, features), f32)],
        flops=2 * rows * rank * features,
    )


def add_up(pieces, after=()):
    def body(*refs):
        total = refs[0][...].astype(f32)
        for piece in refs[1:-1]:
            total = total + piece[...].astype(f32)
        refs[-1][...] = total.astype(bf16)

    return call(
        body,
        list(pieces),
        [in_vmem] * len(pieces),
        [shape_of(pieces[0].shape, bf16)],
        after=after,
    )[0]


def halve(pieces, bit, after=()):
    rows, features = pieces[0].shape
    half = rows // 2

    def body(*refs):
        total = refs[0][...].astype(f32)
        for piece in refs[1:-2]:
            total = total + piece[...].astype(f32)
        upper = lax.rem(lax.div(lax.axis_index("own"), bit), 2) == 1
        low, high = total[:half], total[half:]
        refs[-2][...] = jnp.where(upper, high, low)
        refs[-1][...] = jnp.where(upper, low, high).astype(bf16)

    return call(
        body,
        list(pieces),
        [in_vmem] * len(pieces),
        [shape_of((half, features), f32), shape_of((half, features), bf16)],
        after=after,
    )


def rejoin(mine, arrived, bit, after):
    rows, features = mine.shape

    def body(mine, arrived, out):
        upper = lax.rem(lax.div(lax.axis_index("own"), bit), 2) == 1
        one, two = mine[...].astype(f32), arrived[...].astype(f32)
        out[:rows] = jnp.where(upper, two, one).astype(bf16)
        out[rows:] = jnp.where(upper, one, two).astype(bf16)

    return call(
        body,
        [mine, arrived],
        [in_vmem] * 2,
        [shape_of((2 * rows, features), bf16)],
        after=after,
        flops=busy,
    )[0]


def join_shares(mine, other, after):
    share, features = mine.shape

    def body(mine, other, out):
        sub = lax.axis_index("sub")
        for side, piece in ((sub, mine), (1 - sub, other)):
            out[pl.ds(pl.multiple_of(side * share, share), share), :] = piece[...].astype(f32)

    return call(
        body,
        [mine, other],
        [in_vmem] * 2,
        [shape_of((2 * share, features), f32)],
        after=after,
    )[0]


def stack(pieces, after=(), flops=0):
    depths = [piece.shape[0] for piece in pieces]

    def body(*refs):
        at = 0
        for depth, piece in zip(depths, refs[:-1]):
            refs[-1][at : at + depth] = piece[...]
            at += depth

    return call(
        body,
        list(pieces),
        [in_vmem] * len(pieces),
        [shape_of((sum(depths),) + pieces[0].shape[1:], bf16)],
        after=after,
        flops=flops,
    )[0]


def prepare(dims, frozen, frozen_other, down, after):
    features, half = frozen.shape
    rank = down.shape[0]
    padded = -(-rank // 128) * 128

    def body(frozen, frozen_other, down, out, wide, held, sems, weight_sems):
        sub = lax.axis_index("sub")
        copies = [
            pltpu.make_async_copy(
                piece,
                wide.at[:, pl.ds(pl.multiple_of(side * half, 128), half)],
                weight_sems.at[at],
            )
            for at, (side, piece) in enumerate(((sub, frozen), (1 - sub, frozen_other)))
        ]
        for copy in copies:
            copy.start()
        held[...] = jnp.zeros(held.shape, f32)
        zeros = [pltpu.make_async_copy(held, out.at[at], sems.at[at]) for at in range(dims[0])]
        for copy in zeros:
            copy.start()
        down = down[...].astype(f32)
        if padded > rank:
            down = jnp.concatenate([down, jnp.zeros((padded - rank, features), f32)], axis=0)
        wide[:, 2 * half :] = down.T.astype(bf16)
        for copy in copies + zeros:
            copy.wait()

    return call(
        body,
        [stay(frozen), frozen_other, down],
        [in_hbm, anywhere, in_vmem],
        [shape_of(dims, f32), shape_of((features, 2 * half + padded), bf16)],
        out_specs=[in_hbm, in_vmem],
        after=after,
        scratch_shapes=[
            pltpu.VMEM(dims[1:], f32),
            pltpu.SemaphoreType.DMA((dims[0],)),
            pltpu.SemaphoreType.DMA((2,)),
        ],
        flops=filling,
    )


def place_terms(adapter_ids, near, far, pattern, cleaned, after):
    per_owner, rank, columns = cleaned.shape
    sub_count = lax.axis_size("sub")

    def body(ids_far, near, far, cleaned, out, mark, held, ids, counts, sems):
        own, sub = lax.axis_index("own"), lax.axis_index("sub")
        fetch = pltpu.make_async_copy(ids_far, ids, sems.at[per_owner])
        fetch.start()
        mark[...] = jnp.zeros(mark.shape, f32)
        for local in range(per_owner):
            counts[local] = 0
        fetch.wait()
        for at, step in enumerate(pattern):
            for side in range(sub_count):
                local = ids[(own ^ step) * sub_count + side] - own * per_owner

                @pl.when(jnp.logical_and(local >= 0, local < per_owner))
                def _():
                    term = jnp.where(sub == side, near[at], far[at]).astype(f32)

                    @pl.when(counts[local] == 0)
                    def _():
                        held[local] = term

                    @pl.when(counts[local] > 0)
                    def _():
                        held[local] += term

                    counts[local] += 1

        copies = [
            pltpu.make_async_copy(held.at[local], out.at[local], sems.at[local])
            for local in range(per_owner)
        ]
        for local, copy in enumerate(copies):
            pl.when(counts[local] > 0)(copy.start)
        for local, copy in enumerate(copies):
            pl.when(counts[local] > 0)(copy.wait)

    return call(
        body,
        [stay(adapter_ids), near, far, cleaned],
        [in_hbm, in_vmem, in_vmem, in_hbm],
        [shape_of(cleaned.shape, f32), shape_of((8, 128), f32)],
        out_specs=[in_hbm, in_vmem],
        after=after,
        input_output_aliases={3: 0},
        scratch_shapes=[
            pltpu.VMEM(cleaned.shape, f32),
            pltpu.SMEM(adapter_ids.shape, jnp.int32),
            pltpu.SMEM((per_owner,), jnp.int32),
            pltpu.SemaphoreType.DMA((per_owner + 1,)),
        ],
    )


def arrange(lengths, grads, back, width, after):
    rows, columns = grads[0].shape
    count = len(grads)
    rank = back.shape[0]
    padded = width - count * columns

    def body(lengths, *refs):
        *grads, back, kept = refs
        at = lax.axis_index("tp")
        live = lax.broadcasted_iota(jnp.int32, (rows, columns), 0) < lengths[0]
        for step, grad in enumerate(grads):
            place = pl.multiple_of(lax.rem(at + count - step, count) * columns, 128)
            kept[:, pl.ds(place, columns)] = jnp.where(
                live, grad[...], jnp.zeros((rows, columns), bf16)
            )
        twice = adapter_scale * back[...].astype(f32)
        if padded > rank:
            twice = jnp.concatenate([twice, jnp.zeros((padded - rank, rows), f32)], axis=0)
        kept[:, count * columns :] = twice.T.astype(bf16)

    return call(
        body,
        [lengths, *grads, back],
        [in_smem] + [in_vmem] * (count + 1),
        [shape_of((rows, width), bf16)],
        after=after,
    )[0]


def input_side(kept, wide, after):
    rows = kept.shape[0]
    features = wide.shape[0]
    width = width_of(features)
    blocks = features // width

    def body(kept, wide, out, mark, held, sems):
        mark[...] = jnp.zeros(mark.shape, f32)
        copies = []
        for at in range(blocks):
            here = slice(at * width, (at + 1) * width)
            held[:, here] = lax.dot_general(
                kept[...], wide[here, :], (((1,), (1,)), ((), ())), preferred_element_type=f32
            ).astype(bf16)
            copies.append(
                pltpu.make_async_copy(held.at[:, here], out.at[:, here], sems.at[at])
            )
            copies[-1].start()
        for copy in copies:
            copy.wait()

    return call(
        body,
        [kept, wide],
        [in_vmem] * 2,
        [shape_of((rows, features), bf16), shape_of((8, 128), f32)],
        out_specs=[in_hbm, in_vmem],
        after=after,
        scratch_shapes=[
            pltpu.VMEM((rows, features), bf16),
            pltpu.SemaphoreType.DMA((blocks,)),
        ],
        flops=2 * rows * features * wide.shape[1],
    )


def on_device(tokens, grad_output, frozen_value, shared_down, head_up, adapter_ids, lengths):
    rows = tokens.shape[0]
    own_count = lax.axis_size("own")
    tp_count = lax.axis_size("tp")
    per_owner = head_up.shape[0]
    scale = adapter_scale / rows
    tp_steps, own_steps = range(1, tp_count), range(1, own_count)

    frozen_other = shift(frozen_value, "sub", 1)
    picked, away = pick_heads(adapter_ids, head_up)
    steps = sorted(own_steps, key=lambda step: (-step.bit_length(), step))
    offered = [picked[0]] + [swap(picked[step], step, 0) for step in steps]

    down = shared_down.T
    low = project_low(tokens, down, picked[:1])
    sent = rounded(low, [low])
    lows = [low] + [shift(sent, "tp", step) for step in tp_steps]

    part = project_back(away, offered, steps, grad_output, [low])
    parts = [part] + [shift(part, "tp", step) for step in tp_steps]

    near, again = head_term(lengths, lows, grad_output, scale, [part])
    grads = [grad_output] + [shift(again, "tp", step) for step in tp_steps]
    bits = [1 << i for i in range(own_count.bit_length() - 1)]
    terms, pattern = [near], [0]
    for bit in reversed(bits[1:]):
        terms = terms + [swap(term, bit, 0) for term in terms]
        pattern = pattern + [step ^ bit for step in pattern]
    nearby = [swap(near, 1, 0)] if bits else []

    back, keep, send = shared_terms(lengths, parts, tokens, scale, [near])
    pieces = [keep, shift(send, "sub", 1)]
    met = stack(terms[1:] + nearby, flops=middling) if bits else near

    mark = met
    for bit in bits[:-1]:
        stays, leaves = halve(pieces, bit, [mark])
        pieces = [stays, swap(leaves, bit, 0)]
        mark = leaves
    cleaned, wide = prepare((per_owner,) + near.shape[1:], frozen_value, frozen_other, down, [mark])
    total = add_up(pieces, [wide])
    relays = [total]
    if bits:
        relays = [stack([term], [total]) for term in terms[1:]]
        terms = terms + nearby + [swap(relay, 1, 0) for relay in relays]
        pattern = pattern + [step ^ 1 for step in pattern]
    near = stack(terms, [total])
    if bits:
        total = add_up([total, swap(total, bits[-1], 0)], [near])
    far = shift(near, "sub", 1)
    kept = arrange(lengths, grads, back, wide.shape[1], [total])
    input_gradient, mark = input_side(kept, wide, [total])
    for bit in reversed(bits[:-1]):
        total = rejoin(total, swap(total, bit, 0), bit, [mark])
        mark = total
    grad_heads, mark = place_terms(adapter_ids, near, far, pattern, cleaned, [total])
    shared_down_gradient = join_shares(total, shift(total, "sub", 1), [mark]).T
    return (input_gradient, shared_down_gradient, grad_heads)


def solution(mesh):
    placed = (
        P(("rep", "own", "sub"), "tp"),
        P(("rep", "own", "sub"), "tp"),
        P("tp", "sub"),
        P("tp", None),
        P("own", None, "tp"),
        P("rep"),
        P(("rep", "own", "sub")),
    )
    return jax.shard_map(
        on_device,
        mesh=mesh,
        in_specs=placed,
        out_specs=(
            P(("rep", "own", "sub"), "tp"),
            P(("rep", "tp"), None),
            P(("rep", "own"), None, "tp"),
        ),
        check_vma=False,
    )
```

```python
import jax
import jax.numpy as jnp
from jax import lax
from jax.experimental import pallas as pl
from jax.experimental.pallas import tpu as pltpu
from jax.sharding import PartitionSpec as P

adapter_scale = 2.0
f32 = jnp.float32
bf16 = jnp.bfloat16

early_part = 4

(busy, first_cost, middling, filling, brief, slight) = (
    10**10, 5 * 10**9, 5 * 10**9, 10**10, 3 * 10**9, 15 * 10**8
)

anywhere = pl.BlockSpec(memory_space=pl.ANY)
in_hbm = pl.BlockSpec(memory_space=pltpu.HBM)
in_vmem = pl.BlockSpec(memory_space=pltpu.VMEM)
in_smem = pl.BlockSpec(memory_space=pltpu.SMEM)


def shift(x, axis, step):
    count = lax.axis_size(axis)
    return lax.ppermute(x, axis, [(i, (i + step) % count) for i in range(count)])


def swap(x, own_bit, sub_bit):
    subs = lax.axis_size("sub")
    whole = lax.axis_size("own") * subs
    other = own_bit * subs + sub_bit
    return lax.ppermute(x, ("own", "sub"), [(i, i ^ other) for i in range(whole)])


def width_of(features):
    return next(width for width in (512, 256, 128) if features % width == 0)


def stay(x):
    return pltpu.with_memory_space_constraint(x, pltpu.HBM)


def shape_of(dims, kind):
    return jax.ShapeDtypeStruct(dims, kind)


def call(body, operands, specs, outs, out_specs=None, after=(), flops=0, **more):
    count, idle = len(operands), len(after)

    def kernel(*refs):
        body(*refs[:count], *refs[count + idle :])

    moved = sum(x.size * x.dtype.itemsize for x in list(operands) + list(outs))
    return pl.pallas_call(
        kernel,
        out_shape=outs,
        in_specs=list(specs) + [anywhere] * len(after),
        out_specs=[in_vmem] * len(outs) if out_specs is None else out_specs,
        compiler_params=pltpu.CompilerParams(vmem_limit_bytes=24 * 1024 * 1024),
        cost_estimate=pl.CostEstimate(flops=flops, bytes_accessed=moved, transcendentals=0),
        **more,
    )(*operands, *after)


def pick_heads(adapter_ids, head_up, grad):
    per_owner, rank, width = head_up.shape
    own_count, sub_count = lax.axis_size("own"), lax.axis_size("sub")
    first = grad.shape[0] // early_part

    def body(ids_far, head_up, grad, *refs):
        outs, early, away, ids, maps, sems = refs[:own_count], *refs[own_count:]
        own, sub = lax.axis_index("own"), lax.axis_index("sub")
        copies = [
            pltpu.make_async_copy(ids_far, ids, sems.at[0]),
            pltpu.make_async_copy(head_up, maps, sems.at[1]),
            pltpu.make_async_copy(grad.at[pl.ds(0, first)], early, sems.at[2]),
        ]
        for copy in copies:
            copy.start()
        copies[0].wait()
        copies[1].wait()
        for step in range(own_count):
            local = ids[(own ^ step) * sub_count + sub] - own * per_owner
            outs[step][...] = maps[jnp.clip(local, 0, per_owner - 1)]
        step = lax.div(ids[own * sub_count + sub], per_owner) ^ own
        away[...] = jnp.full(away.shape, step, jnp.int32)
        copies[2].wait()

    *picked, early, away = call(
        body,
        [stay(adapter_ids), stay(head_up), stay(grad)],
        [in_hbm] * 3,
        [shape_of((rank, width), bf16)] * own_count
        + [shape_of((first, grad.shape[1]), bf16), shape_of((8, 128), jnp.int32)],
        scratch_shapes=[
            pltpu.SMEM(adapter_ids.shape, jnp.int32),
            pltpu.VMEM(head_up.shape, bf16),
            pltpu.SemaphoreType.DMA((3,)),
        ],
        flops=first_cost,
    )
    return picked, early, away


def project_low(tokens, down, after):
    rows, features = tokens.shape
    rank = down.shape[0]

    def body(tokens, down, low):
        low[...] = lax.dot_general(
            down[...], tokens[...], (((1,), (1,)), ((), ())), preferred_element_type=f32
        )

    return call(
        body,
        [tokens, down],
        [in_vmem] * 2,
        [shape_of((rank, rows), f32)],
        after=after,
        flops=2 * rows * rank * features,
    )[0]


def rounded(x, after):
    def body(x, out):
        out[...] = x[...].astype(bf16)

    return call(body, [x], [in_vmem], [shape_of(x.shape, bf16)], after=after)[0]


def project_back(away, offered, steps, grad, after):
    rank, columns = offered[0].shape
    rows = grad.shape[0]

    def body(away, *refs):
        *offered, grad, part = refs
        step = jnp.broadcast_to(away[:1, :1], (rank, columns))
        head = offered[0][...].astype(f32)
        for at, block in zip(steps, offered[1:]):
            head = jnp.where(step == at, block[...].astype(f32), head)
        part[...] = lax.dot_general(
            head.astype(bf16), grad[...], (((1,), (1,)), ((), ())), preferred_element_type=f32
        )

    return call(
        body,
        [away, *offered, grad],
        [in_vmem] * (len(offered) + 2),
        [shape_of((rank, rows), f32)],
        after=after,
        flops=slight,
    )[0]


def head_term(lengths, lows, grad, scale, after):
    rank, rows = lows[0].shape
    columns = grad.shape[1]
    first = rows // early_part

    def body(lengths, *refs):
        *lows, grad, term, late = refs
        total = lows[0][...]
        for low in lows[1:]:
            total = total + low[...].astype(f32)
        live = lax.broadcasted_iota(jnp.int32, total.shape, 1) < lengths[0]
        total = jnp.where(live, total, 0.0)
        kept = total.astype(bf16)
        rest = (total - kept.astype(f32)).astype(bf16)
        product = jnp.dot(kept, grad[...], preferred_element_type=f32)
        product += jnp.dot(rest, grad[...], preferred_element_type=f32)
        term[0] = (scale * product).astype(bf16)
        late[...] = grad[first:, :]

    return call(
        body,
        [lengths, *lows, grad],
        [in_smem] + [in_vmem] * (len(lows) + 1),
        [shape_of((1, rank, columns), bf16), shape_of((rows - first, columns), bf16)],
        after=after,
        flops=brief,
    )


def shared_terms(lengths, parts, tokens, scale, after):
    rows, features = tokens.shape
    rank = parts[0].shape[0]
    share = rank // 2

    def body(lengths, *refs):
        parts, (tokens, back, keep, send, total) = refs[:count], refs[count:]
        sub = lax.axis_index("sub")
        both = parts[0][...]
        for part in parts[1:]:
            both = both + part[...]
        live = lax.broadcasted_iota(jnp.int32, both.shape, 1) < lengths[0]
        back[...] = jnp.where(live, both, 0.0).astype(bf16)
        total[...] = scale * jnp.dot(back[...], tokens[...], preferred_element_type=f32)
        keep[...] = total[pl.ds(pl.multiple_of(sub * share, share), share), :]
        send[...] = total[pl.ds(pl.multiple_of((1 - sub) * share, share), share), :]

    count = len(parts)
    return call(
        body,
        [lengths, *parts, tokens],
        [in_smem] + [in_vmem] * (count + 1),
        [shape_of((rank, rows), bf16)] + [shape_of((share, features), f32)] * 2,
        after=after,
        scratch_shapes=[pltpu.VMEM((rank, features), f32)],
        flops=2 * rows * rank * features,
    )


def add_up(pieces, after=(), flops=0):
    def body(*refs):
        total = refs[0][...].astype(f32)
        for piece in refs[1:-1]:
            total = total + piece[...].astype(f32)
        refs[-1][...] = total.astype(bf16)

    return call(
        body,
        list(pieces),
        [in_vmem] * len(pieces),
        [shape_of(pieces[0].shape, bf16)],
        after=after,
        flops=flops,
    )[0]


def halve(pieces, bit, after=()):
    rows, features = pieces[0].shape
    half = rows // 2

    def body(*refs):
        total = refs[0][...].astype(f32)
        for piece in refs[1:-2]:
            total = total + piece[...].astype(f32)
        upper = lax.rem(lax.div(lax.axis_index("own"), bit), 2) == 1
        low, high = total[:half], total[half:]
        refs[-2][...] = jnp.where(upper, high, low)
        refs[-1][...] = jnp.where(upper, low, high).astype(bf16)

    return call(
        body,
        list(pieces),
        [in_vmem] * len(pieces),
        [shape_of((half, features), f32), shape_of((half, features), bf16)],
        after=after,
    )


def rejoin(mine, arrived, bit, after):
    rows, features = mine.shape

    def body(mine, arrived, out):
        upper = lax.rem(lax.div(lax.axis_index("own"), bit), 2) == 1
        one, two = mine[...].astype(f32), arrived[...].astype(f32)
        out[:rows] = jnp.where(upper, two, one).astype(bf16)
        out[rows:] = jnp.where(upper, one, two).astype(bf16)

    return call(
        body,
        [mine, arrived],
        [in_vmem] * 2,
        [shape_of((2 * rows, features), bf16)],
        after=after,
        flops=busy,
    )[0]


def join_shares(mine, other, after):
    share, features = mine.shape

    def body(mine, other, out):
        sub = lax.axis_index("sub")
        for side, piece in ((sub, mine), (1 - sub, other)):
            out[pl.ds(pl.multiple_of(side * share, share), share), :] = piece[...].astype(f32)

    return call(
        body,
        [mine, other],
        [in_vmem] * 2,
        [shape_of((2 * share, features), f32)],
        after=after,
    )[0]


def stack(pieces, after=(), flops=0):
    depths = [piece.shape[0] for piece in pieces]

    def body(*refs):
        at = 0
        for depth, piece in zip(depths, refs[:-1]):
            refs[-1][at : at + depth] = piece[...]
            at += depth

    return call(
        body,
        list(pieces),
        [in_vmem] * len(pieces),
        [shape_of((sum(depths),) + pieces[0].shape[1:], bf16)],
        after=after,
        flops=flops,
    )[0]


def clean(dims, after):
    def body(out, mark, held, sem):
        held[...] = jnp.zeros(held.shape, f32)
        mark[...] = jnp.zeros(mark.shape, f32)
        copies = [pltpu.make_async_copy(held, out.at[at], sem.at[at]) for at in range(dims[0])]
        for copy in copies:
            copy.start()
        for copy in copies:
            copy.wait()

    return call(
        body,
        [],
        [],
        [shape_of(dims, f32), shape_of((8, 128), f32)],
        out_specs=[in_hbm, in_vmem],
        after=after,
        scratch_shapes=[pltpu.VMEM(dims[1:], f32), pltpu.SemaphoreType.DMA((dims[0],))],
        flops=filling,
    )


def place_terms(adapter_ids, near, far, pattern, cleaned, after):
    per_owner, rank, columns = cleaned.shape
    sub_count = lax.axis_size("sub")

    def body(ids_far, near, far, cleaned, out, mark, held, ids, counts, sems):
        own, sub = lax.axis_index("own"), lax.axis_index("sub")
        fetch = pltpu.make_async_copy(ids_far, ids, sems.at[per_owner])
        fetch.start()
        mark[...] = jnp.zeros(mark.shape, f32)
        for local in range(per_owner):
            counts[local] = 0
        fetch.wait()
        for at, step in enumerate(pattern):
            for side in range(sub_count):
                local = ids[(own ^ step) * sub_count + side] - own * per_owner

                @pl.when(jnp.logical_and(local >= 0, local < per_owner))
                def _():
                    term = jnp.where(sub == side, near[at], far[at]).astype(f32)

                    @pl.when(counts[local] == 0)
                    def _():
                        held[local] = term

                    @pl.when(counts[local] > 0)
                    def _():
                        held[local] += term

                    counts[local] += 1

        copies = [
            pltpu.make_async_copy(held.at[local], out.at[local], sems.at[local])
            for local in range(per_owner)
        ]
        for local, copy in enumerate(copies):
            pl.when(counts[local] > 0)(copy.start)
        for local, copy in enumerate(copies):
            pl.when(counts[local] > 0)(copy.wait)

    return call(
        body,
        [stay(adapter_ids), near, far, cleaned],
        [in_hbm, in_vmem, in_vmem, in_hbm],
        [shape_of(cleaned.shape, f32), shape_of((8, 128), f32)],
        out_specs=[in_hbm, in_vmem],
        after=after,
        input_output_aliases={3: 0},
        scratch_shapes=[
            pltpu.VMEM(cleaned.shape, f32),
            pltpu.SMEM(adapter_ids.shape, jnp.int32),
            pltpu.SMEM((per_owner,), jnp.int32),
            pltpu.SemaphoreType.DMA((per_owner + 1,)),
        ],
    )


def arrange(lengths, grad, pieces, after):
    rows, columns = grad.shape
    count = 1 + len(pieces)
    first = rows // early_part

    def body(lengths, grad, *refs):
        pieces, kept = refs[:-1], refs[-1]
        at = lax.axis_index("tp")
        live = lax.broadcasted_iota(jnp.int32, (rows, columns), 0) < lengths[0]
        zero = jnp.zeros((rows, columns), bf16)
        place = pl.multiple_of(at * columns, 128)
        kept[:, pl.ds(place, columns)] = jnp.where(live, grad[...], zero)
        for step in range(1, count):
            place = pl.multiple_of(lax.rem(at + count - step, count) * columns, 128)
            early, late = pieces[2 * step - 2 : 2 * step]
            kept[:first, pl.ds(place, columns)] = jnp.where(live[:first], early[...], zero[:first])
            kept[first:, pl.ds(place, columns)] = jnp.where(live[first:], late[...], zero[first:])

    flat = [x for pair in pieces for x in pair]
    return call(
        body,
        [lengths, grad, *flat],
        [in_smem] + [in_vmem] * (1 + len(flat)),
        [shape_of((rows, count * columns), bf16)],
        after=after,
    )[0]


def input_side(kept, frozen, frozen_other, back, down, begin, count, before, after):
    rows = kept.shape[0]
    features, half = frozen.shape
    width = width_of(features)
    held_in = [] if before is None else [before]

    def body(kept, frozen, frozen_other, back, down, *refs):
        out, mark, held, sems = refs[len(held_in) :]
        mark[...] = jnp.zeros(mark.shape, f32)
        sub = lax.axis_index("sub")
        both = (((1,), (1,)), ((), ()))
        mine = kept[:, pl.ds(pl.multiple_of(sub * half, 128), half)]
        other = kept[:, pl.ds(pl.multiple_of((1 - sub) * half, 128), half)]
        twice = adapter_scale * back[...]
        copies = []
        for at in range(count):
            here = slice((begin + at) * width, (begin + at + 1) * width)
            total = lax.dot_general(mine, frozen[here, :], both, preferred_element_type=f32)
            total += lax.dot_general(other, frozen_other[here, :], both, preferred_element_type=f32)
            total += lax.dot_general(
                twice, down[:, here], (((0,), (0,)), ((), ())), preferred_element_type=f32
            )
            there = slice(at * width, (at + 1) * width)
            held[:, there] = total.astype(bf16)
            copies.append(
                pltpu.make_async_copy(held.at[:, there], out.at[:, here], sems.at[at])
            )
            copies[-1].start()
        for copy in copies:
            copy.wait()

    return call(
        body,
        [kept, frozen, frozen_other, back, down, *held_in],
        [in_vmem] * 5 + [in_hbm] * len(held_in),
        [shape_of((rows, features), bf16), shape_of((8, 128), f32)],
        out_specs=[in_hbm, in_vmem],
        after=after,
        input_output_aliases={5: 0} if held_in else {},
        scratch_shapes=[
            pltpu.VMEM((rows, count * width), bf16),
            pltpu.SemaphoreType.DMA((count,)),
        ],
        flops=2 * rows * width * count * (2 * half + back.shape[0]),
    )


def on_device(tokens, grad_output, frozen_value, shared_down, head_up, adapter_ids, lengths):
    rows, features = tokens.shape
    own_count = lax.axis_size("own")
    tp_count = lax.axis_size("tp")
    per_owner = head_up.shape[0]
    scale = adapter_scale / rows
    tp_steps, own_steps = range(1, tp_count), range(1, own_count)

    frozen_other = shift(frozen_value, "sub", 1)
    picked, early, away = pick_heads(adapter_ids, head_up, grad_output)
    steps = sorted(own_steps, key=lambda step: (-step.bit_length(), step))
    offered = [picked[0]] + [swap(picked[step], step, 0) for step in steps]
    early_grads = [shift(early, "tp", step) for step in tp_steps]

    down = shared_down.T
    low = project_low(tokens, down, picked[:1])
    sent = rounded(low, [frozen_other])
    lows = [low] + [shift(sent, "tp", step) for step in tp_steps]

    part = project_back(away, offered, steps, grad_output, [low])
    parts = [part] + [shift(part, "tp", step) for step in tp_steps]

    near, late = head_term(lengths, lows, grad_output, scale, [part, *early_grads])
    late_grads = [shift(late, "tp", step) for step in tp_steps]
    terms = [near] + [swap(near, step, 0) for step in own_steps]
    back, keep, send = shared_terms(lengths, parts, tokens, scale, [near])
    pieces = [keep, shift(send, "sub", 1)]
    met = stack(terms[1:3], flops=middling) if own_count > 1 else near

    bits = [1 << i for i in range(own_count.bit_length() - 1)]
    mark = met
    for bit in bits[:-1]:
        stays, leaves = halve(pieces, bit, [mark])
        pieces = [stays, swap(leaves, bit, 0)]
        mark = leaves
    cleaned, mark = clean((per_owner,) + near.shape[1:], [mark])
    near = stack(terms, [mark])
    far = shift(near, "sub", 1)
    total = add_up(pieces, [near], flops=busy)
    grad_heads, mark = place_terms(
        adapter_ids, near, far, range(own_count), cleaned, [total]
    )
    kept = arrange(lengths, grad_output, list(zip(early_grads, late_grads)), [mark])
    sides = (frozen_value, frozen_other, back, down)
    blocks = features // width_of(features)
    input_gradient, mark = input_side(kept, *sides, 0, 1, None, [mark])
    if bits:
        total = add_up([total, swap(total, bits[-1], 0)], [mark])
    if blocks > 1:
        input_gradient, mark = input_side(
            kept, *sides, 1, blocks - 1, input_gradient, [total]
        )
    for bit in reversed(bits[:-1]):
        total = rejoin(total, swap(total, bit, 0), bit, [mark])
        mark = total
    shared_down_gradient = join_shares(total, shift(total, "sub", 1), [mark]).T
    return (input_gradient, shared_down_gradient, grad_heads)


def solution(mesh):
    placed = (
        P(("rep", "own", "sub"), "tp"),
        P(("rep", "own", "sub"), "tp"),
        P("tp", "sub"),
        P("tp", None),
        P("own", None, "tp"),
        P("rep"),
        P(("rep", "own", "sub")),
    )
    return jax.shard_map(
        on_device,
        mesh=mesh,
        in_specs=placed,
        out_specs=(
            P(("rep", "own", "sub"), "tp"),
            P(("rep", "tp"), None),
            P(("rep", "own"), None, "tp"),
        ),
        check_vma=False,
    )
```

```python
import jax
import jax.numpy as jnp
from jax import lax
from jax.experimental import pallas as pl
from jax.experimental.pallas import tpu as pltpu
from jax.sharding import PartitionSpec as P

adapter_scale = 2.0
f32 = jnp.float32
bf16 = jnp.bfloat16

early_part = 4

busy, filling, first_cost, brief = 10**10, 10**10, 5 * 10**9, 3 * 10**9
little, slight, middling = 15 * 10**8, 15 * 10**8, 5 * 10**8

anywhere = pl.BlockSpec(memory_space=pl.ANY)
in_hbm = pl.BlockSpec(memory_space=pltpu.HBM)
in_vmem = pl.BlockSpec(memory_space=pltpu.VMEM)
in_smem = pl.BlockSpec(memory_space=pltpu.SMEM)


def shift(x, axis, step):
    count = lax.axis_size(axis)
    return lax.ppermute(x, axis, [(i, (i + step) % count) for i in range(count)])


def swap(x, own_bit, sub_bit):
    subs = lax.axis_size("sub")
    whole = lax.axis_size("own") * subs
    other = own_bit * subs + sub_bit
    return lax.ppermute(x, ("own", "sub"), [(i, i ^ other) for i in range(whole)])


def width_of(features):
    return next(width for width in (512, 256, 128) if features % width == 0)


def stay(x):
    return pltpu.with_memory_space_constraint(x, pltpu.HBM)


def shape_of(dims, kind):
    return jax.ShapeDtypeStruct(dims, kind)


def call(body, operands, specs, outs, out_specs=None, after=(), flops=0, **more):
    count, idle = len(operands), len(after)

    def kernel(*refs):
        body(*refs[:count], *refs[count + idle :])

    moved = sum(x.size * x.dtype.itemsize for x in list(operands) + list(outs))
    return pl.pallas_call(
        kernel,
        out_shape=outs,
        in_specs=list(specs) + [anywhere] * len(after),
        out_specs=[in_vmem] * len(outs) if out_specs is None else out_specs,
        compiler_params=pltpu.CompilerParams(vmem_limit_bytes=24 * 1024 * 1024),
        cost_estimate=pl.CostEstimate(flops=flops, bytes_accessed=moved, transcendentals=0),
        **more,
    )(*operands, *after)


def pick_heads(adapter_ids, head_up, grad):
    per_owner, rank, width = head_up.shape
    own_count, sub_count = lax.axis_size("own"), lax.axis_size("sub")
    first = grad.shape[0] // early_part

    def body(ids_far, head_up, grad, *refs):
        outs, early, away, ids, maps, sems = refs[:own_count], *refs[own_count:]
        own, sub = lax.axis_index("own"), lax.axis_index("sub")
        copies = [
            pltpu.make_async_copy(ids_far, ids, sems.at[0]),
            pltpu.make_async_copy(head_up, maps, sems.at[1]),
            pltpu.make_async_copy(grad.at[pl.ds(0, first)], early, sems.at[2]),
        ]
        for copy in copies:
            copy.start()
        copies[0].wait()
        copies[1].wait()
        for step in range(own_count):
            local = ids[(own ^ step) * sub_count + sub] - own * per_owner
            outs[step][...] = maps[jnp.clip(local, 0, per_owner - 1)]
        step = lax.div(ids[own * sub_count + sub], per_owner) ^ own
        away[...] = jnp.full(away.shape, step, jnp.int32)
        copies[2].wait()

    *picked, early, away = call(
        body,
        [stay(adapter_ids), stay(head_up), stay(grad)],
        [in_hbm] * 3,
        [shape_of((rank, width), bf16)] * own_count
        + [shape_of((first, grad.shape[1]), bf16), shape_of((8, 128), jnp.int32)],
        scratch_shapes=[
            pltpu.SMEM(adapter_ids.shape, jnp.int32),
            pltpu.VMEM(head_up.shape, bf16),
            pltpu.SemaphoreType.DMA((3,)),
        ],
        flops=first_cost,
    )
    return picked, early, away


def project_low(tokens, down, after):
    rows, features = tokens.shape
    rank = down.shape[0]

    def body(tokens, down, low):
        low[...] = lax.dot_general(
            down[...], tokens[...], (((1,), (1,)), ((), ())), preferred_element_type=f32
        )

    return call(
        body,
        [tokens, down],
        [in_vmem] * 2,
        [shape_of((rank, rows), f32)],
        after=after,
        flops=2 * rows * rank * features,
    )[0]


def rounded(x, after):
    def body(x, out):
        out[...] = x[...].astype(bf16)

    return call(body, [x], [in_vmem], [shape_of(x.shape, bf16)], after=after)[0]


def project_back(away, offered, steps, grad, after):
    rank, columns = offered[0].shape
    rows = grad.shape[0]

    def body(away, *refs):
        *offered, grad, part = refs
        step = jnp.broadcast_to(away[:1, :1], (rank, columns))
        head = offered[0][...].astype(f32)
        for at, block in zip(steps, offered[1:]):
            head = jnp.where(step == at, block[...].astype(f32), head)
        part[...] = lax.dot_general(
            head.astype(bf16), grad[...], (((1,), (1,)), ((), ())), preferred_element_type=f32
        )

    return call(
        body,
        [away, *offered, grad],
        [in_vmem] * (len(offered) + 2),
        [shape_of((rank, rows), f32)],
        after=after,
        flops=slight,
    )[0]


def head_term(lengths, lows, grad, scale, after):
    rank, rows = lows[0].shape
    columns = grad.shape[1]
    first = rows // early_part

    def body(lengths, *refs):
        *lows, grad, term, late = refs
        total = lows[0][...]
        for low in lows[1:]:
            total = total + low[...].astype(f32)
        live = lax.broadcasted_iota(jnp.int32, total.shape, 1) < lengths[0]
        total = jnp.where(live, total, 0.0)
        kept = total.astype(bf16)
        rest = (total - kept.astype(f32)).astype(bf16)
        product = jnp.dot(kept, grad[...], preferred_element_type=f32)
        product += jnp.dot(rest, grad[...], preferred_element_type=f32)
        term[0] = (scale * product).astype(bf16)
        late[...] = grad[first:, :]

    return call(
        body,
        [lengths, *lows, grad],
        [in_smem] + [in_vmem] * (len(lows) + 1),
        [shape_of((1, rank, columns), bf16), shape_of((rows - first, columns), bf16)],
        after=after,
        flops=brief,
    )


def shared_terms(lengths, parts, tokens, scale, after):
    rows, features = tokens.shape
    rank = parts[0].shape[0]
    share = rank // 2

    def body(lengths, *refs):
        parts, (tokens, back, keep, send, send_too, total) = refs[:count], refs[count:]
        sub = lax.axis_index("sub")
        both = parts[0][...]
        for part in parts[1:]:
            both = both + part[...]
        live = lax.broadcasted_iota(jnp.int32, both.shape, 1) < lengths[0]
        back[...] = jnp.where(live, both, 0.0).astype(bf16)
        total[...] = scale * jnp.dot(back[...], tokens[...], preferred_element_type=f32)
        half = share // 2
        there = pl.multiple_of((1 - sub) * share, share)
        keep[...] = total[pl.ds(pl.multiple_of(sub * share, share), share), :]
        send[...] = total[pl.ds(there, half), :]
        send_too[...] = total[pl.ds(there + half, half), :]

    count = len(parts)
    return call(
        body,
        [lengths, *parts, tokens],
        [in_smem] + [in_vmem] * (count + 1),
        [shape_of((rank, rows), bf16), shape_of((share, features), f32)]
        + [shape_of((share // 2, features), f32)] * 2,
        after=after,
        scratch_shapes=[pltpu.VMEM((rank, features), f32)],
        flops=2 * rows * rank * features,
    )


def marked(after, flops):
    def body(out):
        out[...] = jnp.zeros(out.shape, f32)

    return call(body, [], [], [shape_of((8, 128), f32)], after=after, flops=flops)[0]


def sum_of(refs):
    total = refs[0][...].astype(f32)
    rows = total.shape[0]
    waiting = []
    for ref in refs[1:]:
        waiting.append(ref[...].astype(f32))
        if sum(piece.shape[0] for piece in waiting) == rows:
            total = total + (waiting[0] if len(waiting) == 1 else jnp.concatenate(waiting, axis=0))
            waiting = []
    return total


def add_up(pieces, after=(), flops=0):
    def body(*refs):
        refs[-1][...] = sum_of(refs[:-1]).astype(bf16)

    return call(
        body,
        list(pieces),
        [in_vmem] * len(pieces),
        [shape_of(pieces[0].shape, bf16)],
        after=after,
        flops=flops,
    )[0]


def halve(pieces, bit, after=()):
    rows, features = pieces[0].shape
    half = rows // 2

    def body(*refs):
        total = sum_of(refs[:-2])
        upper = lax.rem(lax.div(lax.axis_index("own"), bit), 2) == 1
        low, high = total[:half], total[half:]
        refs[-2][...] = jnp.where(upper, high, low)
        refs[-1][...] = jnp.where(upper, low, high).astype(bf16)

    return call(
        body,
        list(pieces),
        [in_vmem] * len(pieces),
        [shape_of((half, features), f32), shape_of((half, features), bf16)],
        after=after,
    )


def rejoin(mine, arrived, bit, after):
    rows, features = mine.shape

    def body(mine, arrived, out):
        upper = lax.rem(lax.div(lax.axis_index("own"), bit), 2) == 1
        one, two = mine[...].astype(f32), arrived[...].astype(f32)
        out[:rows] = jnp.where(upper, two, one).astype(bf16)
        out[rows:] = jnp.where(upper, one, two).astype(bf16)

    return call(
        body,
        [mine, arrived],
        [in_vmem] * 2,
        [shape_of((2 * rows, features), bf16)],
        after=after,
        flops=busy,
    )[0]


def lay_share(share, other, before, after):
    rows, features = share.shape
    held_in = [] if before is None else [before]

    def body(share, *refs):
        out, wide, sem = refs[len(held_in) :]
        sub = lax.axis_index("sub")
        side = 1 - sub if other else sub
        wide[...] = share[...].astype(f32)
        copy = pltpu.make_async_copy(
            wide, out.at[pl.ds(pl.multiple_of(side * rows, rows), rows)], sem
        )
        copy.start()
        copy.wait()

    return call(
        body,
        [share, *held_in],
        [in_vmem] + [in_hbm] * len(held_in),
        [shape_of((2 * rows, features), f32)],
        out_specs=[in_hbm],
        after=after,
        input_output_aliases={1: 0} if held_in else {},
        scratch_shapes=[pltpu.VMEM((rows, features), f32), pltpu.SemaphoreType.DMA],
    )[0]


def stack(pieces, after=(), flops=0):
    depths = [piece.shape[0] for piece in pieces]

    def body(*refs):
        at = 0
        for depth, piece in zip(depths, refs[:-1]):
            refs[-1][at : at + depth] = piece[...]
            at += depth

    return call(
        body,
        list(pieces),
        [in_vmem] * len(pieces),
        [shape_of((sum(depths),) + pieces[0].shape[1:], bf16)],
        after=after,
        flops=flops,
    )[0]


def clean(dims, after):
    def body(out, mark, held, sem):
        held[...] = jnp.zeros(held.shape, f32)
        mark[...] = jnp.zeros(mark.shape, f32)
        copies = [pltpu.make_async_copy(held, out.at[at], sem.at[at]) for at in range(dims[0])]
        for copy in copies:
            copy.start()
        for copy in copies:
            copy.wait()

    return call(
        body,
        [],
        [],
        [shape_of(dims, f32), shape_of((8, 128), f32)],
        out_specs=[in_hbm, in_vmem],
        after=after,
        scratch_shapes=[pltpu.VMEM(dims[1:], f32), pltpu.SemaphoreType.DMA((dims[0],))],
        flops=filling,
    )


def place_terms(adapter_ids, near, far, pattern, cleaned, after):
    per_owner, rank, columns = cleaned.shape
    sub_count = lax.axis_size("sub")

    def body(ids_far, near, far, cleaned, out, mark, held, ids, counts, sems):
        own, sub = lax.axis_index("own"), lax.axis_index("sub")
        fetch = pltpu.make_async_copy(ids_far, ids, sems.at[per_owner])
        fetch.start()
        mark[...] = jnp.zeros(mark.shape, f32)
        for local in range(per_owner):
            counts[local] = 0
        fetch.wait()
        for at, step in enumerate(pattern):
            for side in range(sub_count):
                local = ids[(own ^ step) * sub_count + side] - own * per_owner

                @pl.when(jnp.logical_and(local >= 0, local < per_owner))
                def _():
                    term = jnp.where(sub == side, near[at], far[at]).astype(f32)

                    @pl.when(counts[local] == 0)
                    def _():
                        held[local] = term

                    @pl.when(counts[local] > 0)
                    def _():
                        held[local] += term

                    counts[local] += 1

        copies = [
            pltpu.make_async_copy(held.at[local], out.at[local], sems.at[local])
            for local in range(per_owner)
        ]
        for local, copy in enumerate(copies):
            pl.when(counts[local] > 0)(copy.start)
        for local, copy in enumerate(copies):
            pl.when(counts[local] > 0)(copy.wait)

    return call(
        body,
        [stay(adapter_ids), near, far, cleaned],
        [in_hbm, in_vmem, in_vmem, in_hbm],
        [shape_of(cleaned.shape, f32), shape_of((8, 128), f32)],
        out_specs=[in_hbm, in_vmem],
        after=after,
        input_output_aliases={3: 0},
        scratch_shapes=[
            pltpu.VMEM(cleaned.shape, f32),
            pltpu.SMEM(adapter_ids.shape, jnp.int32),
            pltpu.SMEM((per_owner,), jnp.int32),
            pltpu.SemaphoreType.DMA((per_owner + 1,)),
        ],
    )


def arrange(lengths, grad, pieces, after):
    rows, columns = grad.shape
    count = 1 + len(pieces)
    first = rows // early_part

    def body(lengths, grad, *refs):
        pieces, kept = refs[:-1], refs[-1]
        at = lax.axis_index("tp")
        live = lax.broadcasted_iota(jnp.int32, (rows, columns), 0) < lengths[0]
        zero = jnp.zeros((rows, columns), bf16)
        place = pl.multiple_of(at * columns, 128)
        kept[:, pl.ds(place, columns)] = jnp.where(live, grad[...], zero)
        for step in range(1, count):
            place = pl.multiple_of(lax.rem(at + count - step, count) * columns, 128)
            early, late = pieces[2 * step - 2 : 2 * step]
            kept[:first, pl.ds(place, columns)] = jnp.where(live[:first], early[...], zero[:first])
            kept[first:, pl.ds(place, columns)] = jnp.where(live[first:], late[...], zero[first:])

    flat = [x for pair in pieces for x in pair]
    return call(
        body,
        [lengths, grad, *flat],
        [in_smem] + [in_vmem] * (1 + len(flat)),
        [shape_of((rows, count * columns), bf16)],
        after=after,
    )[0]


def input_side(kept, frozen, frozen_other, back, down, begin, count, before, after):
    rows = kept.shape[0]
    features, half = frozen.shape
    width = width_of(features)
    held_in = [] if before is None else [before]

    def body(kept, frozen, frozen_other, back, down, *refs):
        out, mark, held, sems = refs[len(held_in) :]
        mark[...] = jnp.zeros(mark.shape, f32)
        sub = lax.axis_index("sub")
        both = (((1,), (1,)), ((), ()))
        mine = kept[:, pl.ds(pl.multiple_of(sub * half, 128), half)]
        other = kept[:, pl.ds(pl.multiple_of((1 - sub) * half, 128), half)]
        twice = adapter_scale * back[...]
        copies = []
        for at in range(count):
            here = slice((begin + at) * width, (begin + at + 1) * width)
            total = lax.dot_general(mine, frozen[here, :], both, preferred_element_type=f32)
            total += lax.dot_general(other, frozen_other[here, :], both, preferred_element_type=f32)
            total += lax.dot_general(
                twice, down[:, here], (((0,), (0,)), ((), ())), preferred_element_type=f32
            )
            there = slice(at * width, (at + 1) * width)
            held[:, there] = total.astype(bf16)
            copies.append(
                pltpu.make_async_copy(held.at[:, there], out.at[:, here], sems.at[at])
            )
            copies[-1].start()
        for copy in copies:
            copy.wait()

    return call(
        body,
        [kept, frozen, frozen_other, back, down, *held_in],
        [in_vmem] * 5 + [in_hbm] * len(held_in),
        [shape_of((rows, features), bf16), shape_of((8, 128), f32)],
        out_specs=[in_hbm, in_vmem],
        after=after,
        input_output_aliases={5: 0} if held_in else {},
        scratch_shapes=[
            pltpu.VMEM((rows, count * width), bf16),
            pltpu.SemaphoreType.DMA((count,)),
        ],
        flops=2 * rows * width * count * (2 * half + back.shape[0]),
    )


def on_device(tokens, grad_output, frozen_value, shared_down, head_up, adapter_ids, lengths):
    rows, features = tokens.shape
    own_count = lax.axis_size("own")
    tp_count = lax.axis_size("tp")
    per_owner = head_up.shape[0]
    scale = adapter_scale / rows
    tp_steps, own_steps = range(1, tp_count), range(1, own_count)

    frozen_other = shift(frozen_value, "sub", 1)
    picked, early, away = pick_heads(adapter_ids, head_up, grad_output)
    steps = sorted(own_steps, key=lambda step: (-step.bit_length(), step))
    offered = [picked[0]] + [swap(picked[step], step, 0) for step in steps]
    early_grads = [shift(early, "tp", step) for step in tp_steps]

    down = shared_down.T
    low = project_low(tokens, down, picked[:1])
    sent = rounded(low, [frozen_other])
    lows = [low] + [shift(sent, "tp", step) for step in tp_steps]

    part = project_back(away, offered, steps, grad_output, [low])
    parts = [part] + [shift(part, "tp", step) for step in tp_steps]

    near, late = head_term(lengths, lows, grad_output, scale, [part, *early_grads])
    late_grads = [shift(late, "tp", step) for step in tp_steps]
    terms = [near] + [swap(near, step, 0) for step in own_steps]
    back, keep, *sends = shared_terms(lengths, parts, tokens, scale, [near])
    pieces = [keep, *[shift(send, "sub", 1) for send in sends]]
    pause = marked([back], flops=middling)
    met = pause
    if own_count > 1:
        met = stack(terms[1:2], [pause], flops=little)

    bits = [1 << i for i in range(own_count.bit_length() - 1)]
    mark = met
    for bit in bits[:-1]:
        stays, leaves = halve(pieces, bit, [mark])
        pieces = [stays, swap(leaves, bit, 0)]
        mark = leaves
    cleaned, mark = clean((per_owner,) + near.shape[1:], [mark])
    near = stack(terms, [mark])
    far = shift(near, "sub", 1)
    total = add_up(pieces, [near], flops=busy)
    grad_heads, mark = place_terms(
        adapter_ids, near, far, range(own_count), cleaned, [total]
    )
    kept = arrange(lengths, grad_output, list(zip(early_grads, late_grads)), [mark])
    sides = (frozen_value, frozen_other, back, down)
    blocks = features // width_of(features)
    cut = max(1, blocks // 5)
    input_gradient, mark = input_side(kept, *sides, 0, cut, None, [mark])
    if bits:
        total = add_up([total, swap(total, bits[-1], 0)], [mark])
    if blocks > cut:
        input_gradient, mark = input_side(
            kept, *sides, cut, blocks - cut, input_gradient, [total]
        )
    for bit in reversed(bits[:-1]):
        total = rejoin(total, swap(total, bit, 0), bit, [mark])
        mark = total
    laid = lay_share(total, False, None, [mark])
    shared_down_gradient = lay_share(shift(total, "sub", 1), True, laid, []).T
    return (input_gradient, shared_down_gradient, grad_heads)


def solution(mesh):
    placed = (
        P(("rep", "own", "sub"), "tp"),
        P(("rep", "own", "sub"), "tp"),
        P("tp", "sub"),
        P("tp", None),
        P("own", None, "tp"),
        P("rep"),
        P(("rep", "own", "sub")),
    )
    return jax.shard_map(
        on_device,
        mesh=mesh,
        in_specs=placed,
        out_specs=(
            P(("rep", "own", "sub"), "tp"),
            P(("rep", "tp"), None),
            P(("rep", "own"), None, "tp"),
        ),
        check_vma=False,
    )
```

```python
import jax
import jax.numpy as jnp
from jax import lax
from jax.experimental import pallas as pl
from jax.experimental.pallas import tpu as pltpu
from jax.sharding import PartitionSpec as P

adapter_scale = 2.0
f32 = jnp.float32
bf16 = jnp.bfloat16

early_part = 4

(busy, first_cost, middling, filling, brief, slight) = (
    10**10, 5 * 10**9, 5 * 10**9, 10**10, 3 * 10**9, 15 * 10**8
)

anywhere = pl.BlockSpec(memory_space=pl.ANY)
in_hbm = pl.BlockSpec(memory_space=pltpu.HBM)
in_vmem = pl.BlockSpec(memory_space=pltpu.VMEM)
in_smem = pl.BlockSpec(memory_space=pltpu.SMEM)


def shift(x, axis, step):
    count = lax.axis_size(axis)
    return lax.ppermute(x, axis, [(i, (i + step) % count) for i in range(count)])


def swap(x, own_bit, sub_bit):
    subs = lax.axis_size("sub")
    whole = lax.axis_size("own") * subs
    other = own_bit * subs + sub_bit
    return lax.ppermute(x, ("own", "sub"), [(i, i ^ other) for i in range(whole)])


def width_of(features):
    return next(width for width in (512, 256, 128) if features % width == 0)


def stay(x):
    return pltpu.with_memory_space_constraint(x, pltpu.HBM)


def shape_of(dims, kind):
    return jax.ShapeDtypeStruct(dims, kind)


def call(body, operands, specs, outs, out_specs=None, after=(), flops=0, **more):
    count, idle = len(operands), len(after)

    def kernel(*refs):
        body(*refs[:count], *refs[count + idle :])

    moved = sum(x.size * x.dtype.itemsize for x in list(operands) + list(outs))
    return pl.pallas_call(
        kernel,
        out_shape=outs,
        in_specs=list(specs) + [anywhere] * len(after),
        out_specs=[in_vmem] * len(outs) if out_specs is None else out_specs,
        compiler_params=pltpu.CompilerParams(vmem_limit_bytes=24 * 1024 * 1024),
        cost_estimate=pl.CostEstimate(flops=flops, bytes_accessed=moved, transcendentals=0),
        **more,
    )(*operands, *after)


def pick_heads(adapter_ids, head_up, grad):
    per_owner, rank, width = head_up.shape
    own_count, sub_count = lax.axis_size("own"), lax.axis_size("sub")
    first = grad.shape[0] // early_part

    def body(ids_far, head_up, grad, *refs):
        outs, early, away, ids, maps, sems = refs[:own_count], *refs[own_count:]
        own, sub = lax.axis_index("own"), lax.axis_index("sub")
        copies = [
            pltpu.make_async_copy(ids_far, ids, sems.at[0]),
            pltpu.make_async_copy(head_up, maps, sems.at[1]),
            pltpu.make_async_copy(grad.at[pl.ds(0, first)], early, sems.at[2]),
        ]
        for copy in copies:
            copy.start()
        copies[0].wait()
        copies[1].wait()
        for step in range(own_count):
            local = ids[(own ^ step) * sub_count + sub] - own * per_owner
            outs[step][...] = maps[jnp.clip(local, 0, per_owner - 1)]
        step = lax.div(ids[own * sub_count + sub], per_owner) ^ own
        away[...] = jnp.full(away.shape, step, jnp.int32)
        copies[2].wait()

    *picked, early, away = call(
        body,
        [stay(adapter_ids), stay(head_up), stay(grad)],
        [in_hbm] * 3,
        [shape_of((rank, width), bf16)] * own_count
        + [shape_of((first, grad.shape[1]), bf16), shape_of((8, 128), jnp.int32)],
        scratch_shapes=[
            pltpu.SMEM(adapter_ids.shape, jnp.int32),
            pltpu.VMEM(head_up.shape, bf16),
            pltpu.SemaphoreType.DMA((3,)),
        ],
        flops=first_cost,
    )
    return picked, early, away


def project_low(tokens, down, after):
    rows, features = tokens.shape
    rank = down.shape[0]

    def body(tokens, down, low):
        low[...] = lax.dot_general(
            down[...], tokens[...], (((1,), (1,)), ((), ())), preferred_element_type=f32
        )

    return call(
        body,
        [tokens, down],
        [in_vmem] * 2,
        [shape_of((rank, rows), f32)],
        after=after,
        flops=2 * rows * rank * features,
    )[0]


def rounded(x, after):
    def body(x, out):
        out[...] = x[...].astype(bf16)

    return call(body, [x], [in_vmem], [shape_of(x.shape, bf16)], after=after)[0]


def project_back(away, offered, steps, grad, after):
    rank, columns = offered[0].shape
    rows = grad.shape[0]

    def body(away, *refs):
        *offered, grad, part = refs
        step = jnp.broadcast_to(away[:1, :1], (rank, columns))
        head = offered[0][...].astype(f32)
        for at, block in zip(steps, offered[1:]):
            head = jnp.where(step == at, block[...].astype(f32), head)
        part[...] = lax.dot_general(
            head.astype(bf16), grad[...], (((1,), (1,)), ((), ())), preferred_element_type=f32
        )

    return call(
        body,
        [away, *offered, grad],
        [in_vmem] * (len(offered) + 2),
        [shape_of((rank, rows), f32)],
        after=after,
        flops=slight,
    )[0]


def head_term(lengths, lows, grad, scale, after):
    rank, rows = lows[0].shape
    columns = grad.shape[1]
    first = rows // early_part

    def body(lengths, *refs):
        *lows, grad, term, late = refs
        total = lows[0][...]
        for low in lows[1:]:
            total = total + low[...].astype(f32)
        live = lax.broadcasted_iota(jnp.int32, total.shape, 1) < lengths[0]
        total = jnp.where(live, total, 0.0)
        kept = total.astype(bf16)
        rest = (total - kept.astype(f32)).astype(bf16)
        product = jnp.dot(kept, grad[...], preferred_element_type=f32)
        product += jnp.dot(rest, grad[...], preferred_element_type=f32)
        term[0] = (scale * product).astype(bf16)
        late[...] = grad[first:, :]

    return call(
        body,
        [lengths, *lows, grad],
        [in_smem] + [in_vmem] * (len(lows) + 1),
        [shape_of((1, rank, columns), bf16), shape_of((rows - first, columns), bf16)],
        after=after,
        flops=brief,
    )


def shared_terms(lengths, parts, tokens, scale, after):
    rows, features = tokens.shape
    rank = parts[0].shape[0]
    share = rank // 2

    def body(lengths, *refs):
        parts, (tokens, back, keep, send, total) = refs[:count], refs[count:]
        sub = lax.axis_index("sub")
        both = parts[0][...]
        for part in parts[1:]:
            both = both + part[...]
        live = lax.broadcasted_iota(jnp.int32, both.shape, 1) < lengths[0]
        back[...] = jnp.where(live, both, 0.0).astype(bf16)
        total[...] = scale * jnp.dot(back[...], tokens[...], preferred_element_type=f32)
        keep[...] = total[pl.ds(pl.multiple_of(sub * share, share), share), :]
        send[...] = total[pl.ds(pl.multiple_of((1 - sub) * share, share), share), :]

    count = len(parts)
    return call(
        body,
        [lengths, *parts, tokens],
        [in_smem] + [in_vmem] * (count + 1),
        [shape_of((rank, rows), bf16)] + [shape_of((share, features), f32)] * 2,
        after=after,
        scratch_shapes=[pltpu.VMEM((rank, features), f32)],
        flops=2 * rows * rank * features,
    )


def add_up(pieces, after=(), flops=0):
    def body(*refs):
        total = refs[0][...].astype(f32)
        for piece in refs[1:-1]:
            total = total + piece[...].astype(f32)
        refs[-1][...] = total.astype(bf16)

    return call(
        body,
        list(pieces),
        [in_vmem] * len(pieces),
        [shape_of(pieces[0].shape, bf16)],
        after=after,
        flops=flops,
    )[0]


def halve(pieces, bit, after=()):
    rows, features = pieces[0].shape
    half = rows // 2

    def body(*refs):
        total = refs[0][...].astype(f32)
        for piece in refs[1:-2]:
            total = total + piece[...].astype(f32)
        upper = lax.rem(lax.div(lax.axis_index("own"), bit), 2) == 1
        low, high = total[:half], total[half:]
        refs[-2][...] = jnp.where(upper, high, low)
        refs[-1][...] = jnp.where(upper, low, high).astype(bf16)

    return call(
        body,
        list(pieces),
        [in_vmem] * len(pieces),
        [shape_of((half, features), f32), shape_of((half, features), bf16)],
        after=after,
    )


def rejoin(mine, arrived, bit, after):
    rows, features = mine.shape

    def body(mine, arrived, out):
        upper = lax.rem(lax.div(lax.axis_index("own"), bit), 2) == 1
        one, two = mine[...].astype(f32), arrived[...].astype(f32)
        out[:rows] = jnp.where(upper, two, one).astype(bf16)
        out[rows:] = jnp.where(upper, one, two).astype(bf16)

    return call(
        body,
        [mine, arrived],
        [in_vmem] * 2,
        [shape_of((2 * rows, features), bf16)],
        after=after,
        flops=busy,
    )[0]


def join_shares(mine, other, after):
    share, features = mine.shape

    def body(mine, other, out):
        sub = lax.axis_index("sub")
        for side, piece in ((sub, mine), (1 - sub, other)):
            out[pl.ds(pl.multiple_of(side * share, share), share), :] = piece[...].astype(f32)

    return call(
        body,
        [mine, other],
        [in_vmem] * 2,
        [shape_of((2 * share, features), f32)],
        after=after,
    )[0]


def stack(pieces, after=(), flops=0):
    depths = [piece.shape[0] for piece in pieces]

    def body(*refs):
        at = 0
        for depth, piece in zip(depths, refs[:-1]):
            refs[-1][at : at + depth] = piece[...]
            at += depth

    return call(
        body,
        list(pieces),
        [in_vmem] * len(pieces),
        [shape_of((sum(depths),) + pieces[0].shape[1:], bf16)],
        after=after,
        flops=flops,
    )[0]


def clean(dims, after):
    def body(out, mark, held, sem):
        held[...] = jnp.zeros(held.shape, f32)
        mark[...] = jnp.zeros(mark.shape, f32)
        copies = [pltpu.make_async_copy(held, out.at[at], sem.at[at]) for at in range(dims[0])]
        for copy in copies:
            copy.start()
        for copy in copies:
            copy.wait()

    return call(
        body,
        [],
        [],
        [shape_of(dims, f32), shape_of((8, 128), f32)],
        out_specs=[in_hbm, in_vmem],
        after=after,
        scratch_shapes=[pltpu.VMEM(dims[1:], f32), pltpu.SemaphoreType.DMA((dims[0],))],
        flops=filling,
    )


def place_terms(adapter_ids, near, far, pattern, cleaned, after):
    per_owner, rank, columns = cleaned.shape
    sub_count = lax.axis_size("sub")

    def body(ids_far, near, far, cleaned, out, mark, held, ids, counts, sems):
        own, sub = lax.axis_index("own"), lax.axis_index("sub")
        fetch = pltpu.make_async_copy(ids_far, ids, sems.at[per_owner])
        fetch.start()
        mark[...] = jnp.zeros(mark.shape, f32)
        for local in range(per_owner):
            counts[local] = 0
        fetch.wait()
        for at, step in enumerate(pattern):
            for side in range(sub_count):
                local = ids[(own ^ step) * sub_count + side] - own * per_owner

                @pl.when(jnp.logical_and(local >= 0, local < per_owner))
                def _():
                    term = jnp.where(sub == side, near[at], far[at]).astype(f32)

                    @pl.when(counts[local] == 0)
                    def _():
                        held[local] = term

                    @pl.when(counts[local] > 0)
                    def _():
                        held[local] += term

                    counts[local] += 1

        copies = [
            pltpu.make_async_copy(held.at[local], out.at[local], sems.at[local])
            for local in range(per_owner)
        ]
        for local, copy in enumerate(copies):
            pl.when(counts[local] > 0)(copy.start)
        for local, copy in enumerate(copies):
            pl.when(counts[local] > 0)(copy.wait)

    return call(
        body,
        [stay(adapter_ids), near, far, cleaned],
        [in_hbm, in_vmem, in_vmem, in_hbm],
        [shape_of(cleaned.shape, f32), shape_of((8, 128), f32)],
        out_specs=[in_hbm, in_vmem],
        after=after,
        input_output_aliases={3: 0},
        scratch_shapes=[
            pltpu.VMEM(cleaned.shape, f32),
            pltpu.SMEM(adapter_ids.shape, jnp.int32),
            pltpu.SMEM((per_owner,), jnp.int32),
            pltpu.SemaphoreType.DMA((per_owner + 1,)),
        ],
    )


def arrange(lengths, grad, pieces, after):
    rows, columns = grad.shape
    count = 1 + len(pieces)
    first = rows // early_part

    def body(lengths, grad, *refs):
        pieces, kept = refs[:-1], refs[-1]
        at = lax.axis_index("tp")
        live = lax.broadcasted_iota(jnp.int32, (rows, columns), 0) < lengths[0]
        zero = jnp.zeros((rows, columns), bf16)
        place = pl.multiple_of(at * columns, 128)
        kept[:, pl.ds(place, columns)] = jnp.where(live, grad[...], zero)
        for step in range(1, count):
            place = pl.multiple_of(lax.rem(at + count - step, count) * columns, 128)
            early, late = pieces[2 * step - 2 : 2 * step]
            kept[:first, pl.ds(place, columns)] = jnp.where(live[:first], early[...], zero[:first])
            kept[first:, pl.ds(place, columns)] = jnp.where(live[first:], late[...], zero[first:])

    flat = [x for pair in pieces for x in pair]
    return call(
        body,
        [lengths, grad, *flat],
        [in_smem] + [in_vmem] * (1 + len(flat)),
        [shape_of((rows, count * columns), bf16)],
        after=after,
    )[0]


def input_side(kept, frozen, frozen_other, back, down, begin, count, before, after):
    rows = kept.shape[0]
    features, half = frozen.shape
    width = width_of(features)
    held_in = [] if before is None else [before]

    def body(kept, frozen, frozen_other, back, down, *refs):
        out, mark, held, sems = refs[len(held_in) :]
        mark[...] = jnp.zeros(mark.shape, f32)
        sub = lax.axis_index("sub")
        both = (((1,), (1,)), ((), ()))
        mine = kept[:, pl.ds(pl.multiple_of(sub * half, 128), half)]
        other = kept[:, pl.ds(pl.multiple_of((1 - sub) * half, 128), half)]
        twice = adapter_scale * back[...]
        copies = []
        for at in range(count):
            here = slice((begin + at) * width, (begin + at + 1) * width)
            total = lax.dot_general(mine, frozen[here, :], both, preferred_element_type=f32)
            total += lax.dot_general(other, frozen_other[here, :], both, preferred_element_type=f32)
            total += lax.dot_general(
                twice, down[:, here], (((0,), (0,)), ((), ())), preferred_element_type=f32
            )
            there = slice(at * width, (at + 1) * width)
            held[:, there] = total.astype(bf16)
            copies.append(
                pltpu.make_async_copy(held.at[:, there], out.at[:, here], sems.at[at])
            )
            copies[-1].start()
        for copy in copies:
            copy.wait()

    return call(
        body,
        [kept, frozen, frozen_other, back, down, *held_in],
        [in_vmem] * 5 + [in_hbm] * len(held_in),
        [shape_of((rows, features), bf16), shape_of((8, 128), f32)],
        out_specs=[in_hbm, in_vmem],
        after=after,
        input_output_aliases={5: 0} if held_in else {},
        scratch_shapes=[
            pltpu.VMEM((rows, count * width), bf16),
            pltpu.SemaphoreType.DMA((count,)),
        ],
        flops=2 * rows * width * count * (2 * half + back.shape[0]),
    )


def on_device(tokens, grad_output, frozen_value, shared_down, head_up, adapter_ids, lengths):
    rows, features = tokens.shape
    own_count = lax.axis_size("own")
    tp_count = lax.axis_size("tp")
    per_owner = head_up.shape[0]
    scale = adapter_scale / rows
    tp_steps, own_steps = range(1, tp_count), range(1, own_count)

    frozen_other = shift(frozen_value, "sub", 1)
    picked, early, away = pick_heads(adapter_ids, head_up, grad_output)
    steps = sorted(own_steps, key=lambda step: (-step.bit_length(), step))
    offered = [picked[0]] + [swap(picked[step], step, 0) for step in steps]
    early_grads = [shift(early, "tp", step) for step in tp_steps]

    down = shared_down.T
    low = project_low(tokens, down, picked[:1])
    sent = rounded(low, [frozen_other])
    lows = [low] + [shift(sent, "tp", step) for step in tp_steps]

    part = project_back(away, offered, steps, grad_output, [low])
    parts = [part] + [shift(part, "tp", step) for step in tp_steps]

    near, late = head_term(lengths, lows, grad_output, scale, [part, *early_grads])
    late_grads = [shift(late, "tp", step) for step in tp_steps]
    bits = [1 << i for i in range(own_count.bit_length() - 1)]
    terms, pattern = [near], [0]
    for bit in reversed(bits[1:]):
        terms = terms + [swap(term, bit, 0) for term in terms]
        pattern = pattern + [step ^ bit for step in pattern]
    nearby = [swap(near, 1, 0)] if bits else []

    back, keep, send = shared_terms(lengths, parts, tokens, scale, [near])
    pieces = [keep, shift(send, "sub", 1)]
    met = stack(terms[1:]) if terms[1:] else near
    met = stack(nearby, [met], flops=middling) if nearby else met

    mark = met
    for bit in bits[:-1]:
        stays, leaves = halve(pieces, bit, [mark])
        pieces = [stays, swap(leaves, bit, 0)]
        mark = leaves
    cleaned, mark = clean((per_owner,) + near.shape[1:], [mark])
    total = add_up(pieces, [mark], flops=busy)
    relays = [total]
    if bits:
        relays = [stack([term], [total]) for term in terms[1:]]
        terms = terms + nearby + [swap(relay, 1, 0) for relay in relays]
        pattern = pattern + [step ^ 1 for step in pattern]
    kept = arrange(lengths, grad_output, list(zip(early_grads, late_grads)), relays)
    sides = (frozen_value, frozen_other, back, down)
    blocks = features // width_of(features)
    cut = max(1, blocks * 2 // 5)
    input_gradient, mark = input_side(kept, *sides, 0, cut, None, relays)
    near = stack(terms, [mark])
    far = shift(near, "sub", 1)
    if bits:
        total = add_up([total, swap(total, bits[-1], 0)], [near], flops=busy)
    if blocks > cut:
        input_gradient, mark = input_side(
            kept, *sides, cut, blocks - cut, input_gradient, [total]
        )
    grad_heads, mark = place_terms(adapter_ids, near, far, pattern, cleaned, [mark])
    for bit in reversed(bits[:-1]):
        total = rejoin(total, swap(total, bit, 0), bit, [mark])
        mark = total
    shared_down_gradient = join_shares(total, shift(total, "sub", 1), [mark]).T
    return (input_gradient, shared_down_gradient, grad_heads)


def solution(mesh):
    placed = (
        P(("rep", "own", "sub"), "tp"),
        P(("rep", "own", "sub"), "tp"),
        P("tp", "sub"),
        P("tp", None),
        P("own", None, "tp"),
        P("rep"),
        P(("rep", "own", "sub")),
    )
    return jax.shard_map(
        on_device,
        mesh=mesh,
        in_specs=placed,
        out_specs=(
            P(("rep", "own", "sub"), "tp"),
            P(("rep", "tp"), None),
            P(("rep", "own"), None, "tp"),
        ),
        check_vma=False,
    )
```

```python
import jax
import jax.numpy as jnp
from jax import lax
from jax.experimental import pallas as pl
from jax.experimental.pallas import tpu as pltpu
from jax.sharding import PartitionSpec as P

adapter_scale = 2.0
f32 = jnp.float32
bf16 = jnp.bfloat16

early_part = 4

(busy, first_cost, middling, filling, brief, slight) = (
    10**10, 5 * 10**9, 5 * 10**9, 10**10, 3 * 10**9, 15 * 10**8
)

anywhere = pl.BlockSpec(memory_space=pl.ANY)
in_hbm = pl.BlockSpec(memory_space=pltpu.HBM)
in_vmem = pl.BlockSpec(memory_space=pltpu.VMEM)
in_smem = pl.BlockSpec(memory_space=pltpu.SMEM)


def shift(x, axis, step):
    count = lax.axis_size(axis)
    return lax.ppermute(x, axis, [(i, (i + step) % count) for i in range(count)])


def swap(x, own_bit, sub_bit):
    subs = lax.axis_size("sub")
    whole = lax.axis_size("own") * subs
    other = own_bit * subs + sub_bit
    return lax.ppermute(x, ("own", "sub"), [(i, i ^ other) for i in range(whole)])


def width_of(features):
    return next(width for width in (512, 256, 128) if features % width == 0)


def stay(x):
    return pltpu.with_memory_space_constraint(x, pltpu.HBM)


def shape_of(dims, kind):
    return jax.ShapeDtypeStruct(dims, kind)


def call(body, operands, specs, outs, out_specs=None, after=(), flops=0, **more):
    count, idle = len(operands), len(after)

    def kernel(*refs):
        body(*refs[:count], *refs[count + idle :])

    moved = sum(x.size * x.dtype.itemsize for x in list(operands) + list(outs))
    return pl.pallas_call(
        kernel,
        out_shape=outs,
        in_specs=list(specs) + [anywhere] * len(after),
        out_specs=[in_vmem] * len(outs) if out_specs is None else out_specs,
        compiler_params=pltpu.CompilerParams(vmem_limit_bytes=24 * 1024 * 1024),
        cost_estimate=pl.CostEstimate(flops=flops, bytes_accessed=moved, transcendentals=0),
        **more,
    )(*operands, *after)


def pick_heads(adapter_ids, head_up, grad):
    per_owner, rank, width = head_up.shape
    own_count, sub_count = lax.axis_size("own"), lax.axis_size("sub")
    first = grad.shape[0] // early_part

    def body(ids_far, head_up, grad, *refs):
        outs, early, away, ids, maps, sems = refs[:own_count], *refs[own_count:]
        own, sub = lax.axis_index("own"), lax.axis_index("sub")
        copies = [
            pltpu.make_async_copy(ids_far, ids, sems.at[0]),
            pltpu.make_async_copy(head_up, maps, sems.at[1]),
            pltpu.make_async_copy(grad.at[pl.ds(0, first)], early, sems.at[2]),
        ]
        for copy in copies:
            copy.start()
        copies[0].wait()
        copies[1].wait()
        for step in range(own_count):
            local = ids[(own ^ step) * sub_count + sub] - own * per_owner
            outs[step][...] = maps[jnp.clip(local, 0, per_owner - 1)]
        step = lax.div(ids[own * sub_count + sub], per_owner) ^ own
        away[...] = jnp.full(away.shape, step, jnp.int32)
        copies[2].wait()

    *picked, early, away = call(
        body,
        [stay(adapter_ids), stay(head_up), stay(grad)],
        [in_hbm] * 3,
        [shape_of((rank, width), bf16)] * own_count
        + [shape_of((first, grad.shape[1]), bf16), shape_of((8, 128), jnp.int32)],
        scratch_shapes=[
            pltpu.SMEM(adapter_ids.shape, jnp.int32),
            pltpu.VMEM(head_up.shape, bf16),
            pltpu.SemaphoreType.DMA((3,)),
        ],
        flops=first_cost,
    )
    return picked, early, away


def project_low(tokens, down, after):
    rows, features = tokens.shape
    rank = down.shape[0]

    def body(tokens, down, low):
        low[...] = lax.dot_general(
            down[...], tokens[...], (((1,), (1,)), ((), ())), preferred_element_type=f32
        )

    return call(
        body,
        [tokens, down],
        [in_vmem] * 2,
        [shape_of((rank, rows), f32)],
        after=after,
        flops=2 * rows * rank * features,
    )[0]


def rounded(x, after):
    def body(x, out):
        out[...] = x[...].astype(bf16)

    return call(body, [x], [in_vmem], [shape_of(x.shape, bf16)], after=after)[0]


def project_back(away, offered, steps, grad, after):
    rank, columns = offered[0].shape
    rows = grad.shape[0]

    def body(away, *refs):
        *offered, grad, part = refs
        step = jnp.broadcast_to(away[:1, :1], (rank, columns))
        head = offered[0][...].astype(f32)
        for at, block in zip(steps, offered[1:]):
            head = jnp.where(step == at, block[...].astype(f32), head)
        part[...] = lax.dot_general(
            head.astype(bf16), grad[...], (((1,), (1,)), ((), ())), preferred_element_type=f32
        )

    return call(
        body,
        [away, *offered, grad],
        [in_vmem] * (len(offered) + 2),
        [shape_of((rank, rows), f32)],
        after=after,
        flops=slight,
    )[0]


def head_term(lengths, lows, grad, scale, after):
    rank, rows = lows[0].shape
    columns = grad.shape[1]
    first = rows // early_part

    def body(lengths, *refs):
        *lows, grad, term, late = refs
        total = lows[0][...]
        for low in lows[1:]:
            total = total + low[...].astype(f32)
        live = lax.broadcasted_iota(jnp.int32, total.shape, 1) < lengths[0]
        total = jnp.where(live, total, 0.0)
        kept = total.astype(bf16)
        rest = (total - kept.astype(f32)).astype(bf16)
        product = jnp.dot(kept, grad[...], preferred_element_type=f32)
        product += jnp.dot(rest, grad[...], preferred_element_type=f32)
        term[0] = (scale * product).astype(bf16)
        late[...] = grad[first:, :]

    return call(
        body,
        [lengths, *lows, grad],
        [in_smem] + [in_vmem] * (len(lows) + 1),
        [shape_of((1, rank, columns), bf16), shape_of((rows - first, columns), bf16)],
        after=after,
        flops=brief,
    )


def shared_terms(lengths, parts, tokens, scale, after):
    rows, features = tokens.shape
    rank = parts[0].shape[0]
    share = rank // 2

    def body(lengths, *refs):
        parts, (tokens, back, keep, send, total) = refs[:count], refs[count:]
        sub = lax.axis_index("sub")
        both = parts[0][...]
        for part in parts[1:]:
            both = both + part[...]
        live = lax.broadcasted_iota(jnp.int32, both.shape, 1) < lengths[0]
        back[...] = jnp.where(live, both, 0.0).astype(bf16)
        total[...] = scale * jnp.dot(back[...], tokens[...], preferred_element_type=f32)
        keep[...] = total[pl.ds(pl.multiple_of(sub * share, share), share), :]
        send[...] = total[pl.ds(pl.multiple_of((1 - sub) * share, share), share), :]

    count = len(parts)
    return call(
        body,
        [lengths, *parts, tokens],
        [in_smem] + [in_vmem] * (count + 1),
        [shape_of((rank, rows), bf16)] + [shape_of((share, features), f32)] * 2,
        after=after,
        scratch_shapes=[pltpu.VMEM((rank, features), f32)],
        flops=2 * rows * rank * features,
    )


def add_up(pieces, after=(), flops=0):
    def body(*refs):
        total = refs[0][...].astype(f32)
        for piece in refs[1:-1]:
            total = total + piece[...].astype(f32)
        refs[-1][...] = total.astype(bf16)

    return call(
        body,
        list(pieces),
        [in_vmem] * len(pieces),
        [shape_of(pieces[0].shape, bf16)],
        after=after,
        flops=flops,
    )[0]


def halve(pieces, bit, after=()):
    rows, features = pieces[0].shape
    half = rows // 2

    def body(*refs):
        total = refs[0][...].astype(f32)
        for piece in refs[1:-2]:
            total = total + piece[...].astype(f32)
        upper = lax.rem(lax.div(lax.axis_index("own"), bit), 2) == 1
        low, high = total[:half], total[half:]
        refs[-2][...] = jnp.where(upper, high, low)
        refs[-1][...] = jnp.where(upper, low, high).astype(bf16)

    return call(
        body,
        list(pieces),
        [in_vmem] * len(pieces),
        [shape_of((half, features), f32), shape_of((half, features), bf16)],
        after=after,
    )


def rejoin(mine, arrived, bit, after):
    rows, features = mine.shape

    def body(mine, arrived, out):
        upper = lax.rem(lax.div(lax.axis_index("own"), bit), 2) == 1
        one, two = mine[...].astype(f32), arrived[...].astype(f32)
        out[:rows] = jnp.where(upper, two, one).astype(bf16)
        out[rows:] = jnp.where(upper, one, two).astype(bf16)

    return call(
        body,
        [mine, arrived],
        [in_vmem] * 2,
        [shape_of((2 * rows, features), bf16)],
        after=after,
        flops=busy,
    )[0]


def join_shares(mine, other, after):
    share, features = mine.shape

    def body(mine, other, out):
        sub = lax.axis_index("sub")
        for side, piece in ((sub, mine), (1 - sub, other)):
            out[pl.ds(pl.multiple_of(side * share, share), share), :] = piece[...].astype(f32)

    return call(
        body,
        [mine, other],
        [in_vmem] * 2,
        [shape_of((2 * share, features), f32)],
        after=after,
    )[0]


def stack(pieces, after=(), flops=0):
    depths = [piece.shape[0] for piece in pieces]

    def body(*refs):
        at = 0
        for depth, piece in zip(depths, refs[:-1]):
            refs[-1][at : at + depth] = piece[...]
            at += depth

    return call(
        body,
        list(pieces),
        [in_vmem] * len(pieces),
        [shape_of((sum(depths),) + pieces[0].shape[1:], bf16)],
        after=after,
        flops=flops,
    )[0]


def clean(dims, after):
    def body(out, mark, held, sem):
        held[...] = jnp.zeros(held.shape, f32)
        mark[...] = jnp.zeros(mark.shape, f32)
        copies = [pltpu.make_async_copy(held, out.at[at], sem.at[at]) for at in range(dims[0])]
        for copy in copies:
            copy.start()
        for copy in copies:
            copy.wait()

    return call(
        body,
        [],
        [],
        [shape_of(dims, f32), shape_of((8, 128), f32)],
        out_specs=[in_hbm, in_vmem],
        after=after,
        scratch_shapes=[pltpu.VMEM(dims[1:], f32), pltpu.SemaphoreType.DMA((dims[0],))],
        flops=filling,
    )


def place_terms(adapter_ids, near, far, pattern, cleaned, after):
    per_owner, rank, columns = cleaned.shape
    sub_count = lax.axis_size("sub")

    def body(ids_far, near, far, cleaned, out, mark, held, ids, counts, sems):
        own, sub = lax.axis_index("own"), lax.axis_index("sub")
        fetch = pltpu.make_async_copy(ids_far, ids, sems.at[per_owner])
        fetch.start()
        mark[...] = jnp.zeros(mark.shape, f32)
        for local in range(per_owner):
            counts[local] = 0
        fetch.wait()
        for at, step in enumerate(pattern):
            for side in range(sub_count):
                local = ids[(own ^ step) * sub_count + side] - own * per_owner

                @pl.when(jnp.logical_and(local >= 0, local < per_owner))
                def _():
                    term = jnp.where(sub == side, near[at], far[at]).astype(f32)

                    @pl.when(counts[local] == 0)
                    def _():
                        held[local] = term

                    @pl.when(counts[local] > 0)
                    def _():
                        held[local] += term

                    counts[local] += 1

        copies = [
            pltpu.make_async_copy(held.at[local], out.at[local], sems.at[local])
            for local in range(per_owner)
        ]
        for local, copy in enumerate(copies):
            pl.when(counts[local] > 0)(copy.start)
        for local, copy in enumerate(copies):
            pl.when(counts[local] > 0)(copy.wait)

    return call(
        body,
        [stay(adapter_ids), near, far, cleaned],
        [in_hbm, in_vmem, in_vmem, in_hbm],
        [shape_of(cleaned.shape, f32), shape_of((8, 128), f32)],
        out_specs=[in_hbm, in_vmem],
        after=after,
        input_output_aliases={3: 0},
        scratch_shapes=[
            pltpu.VMEM(cleaned.shape, f32),
            pltpu.SMEM(adapter_ids.shape, jnp.int32),
            pltpu.SMEM((per_owner,), jnp.int32),
            pltpu.SemaphoreType.DMA((per_owner + 1,)),
        ],
    )


def arrange(lengths, grad, pieces, after):
    rows, columns = grad.shape
    count = 1 + len(pieces)
    first = rows // early_part

    def body(lengths, grad, *refs):
        pieces, kept = refs[:-1], refs[-1]
        at = lax.axis_index("tp")
        live = lax.broadcasted_iota(jnp.int32, (rows, columns), 0) < lengths[0]
        zero = jnp.zeros((rows, columns), bf16)
        place = pl.multiple_of(at * columns, 128)
        kept[:, pl.ds(place, columns)] = jnp.where(live, grad[...], zero)
        for step in range(1, count):
            place = pl.multiple_of(lax.rem(at + count - step, count) * columns, 128)
            early, late = pieces[2 * step - 2 : 2 * step]
            kept[:first, pl.ds(place, columns)] = jnp.where(live[:first], early[...], zero[:first])
            kept[first:, pl.ds(place, columns)] = jnp.where(live[first:], late[...], zero[first:])

    flat = [x for pair in pieces for x in pair]
    return call(
        body,
        [lengths, grad, *flat],
        [in_smem] + [in_vmem] * (1 + len(flat)),
        [shape_of((rows, count * columns), bf16)],
        after=after,
    )[0]


def input_side(kept, frozen, frozen_other, back, down, begin, count, before, after):
    rows = kept.shape[0]
    features, half = frozen.shape
    width = width_of(features)
    held_in = [] if before is None else [before]

    def body(kept, frozen, frozen_other, back, down, *refs):
        out, mark, held, sems = refs[len(held_in) :]
        mark[...] = jnp.zeros(mark.shape, f32)
        sub = lax.axis_index("sub")
        both = (((1,), (1,)), ((), ()))
        mine = kept[:, pl.ds(pl.multiple_of(sub * half, 128), half)]
        other = kept[:, pl.ds(pl.multiple_of((1 - sub) * half, 128), half)]
        twice = adapter_scale * back[...]
        copies = []
        for at in range(count):
            here = slice((begin + at) * width, (begin + at + 1) * width)
            total = lax.dot_general(mine, frozen[here, :], both, preferred_element_type=f32)
            total += lax.dot_general(other, frozen_other[here, :], both, preferred_element_type=f32)
            total += lax.dot_general(
                twice, down[:, here], (((0,), (0,)), ((), ())), preferred_element_type=f32
            )
            there = slice(at * width, (at + 1) * width)
            held[:, there] = total.astype(bf16)
            copies.append(
                pltpu.make_async_copy(held.at[:, there], out.at[:, here], sems.at[at])
            )
            copies[-1].start()
        for copy in copies:
            copy.wait()

    return call(
        body,
        [kept, frozen, frozen_other, back, down, *held_in],
        [in_vmem] * 5 + [in_hbm] * len(held_in),
        [shape_of((rows, features), bf16), shape_of((8, 128), f32)],
        out_specs=[in_hbm, in_vmem],
        after=after,
        input_output_aliases={5: 0} if held_in else {},
        scratch_shapes=[
            pltpu.VMEM((rows, count * width), bf16),
            pltpu.SemaphoreType.DMA((count,)),
        ],
        flops=2 * rows * width * count * (2 * half + back.shape[0]),
    )


def on_device(tokens, grad_output, frozen_value, shared_down, head_up, adapter_ids, lengths):
    rows, features = tokens.shape
    own_count = lax.axis_size("own")
    tp_count = lax.axis_size("tp")
    per_owner = head_up.shape[0]
    scale = adapter_scale / rows
    tp_steps, own_steps = range(1, tp_count), range(1, own_count)

    frozen_other = shift(frozen_value, "sub", 1)
    picked, early, away = pick_heads(adapter_ids, head_up, grad_output)
    steps = sorted(own_steps, key=lambda step: (-step.bit_length(), step))
    offered = [picked[0]] + [swap(picked[step], step, 0) for step in steps]
    early_grads = [shift(early, "tp", step) for step in tp_steps]

    down = shared_down.T
    low = project_low(tokens, down, picked[:1])
    sent = rounded(low, [frozen_other])
    lows = [low] + [shift(sent, "tp", step) for step in tp_steps]

    part = project_back(away, offered, steps, grad_output, [low])
    parts = [part] + [shift(part, "tp", step) for step in tp_steps]

    near, late = head_term(lengths, lows, grad_output, scale, [part, *early_grads])
    late_grads = [shift(late, "tp", step) for step in tp_steps]
    terms = [near] + [swap(near, step, 0) for step in own_steps]
    back, keep, send = shared_terms(lengths, parts, tokens, scale, [near])
    pieces = [keep, shift(send, "sub", 1)]
    met = stack(terms[1:3], flops=middling) if own_count > 1 else near

    bits = [1 << i for i in range(own_count.bit_length() - 1)]
    mark = met
    for bit in bits[:-1]:
        stays, leaves = halve(pieces, bit, [mark])
        pieces = [stays, swap(leaves, bit, 0)]
        mark = leaves
    cleaned, mark = clean((per_owner,) + near.shape[1:], [mark])
    near = stack(terms, [mark])
    far = shift(near, "sub", 1)
    total = add_up(pieces, [near], flops=busy)
    grad_heads, mark = place_terms(
        adapter_ids, near, far, range(own_count), cleaned, [total]
    )
    kept = arrange(lengths, grad_output, list(zip(early_grads, late_grads)), [mark])
    sides = (frozen_value, frozen_other, back, down)
    blocks = features // width_of(features)
    cut = max(1, blocks * 2 // 5)
    input_gradient, mark = input_side(kept, *sides, 0, cut, None, [mark])
    if bits:
        total = add_up([total, swap(total, bits[-1], 0)], [mark])
    if blocks > cut:
        input_gradient, mark = input_side(
            kept, *sides, cut, blocks - cut, input_gradient, [total]
        )
    for bit in reversed(bits[:-1]):
        total = rejoin(total, swap(total, bit, 0), bit, [mark])
        mark = total
    shared_down_gradient = join_shares(total, shift(total, "sub", 1), [mark]).T
    return (input_gradient, shared_down_gradient, grad_heads)


def solution(mesh):
    placed = (
        P(("rep", "own", "sub"), "tp"),
        P(("rep", "own", "sub"), "tp"),
        P("tp", "sub"),
        P("tp", None),
        P("own", None, "tp"),
        P("rep"),
        P(("rep", "own", "sub")),
    )
    return jax.shard_map(
        on_device,
        mesh=mesh,
        in_specs=placed,
        out_specs=(
            P(("rep", "own", "sub"), "tp"),
            P(("rep", "tp"), None),
            P(("rep", "own"), None, "tp"),
        ),
        check_vma=False,
    )
```

```python
import jax
import jax.numpy as jnp
from jax import lax
from jax.experimental import pallas as pl
from jax.experimental.pallas import tpu as pltpu
from jax.sharding import PartitionSpec as P

adapter_scale = 2.0
f32 = jnp.float32
bf16 = jnp.bfloat16

early_part = 4

(busy, first_cost, middling, filling, brief, slight) = (
    10**10, 5 * 10**9, 5 * 10**9, 10**10, 3 * 10**9, 15 * 10**8
)

anywhere = pl.BlockSpec(memory_space=pl.ANY)
in_hbm = pl.BlockSpec(memory_space=pltpu.HBM)
in_vmem = pl.BlockSpec(memory_space=pltpu.VMEM)
in_smem = pl.BlockSpec(memory_space=pltpu.SMEM)


def shift(x, axis, step):
    count = lax.axis_size(axis)
    return lax.ppermute(x, axis, [(i, (i + step) % count) for i in range(count)])


def swap(x, own_bit, sub_bit):
    subs = lax.axis_size("sub")
    whole = lax.axis_size("own") * subs
    other = own_bit * subs + sub_bit
    return lax.ppermute(x, ("own", "sub"), [(i, i ^ other) for i in range(whole)])


def width_of(features):
    return next(width for width in (512, 256, 128) if features % width == 0)


def stay(x):
    return pltpu.with_memory_space_constraint(x, pltpu.HBM)


def shape_of(dims, kind):
    return jax.ShapeDtypeStruct(dims, kind)


def call(body, operands, specs, outs, out_specs=None, after=(), flops=0, **more):
    count, idle = len(operands), len(after)

    def kernel(*refs):
        body(*refs[:count], *refs[count + idle :])

    moved = sum(x.size * x.dtype.itemsize for x in list(operands) + list(outs))
    return pl.pallas_call(
        kernel,
        out_shape=outs,
        in_specs=list(specs) + [anywhere] * len(after),
        out_specs=[in_vmem] * len(outs) if out_specs is None else out_specs,
        compiler_params=pltpu.CompilerParams(vmem_limit_bytes=24 * 1024 * 1024),
        cost_estimate=pl.CostEstimate(flops=flops, bytes_accessed=moved, transcendentals=0),
        **more,
    )(*operands, *after)


def pick_heads(adapter_ids, head_up, grad):
    per_owner, rank, width = head_up.shape
    own_count, sub_count = lax.axis_size("own"), lax.axis_size("sub")
    first = grad.shape[0] // early_part

    def body(ids_far, head_up, grad, *refs):
        outs, early, away, ids, maps, sems = refs[:own_count], *refs[own_count:]
        own, sub = lax.axis_index("own"), lax.axis_index("sub")
        copies = [
            pltpu.make_async_copy(ids_far, ids, sems.at[0]),
            pltpu.make_async_copy(head_up, maps, sems.at[1]),
            pltpu.make_async_copy(grad.at[pl.ds(0, first)], early, sems.at[2]),
        ]
        for copy in copies:
            copy.start()
        copies[0].wait()
        copies[1].wait()
        for step in range(own_count):
            local = ids[(own ^ step) * sub_count + sub] - own * per_owner
            outs[step][...] = maps[jnp.clip(local, 0, per_owner - 1)]
        step = lax.div(ids[own * sub_count + sub], per_owner) ^ own
        away[...] = jnp.full(away.shape, step, jnp.int32)
        copies[2].wait()

    *picked, early, away = call(
        body,
        [stay(adapter_ids), stay(head_up), stay(grad)],
        [in_hbm] * 3,
        [shape_of((rank, width), bf16)] * own_count
        + [shape_of((first, grad.shape[1]), bf16), shape_of((8, 128), jnp.int32)],
        scratch_shapes=[
            pltpu.SMEM(adapter_ids.shape, jnp.int32),
            pltpu.VMEM(head_up.shape, bf16),
            pltpu.SemaphoreType.DMA((3,)),
        ],
        flops=first_cost,
    )
    return picked, early, away


def project_low(tokens, down, after):
    rows, features = tokens.shape
    rank = down.shape[0]

    def body(tokens, down, low):
        low[...] = lax.dot_general(
            down[...], tokens[...], (((1,), (1,)), ((), ())), preferred_element_type=f32
        )

    return call(
        body,
        [tokens, down],
        [in_vmem] * 2,
        [shape_of((rank, rows), f32)],
        after=after,
        flops=2 * rows * rank * features,
    )[0]


def rounded(x, after):
    def body(x, out):
        out[...] = x[...].astype(bf16)

    return call(body, [x], [in_vmem], [shape_of(x.shape, bf16)], after=after)[0]


def project_back(away, offered, steps, grad, after):
    rank, columns = offered[0].shape
    rows = grad.shape[0]

    def body(away, *refs):
        *offered, grad, part = refs
        step = jnp.broadcast_to(away[:1, :1], (rank, columns))
        head = offered[0][...].astype(f32)
        for at, block in zip(steps, offered[1:]):
            head = jnp.where(step == at, block[...].astype(f32), head)
        part[...] = lax.dot_general(
            head.astype(bf16), grad[...], (((1,), (1,)), ((), ())), preferred_element_type=f32
        )

    return call(
        body,
        [away, *offered, grad],
        [in_vmem] * (len(offered) + 2),
        [shape_of((rank, rows), f32)],
        after=after,
        flops=slight,
    )[0]


def head_term(lengths, lows, grad, scale, after):
    rank, rows = lows[0].shape
    columns = grad.shape[1]
    first = rows // early_part

    def body(lengths, *refs):
        *lows, grad, term, late = refs
        total = lows[0][...]
        for low in lows[1:]:
            total = total + low[...].astype(f32)
        live = lax.broadcasted_iota(jnp.int32, total.shape, 1) < lengths[0]
        total = jnp.where(live, total, 0.0)
        kept = total.astype(bf16)
        rest = (total - kept.astype(f32)).astype(bf16)
        product = jnp.dot(kept, grad[...], preferred_element_type=f32)
        product += jnp.dot(rest, grad[...], preferred_element_type=f32)
        term[0] = (scale * product).astype(bf16)
        late[...] = grad[first:, :]

    return call(
        body,
        [lengths, *lows, grad],
        [in_smem] + [in_vmem] * (len(lows) + 1),
        [shape_of((1, rank, columns), bf16), shape_of((rows - first, columns), bf16)],
        after=after,
        flops=brief,
    )


def shared_terms(lengths, parts, tokens, scale, after):
    rows, features = tokens.shape
    rank = parts[0].shape[0]
    share = rank // 2

    def body(lengths, *refs):
        parts, (tokens, back, keep, send, total) = refs[:count], refs[count:]
        sub = lax.axis_index("sub")
        both = parts[0][...]
        for part in parts[1:]:
            both = both + part[...]
        live = lax.broadcasted_iota(jnp.int32, both.shape, 1) < lengths[0]
        back[...] = jnp.where(live, both, 0.0).astype(bf16)
        total[...] = scale * jnp.dot(back[...], tokens[...], preferred_element_type=f32)
        keep[...] = total[pl.ds(pl.multiple_of(sub * share, share), share), :]
        send[...] = total[pl.ds(pl.multiple_of((1 - sub) * share, share), share), :]

    count = len(parts)
    return call(
        body,
        [lengths, *parts, tokens],
        [in_smem] + [in_vmem] * (count + 1),
        [shape_of((rank, rows), bf16)] + [shape_of((share, features), f32)] * 2,
        after=after,
        scratch_shapes=[pltpu.VMEM((rank, features), f32)],
        flops=2 * rows * rank * features,
    )


def marked(after, flops):
    def body(out):
        out[...] = jnp.zeros(out.shape, f32)

    return call(body, [], [], [shape_of((8, 128), f32)], after=after, flops=flops)[0]


def add_up(pieces, after=(), flops=0):
    def body(*refs):
        total = refs[0][...].astype(f32)
        for piece in refs[1:-1]:
            total = total + piece[...].astype(f32)
        refs[-1][...] = total.astype(bf16)

    return call(
        body,
        list(pieces),
        [in_vmem] * len(pieces),
        [shape_of(pieces[0].shape, bf16)],
        after=after,
        flops=flops,
    )[0]


def halve(pieces, bit, after=()):
    rows, features = pieces[0].shape
    half = rows // 2

    def body(*refs):
        total = refs[0][...].astype(f32)
        for piece in refs[1:-2]:
            total = total + piece[...].astype(f32)
        upper = lax.rem(lax.div(lax.axis_index("own"), bit), 2) == 1
        low, high = total[:half], total[half:]
        refs[-2][...] = jnp.where(upper, high, low)
        refs[-1][...] = jnp.where(upper, low, high).astype(bf16)

    return call(
        body,
        list(pieces),
        [in_vmem] * len(pieces),
        [shape_of((half, features), f32), shape_of((half, features), bf16)],
        after=after,
    )


def rejoin(mine, arrived, bit, after):
    rows, features = mine.shape

    def body(mine, arrived, out):
        upper = lax.rem(lax.div(lax.axis_index("own"), bit), 2) == 1
        one, two = mine[...].astype(f32), arrived[...].astype(f32)
        out[:rows] = jnp.where(upper, two, one).astype(bf16)
        out[rows:] = jnp.where(upper, one, two).astype(bf16)

    return call(
        body,
        [mine, arrived],
        [in_vmem] * 2,
        [shape_of((2 * rows, features), bf16)],
        after=after,
        flops=busy,
    )[0]


def join_shares(mine, other, after):
    share, features = mine.shape

    def body(mine, other, out):
        sub = lax.axis_index("sub")
        for side, piece in ((sub, mine), (1 - sub, other)):
            out[pl.ds(pl.multiple_of(side * share, share), share), :] = piece[...].astype(f32)

    return call(
        body,
        [mine, other],
        [in_vmem] * 2,
        [shape_of((2 * share, features), f32)],
        after=after,
    )[0]


def stack(pieces, after=(), flops=0):
    depths = [piece.shape[0] for piece in pieces]

    def body(*refs):
        at = 0
        for depth, piece in zip(depths, refs[:-1]):
            refs[-1][at : at + depth] = piece[...]
            at += depth

    return call(
        body,
        list(pieces),
        [in_vmem] * len(pieces),
        [shape_of((sum(depths),) + pieces[0].shape[1:], bf16)],
        after=after,
        flops=flops,
    )[0]


def clean(dims, after):
    def body(out, mark, held, sem):
        held[...] = jnp.zeros(held.shape, f32)
        mark[...] = jnp.zeros(mark.shape, f32)
        copies = [pltpu.make_async_copy(held, out.at[at], sem.at[at]) for at in range(dims[0])]
        for copy in copies:
            copy.start()
        for copy in copies:
            copy.wait()

    return call(
        body,
        [],
        [],
        [shape_of(dims, f32), shape_of((8, 128), f32)],
        out_specs=[in_hbm, in_vmem],
        after=after,
        scratch_shapes=[pltpu.VMEM(dims[1:], f32), pltpu.SemaphoreType.DMA((dims[0],))],
        flops=filling,
    )


def place_terms(adapter_ids, near, far, pattern, cleaned, after):
    per_owner, rank, columns = cleaned.shape
    sub_count = lax.axis_size("sub")

    def body(ids_far, near, far, cleaned, out, mark, held, ids, counts, sems):
        own, sub = lax.axis_index("own"), lax.axis_index("sub")
        fetch = pltpu.make_async_copy(ids_far, ids, sems.at[per_owner])
        fetch.start()
        mark[...] = jnp.zeros(mark.shape, f32)
        for local in range(per_owner):
            counts[local] = 0
        fetch.wait()
        for at, step in enumerate(pattern):
            for side in range(sub_count):
                local = ids[(own ^ step) * sub_count + side] - own * per_owner

                @pl.when(jnp.logical_and(local >= 0, local < per_owner))
                def _():
                    term = jnp.where(sub == side, near[at], far[at]).astype(f32)

                    @pl.when(counts[local] == 0)
                    def _():
                        held[local] = term

                    @pl.when(counts[local] > 0)
                    def _():
                        held[local] += term

                    counts[local] += 1

        copies = [
            pltpu.make_async_copy(held.at[local], out.at[local], sems.at[local])
            for local in range(per_owner)
        ]
        for local, copy in enumerate(copies):
            pl.when(counts[local] > 0)(copy.start)
        for local, copy in enumerate(copies):
            pl.when(counts[local] > 0)(copy.wait)

    return call(
        body,
        [stay(adapter_ids), near, far, cleaned],
        [in_hbm, in_vmem, in_vmem, in_hbm],
        [shape_of(cleaned.shape, f32), shape_of((8, 128), f32)],
        out_specs=[in_hbm, in_vmem],
        after=after,
        input_output_aliases={3: 0},
        scratch_shapes=[
            pltpu.VMEM(cleaned.shape, f32),
            pltpu.SMEM(adapter_ids.shape, jnp.int32),
            pltpu.SMEM((per_owner,), jnp.int32),
            pltpu.SemaphoreType.DMA((per_owner + 1,)),
        ],
    )


def arrange(lengths, grad, pieces, after):
    rows, columns = grad.shape
    count = 1 + len(pieces)
    first = rows // early_part

    def body(lengths, grad, *refs):
        pieces, kept = refs[:-1], refs[-1]
        at = lax.axis_index("tp")
        live = lax.broadcasted_iota(jnp.int32, (rows, columns), 0) < lengths[0]
        zero = jnp.zeros((rows, columns), bf16)
        place = pl.multiple_of(at * columns, 128)
        kept[:, pl.ds(place, columns)] = jnp.where(live, grad[...], zero)
        for step in range(1, count):
            place = pl.multiple_of(lax.rem(at + count - step, count) * columns, 128)
            early, late = pieces[2 * step - 2 : 2 * step]
            kept[:first, pl.ds(place, columns)] = jnp.where(live[:first], early[...], zero[:first])
            kept[first:, pl.ds(place, columns)] = jnp.where(live[first:], late[...], zero[first:])

    flat = [x for pair in pieces for x in pair]
    return call(
        body,
        [lengths, grad, *flat],
        [in_smem] + [in_vmem] * (1 + len(flat)),
        [shape_of((rows, count * columns), bf16)],
        after=after,
    )[0]


def input_side(kept, frozen, frozen_other, back, down, begin, count, before, after):
    rows = kept.shape[0]
    features, half = frozen.shape
    width = width_of(features)
    held_in = [] if before is None else [before]

    def body(kept, frozen, frozen_other, back, down, *refs):
        out, mark, held, sems = refs[len(held_in) :]
        mark[...] = jnp.zeros(mark.shape, f32)
        sub = lax.axis_index("sub")
        both = (((1,), (1,)), ((), ()))
        mine = kept[:, pl.ds(pl.multiple_of(sub * half, 128), half)]
        other = kept[:, pl.ds(pl.multiple_of((1 - sub) * half, 128), half)]
        twice = adapter_scale * back[...]
        copies = []
        for at in range(count):
            here = slice((begin + at) * width, (begin + at + 1) * width)
            total = lax.dot_general(mine, frozen[here, :], both, preferred_element_type=f32)
            total += lax.dot_general(other, frozen_other[here, :], both, preferred_element_type=f32)
            total += lax.dot_general(
                twice, down[:, here], (((0,), (0,)), ((), ())), preferred_element_type=f32
            )
            there = slice(at * width, (at + 1) * width)
            held[:, there] = total.astype(bf16)
            copies.append(
                pltpu.make_async_copy(held.at[:, there], out.at[:, here], sems.at[at])
            )
            copies[-1].start()
        for copy in copies:
            copy.wait()

    return call(
        body,
        [kept, frozen, frozen_other, back, down, *held_in],
        [in_vmem] * 5 + [in_hbm] * len(held_in),
        [shape_of((rows, features), bf16), shape_of((8, 128), f32)],
        out_specs=[in_hbm, in_vmem],
        after=after,
        input_output_aliases={5: 0} if held_in else {},
        scratch_shapes=[
            pltpu.VMEM((rows, count * width), bf16),
            pltpu.SemaphoreType.DMA((count,)),
        ],
        flops=2 * rows * width * count * (2 * half + back.shape[0]),
    )


def on_device(tokens, grad_output, frozen_value, shared_down, head_up, adapter_ids, lengths):
    rows, features = tokens.shape
    own_count = lax.axis_size("own")
    tp_count = lax.axis_size("tp")
    per_owner = head_up.shape[0]
    scale = adapter_scale / rows
    tp_steps, own_steps = range(1, tp_count), range(1, own_count)

    frozen_other = shift(frozen_value, "sub", 1)
    picked, early, away = pick_heads(adapter_ids, head_up, grad_output)
    steps = sorted(own_steps, key=lambda step: (-step.bit_length(), step))
    offered = [picked[0]] + [swap(picked[step], step, 0) for step in steps]
    early_grads = [shift(early, "tp", step) for step in tp_steps]

    down = shared_down.T
    low = project_low(tokens, down, picked[:1])
    sent = rounded(low, [frozen_other])
    lows = [low] + [shift(sent, "tp", step) for step in tp_steps]

    part = project_back(away, offered, steps, grad_output, [low])
    parts = [part] + [shift(part, "tp", step) for step in tp_steps]

    near, late = head_term(lengths, lows, grad_output, scale, [part, *early_grads])
    late_grads = [shift(late, "tp", step) for step in tp_steps]
    terms = [near] + [swap(near, step, 0) for step in steps[::-1]]
    back, keep, send = shared_terms(lengths, parts, tokens, scale, [near])
    pieces = [keep, shift(send, "sub", 1)]
    met = marked([back], flops=middling)

    bits = [1 << i for i in range(own_count.bit_length() - 1)]
    mark = met
    for bit in bits[:-1]:
        stays, leaves = halve(pieces, bit, [mark])
        pieces = [stays, swap(leaves, bit, 0)]
        mark = leaves
    cleaned, mark = clean((per_owner,) + near.shape[1:], [mark])
    near = stack(terms, [mark])
    far = shift(near, "sub", 1)
    total = add_up(pieces, [near], flops=busy)
    grad_heads, mark = place_terms(
        adapter_ids, near, far, [0] + steps[::-1], cleaned, [total]
    )
    kept = arrange(lengths, grad_output, list(zip(early_grads, late_grads)), [mark])
    sides = (frozen_value, frozen_other, back, down)
    blocks = features // width_of(features)
    cut = max(1, blocks * 2 // 5)
    input_gradient, mark = input_side(kept, *sides, 0, cut, None, [mark])
    if bits:
        total = add_up([total, swap(total, bits[-1], 0)], [mark])
    if blocks > cut:
        input_gradient, mark = input_side(
            kept, *sides, cut, blocks - cut, input_gradient, [total]
        )
    for bit in reversed(bits[:-1]):
        total = rejoin(total, swap(total, bit, 0), bit, [mark])
        mark = total
    shared_down_gradient = join_shares(total, shift(total, "sub", 1), [mark]).T
    return (input_gradient, shared_down_gradient, grad_heads)


def solution(mesh):
    placed = (
        P(("rep", "own", "sub"), "tp"),
        P(("rep", "own", "sub"), "tp"),
        P("tp", "sub"),
        P("tp", None),
        P("own", None, "tp"),
        P("rep"),
        P(("rep", "own", "sub")),
    )
    return jax.shard_map(
        on_device,
        mesh=mesh,
        in_specs=placed,
        out_specs=(
            P(("rep", "own", "sub"), "tp"),
            P(("rep", "tp"), None),
            P(("rep", "own"), None, "tp"),
        ),
        check_vma=False,
    )
```

```python
import jax
import jax.numpy as jnp
from jax import lax
from jax.experimental import pallas as pl
from jax.experimental.pallas import tpu as pltpu
from jax.sharding import PartitionSpec as P

adapter_scale = 2.0
f32 = jnp.float32
bf16 = jnp.bfloat16

early_part = 4

(busy, first_cost, middling, filling, brief, slight) = (
    10**10, 5 * 10**9, 5 * 10**9, 10**10, 3 * 10**9, 15 * 10**8
)

anywhere = pl.BlockSpec(memory_space=pl.ANY)
in_hbm = pl.BlockSpec(memory_space=pltpu.HBM)
in_vmem = pl.BlockSpec(memory_space=pltpu.VMEM)
in_smem = pl.BlockSpec(memory_space=pltpu.SMEM)


def shift(x, axis, step):
    count = lax.axis_size(axis)
    return lax.ppermute(x, axis, [(i, (i + step) % count) for i in range(count)])


def swap(x, own_bit, sub_bit):
    subs = lax.axis_size("sub")
    whole = lax.axis_size("own") * subs
    other = own_bit * subs + sub_bit
    return lax.ppermute(x, ("own", "sub"), [(i, i ^ other) for i in range(whole)])


def width_of(features):
    return next(width for width in (512, 256, 128) if features % width == 0)


def stay(x):
    return pltpu.with_memory_space_constraint(x, pltpu.HBM)


def shape_of(dims, kind):
    return jax.ShapeDtypeStruct(dims, kind)


def call(body, operands, specs, outs, out_specs=None, after=(), flops=0, **more):
    count, idle = len(operands), len(after)

    def kernel(*refs):
        body(*refs[:count], *refs[count + idle :])

    moved = sum(x.size * x.dtype.itemsize for x in list(operands) + list(outs))
    return pl.pallas_call(
        kernel,
        out_shape=outs,
        in_specs=list(specs) + [anywhere] * len(after),
        out_specs=[in_vmem] * len(outs) if out_specs is None else out_specs,
        compiler_params=pltpu.CompilerParams(vmem_limit_bytes=24 * 1024 * 1024),
        cost_estimate=pl.CostEstimate(flops=flops, bytes_accessed=moved, transcendentals=0),
        **more,
    )(*operands, *after)


def pick_heads(adapter_ids, head_up, grad):
    per_owner, rank, width = head_up.shape
    own_count, sub_count = lax.axis_size("own"), lax.axis_size("sub")
    first = grad.shape[0] // early_part

    def body(ids_far, head_up, grad, *refs):
        outs, early, away, ids, maps, sems = refs[:own_count], *refs[own_count:]
        own, sub = lax.axis_index("own"), lax.axis_index("sub")
        copies = [
            pltpu.make_async_copy(ids_far, ids, sems.at[0]),
            pltpu.make_async_copy(head_up, maps, sems.at[1]),
            pltpu.make_async_copy(grad.at[pl.ds(0, first)], early, sems.at[2]),
        ]
        for copy in copies:
            copy.start()
        copies[0].wait()
        copies[1].wait()
        for step in range(own_count):
            local = ids[(own ^ step) * sub_count + sub] - own * per_owner
            outs[step][...] = maps[jnp.clip(local, 0, per_owner - 1)]
        step = lax.div(ids[own * sub_count + sub], per_owner) ^ own
        away[...] = jnp.full(away.shape, step, jnp.int32)
        copies[2].wait()

    *picked, early, away = call(
        body,
        [stay(adapter_ids), stay(head_up), stay(grad)],
        [in_hbm] * 3,
        [shape_of((rank, width), bf16)] * own_count
        + [shape_of((first, grad.shape[1]), bf16), shape_of((8, 128), jnp.int32)],
        scratch_shapes=[
            pltpu.SMEM(adapter_ids.shape, jnp.int32),
            pltpu.VMEM(head_up.shape, bf16),
            pltpu.SemaphoreType.DMA((3,)),
        ],
        flops=first_cost,
    )
    return picked, early, away


def project_low(tokens, down, after):
    rows, features = tokens.shape
    rank = down.shape[0]

    def body(tokens, down, low):
        low[...] = lax.dot_general(
            down[...], tokens[...], (((1,), (1,)), ((), ())), preferred_element_type=f32
        )

    return call(
        body,
        [tokens, down],
        [in_vmem] * 2,
        [shape_of((rank, rows), f32)],
        after=after,
        flops=2 * rows * rank * features,
    )[0]


def rounded(x, after):
    def body(x, out):
        out[...] = x[...].astype(bf16)

    return call(body, [x], [in_vmem], [shape_of(x.shape, bf16)], after=after)[0]


def project_back(away, offered, steps, grad, after):
    rank, columns = offered[0].shape
    rows = grad.shape[0]

    def body(away, *refs):
        *offered, grad, part = refs
        step = jnp.broadcast_to(away[:1, :1], (rank, columns))
        head = offered[0][...].astype(f32)
        for at, block in zip(steps, offered[1:]):
            head = jnp.where(step == at, block[...].astype(f32), head)
        part[...] = lax.dot_general(
            head.astype(bf16), grad[...], (((1,), (1,)), ((), ())), preferred_element_type=f32
        )

    return call(
        body,
        [away, *offered, grad],
        [in_vmem] * (len(offered) + 2),
        [shape_of((rank, rows), f32)],
        after=after,
        flops=slight,
    )[0]


def head_term(lengths, lows, grad, scale, after):
    rank, rows = lows[0].shape
    columns = grad.shape[1]
    first = rows // early_part

    def body(lengths, *refs):
        *lows, grad, term, late = refs
        total = lows[0][...]
        for low in lows[1:]:
            total = total + low[...].astype(f32)
        live = lax.broadcasted_iota(jnp.int32, total.shape, 1) < lengths[0]
        total = jnp.where(live, total, 0.0)
        kept = total.astype(bf16)
        rest = (total - kept.astype(f32)).astype(bf16)
        product = jnp.dot(kept, grad[...], preferred_element_type=f32)
        product += jnp.dot(rest, grad[...], preferred_element_type=f32)
        term[0] = (scale * product).astype(bf16)
        late[...] = grad[first:, :]

    return call(
        body,
        [lengths, *lows, grad],
        [in_smem] + [in_vmem] * (len(lows) + 1),
        [shape_of((1, rank, columns), bf16), shape_of((rows - first, columns), bf16)],
        after=after,
        flops=brief,
    )


def shared_terms(lengths, parts, tokens, scale, after):
    rows, features = tokens.shape
    rank = parts[0].shape[0]
    share = rank // 2

    def body(lengths, *refs):
        parts, (tokens, back, keep, send, total) = refs[:count], refs[count:]
        sub = lax.axis_index("sub")
        both = parts[0][...]
        for part in parts[1:]:
            both = both + part[...]
        live = lax.broadcasted_iota(jnp.int32, both.shape, 1) < lengths[0]
        back[...] = jnp.where(live, both, 0.0).astype(bf16)
        total[...] = scale * jnp.dot(back[...], tokens[...], preferred_element_type=f32)
        keep[...] = total[pl.ds(pl.multiple_of(sub * share, share), share), :]
        send[...] = total[pl.ds(pl.multiple_of((1 - sub) * share, share), share), :]

    count = len(parts)
    return call(
        body,
        [lengths, *parts, tokens],
        [in_smem] + [in_vmem] * (count + 1),
        [shape_of((rank, rows), bf16)] + [shape_of((share, features), f32)] * 2,
        after=after,
        scratch_shapes=[pltpu.VMEM((rank, features), f32)],
        flops=2 * rows * rank * features,
    )


def add_up(pieces, after=(), flops=0):
    def body(*refs):
        total = refs[0][...].astype(f32)
        for piece in refs[1:-1]:
            total = total + piece[...].astype(f32)
        refs[-1][...] = total.astype(bf16)

    return call(
        body,
        list(pieces),
        [in_vmem] * len(pieces),
        [shape_of(pieces[0].shape, bf16)],
        after=after,
        flops=flops,
    )[0]


def halve(pieces, bit, after=()):
    rows, features = pieces[0].shape
    half = rows // 2

    def body(*refs):
        total = refs[0][...].astype(f32)
        for piece in refs[1:-2]:
            total = total + piece[...].astype(f32)
        upper = lax.rem(lax.div(lax.axis_index("own"), bit), 2) == 1
        low, high = total[:half], total[half:]
        refs[-2][...] = jnp.where(upper, high, low)
        refs[-1][...] = jnp.where(upper, low, high).astype(bf16)

    return call(
        body,
        list(pieces),
        [in_vmem] * len(pieces),
        [shape_of((half, features), f32), shape_of((half, features), bf16)],
        after=after,
    )


def rejoin(mine, arrived, bit, after):
    rows, features = mine.shape

    def body(mine, arrived, out):
        upper = lax.rem(lax.div(lax.axis_index("own"), bit), 2) == 1
        one, two = mine[...].astype(f32), arrived[...].astype(f32)
        out[:rows] = jnp.where(upper, two, one).astype(bf16)
        out[rows:] = jnp.where(upper, one, two).astype(bf16)

    return call(
        body,
        [mine, arrived],
        [in_vmem] * 2,
        [shape_of((2 * rows, features), bf16)],
        after=after,
        flops=busy,
    )[0]


def join_shares(mine, other, after):
    share, features = mine.shape

    def body(mine, other, out):
        sub = lax.axis_index("sub")
        for side, piece in ((sub, mine), (1 - sub, other)):
            out[pl.ds(pl.multiple_of(side * share, share), share), :] = piece[...].astype(f32)

    return call(
        body,
        [mine, other],
        [in_vmem] * 2,
        [shape_of((2 * share, features), f32)],
        after=after,
    )[0]


def stack(pieces, after=(), flops=0):
    depths = [piece.shape[0] for piece in pieces]

    def body(*refs):
        at = 0
        for depth, piece in zip(depths, refs[:-1]):
            refs[-1][at : at + depth] = piece[...]
            at += depth

    return call(
        body,
        list(pieces),
        [in_vmem] * len(pieces),
        [shape_of((sum(depths),) + pieces[0].shape[1:], bf16)],
        after=after,
        flops=flops,
    )[0]


def clean(dims, after):
    def body(out, mark, held, sem):
        held[...] = jnp.zeros(held.shape, f32)
        mark[...] = jnp.zeros(mark.shape, f32)
        copies = [pltpu.make_async_copy(held, out.at[at], sem.at[at]) for at in range(dims[0])]
        for copy in copies:
            copy.start()
        for copy in copies:
            copy.wait()

    return call(
        body,
        [],
        [],
        [shape_of(dims, f32), shape_of((8, 128), f32)],
        out_specs=[in_hbm, in_vmem],
        after=after,
        scratch_shapes=[pltpu.VMEM(dims[1:], f32), pltpu.SemaphoreType.DMA((dims[0],))],
        flops=filling,
    )


def place_terms(adapter_ids, near, far, pattern, cleaned, after):
    per_owner, rank, columns = cleaned.shape
    sub_count = lax.axis_size("sub")

    def body(ids_far, near, far, cleaned, out, mark, held, ids, counts, sems):
        own, sub = lax.axis_index("own"), lax.axis_index("sub")
        fetch = pltpu.make_async_copy(ids_far, ids, sems.at[per_owner])
        fetch.start()
        mark[...] = jnp.zeros(mark.shape, f32)
        for local in range(per_owner):
            counts[local] = 0
        fetch.wait()
        for at, step in enumerate(pattern):
            for side in range(sub_count):
                local = ids[(own ^ step) * sub_count + side] - own * per_owner

                @pl.when(jnp.logical_and(local >= 0, local < per_owner))
                def _():
                    term = jnp.where(sub == side, near[at], far[at]).astype(f32)

                    @pl.when(counts[local] == 0)
                    def _():
                        held[local] = term

                    @pl.when(counts[local] > 0)
                    def _():
                        held[local] += term

                    counts[local] += 1

        copies = [
            pltpu.make_async_copy(held.at[local], out.at[local], sems.at[local])
            for local in range(per_owner)
        ]
        for local, copy in enumerate(copies):
            pl.when(counts[local] > 0)(copy.start)
        for local, copy in enumerate(copies):
            pl.when(counts[local] > 0)(copy.wait)

    return call(
        body,
        [stay(adapter_ids), near, far, cleaned],
        [in_hbm, in_vmem, in_vmem, in_hbm],
        [shape_of(cleaned.shape, f32), shape_of((8, 128), f32)],
        out_specs=[in_hbm, in_vmem],
        after=after,
        input_output_aliases={3: 0},
        scratch_shapes=[
            pltpu.VMEM(cleaned.shape, f32),
            pltpu.SMEM(adapter_ids.shape, jnp.int32),
            pltpu.SMEM((per_owner,), jnp.int32),
            pltpu.SemaphoreType.DMA((per_owner + 1,)),
        ],
    )


def arrange(lengths, grad, pieces, after):
    rows, columns = grad.shape
    count = 1 + len(pieces)
    first = rows // early_part

    def body(lengths, grad, *refs):
        pieces, kept = refs[:-1], refs[-1]
        at = lax.axis_index("tp")
        live = lax.broadcasted_iota(jnp.int32, (rows, columns), 0) < lengths[0]
        zero = jnp.zeros((rows, columns), bf16)
        place = pl.multiple_of(at * columns, 128)
        kept[:, pl.ds(place, columns)] = jnp.where(live, grad[...], zero)
        for step in range(1, count):
            place = pl.multiple_of(lax.rem(at + count - step, count) * columns, 128)
            early, late = pieces[2 * step - 2 : 2 * step]
            kept[:first, pl.ds(place, columns)] = jnp.where(live[:first], early[...], zero[:first])
            kept[first:, pl.ds(place, columns)] = jnp.where(live[first:], late[...], zero[first:])

    flat = [x for pair in pieces for x in pair]
    return call(
        body,
        [lengths, grad, *flat],
        [in_smem] + [in_vmem] * (1 + len(flat)),
        [shape_of((rows, count * columns), bf16)],
        after=after,
    )[0]


def input_side(kept, frozen, frozen_other, back, down, begin, count, before, after):
    rows = kept.shape[0]
    features, half = frozen.shape
    width = width_of(features)
    held_in = [] if before is None else [before]

    def body(kept, frozen, frozen_other, back, down, *refs):
        out, mark, held, sems = refs[len(held_in) :]
        mark[...] = jnp.zeros(mark.shape, f32)
        sub = lax.axis_index("sub")
        both = (((1,), (1,)), ((), ()))
        mine = kept[:, pl.ds(pl.multiple_of(sub * half, 128), half)]
        other = kept[:, pl.ds(pl.multiple_of((1 - sub) * half, 128), half)]
        twice = adapter_scale * back[...]
        copies = []
        for at in range(count):
            here = slice((begin + at) * width, (begin + at + 1) * width)
            total = lax.dot_general(mine, frozen[here, :], both, preferred_element_type=f32)
            total += lax.dot_general(other, frozen_other[here, :], both, preferred_element_type=f32)
            total += lax.dot_general(
                twice, down[:, here], (((0,), (0,)), ((), ())), preferred_element_type=f32
            )
            there = slice(at * width, (at + 1) * width)
            held[:, there] = total.astype(bf16)
            copies.append(
                pltpu.make_async_copy(held.at[:, there], out.at[:, here], sems.at[at])
            )
            copies[-1].start()
        for copy in copies:
            copy.wait()

    return call(
        body,
        [kept, frozen, frozen_other, back, down, *held_in],
        [in_vmem] * 5 + [in_hbm] * len(held_in),
        [shape_of((rows, features), bf16), shape_of((8, 128), f32)],
        out_specs=[in_hbm, in_vmem],
        after=after,
        input_output_aliases={5: 0} if held_in else {},
        scratch_shapes=[
            pltpu.VMEM((rows, count * width), bf16),
            pltpu.SemaphoreType.DMA((count,)),
        ],
        flops=2 * rows * width * count * (2 * half + back.shape[0]),
    )


def on_device(tokens, grad_output, frozen_value, shared_down, head_up, adapter_ids, lengths):
    rows, features = tokens.shape
    own_count = lax.axis_size("own")
    tp_count = lax.axis_size("tp")
    per_owner = head_up.shape[0]
    scale = adapter_scale / rows
    tp_steps, own_steps = range(1, tp_count), range(1, own_count)

    frozen_other = shift(frozen_value, "sub", 1)
    picked, early, away = pick_heads(adapter_ids, head_up, grad_output)
    steps = sorted(own_steps, key=lambda step: (-step.bit_length(), step))
    offered = [picked[0]] + [swap(picked[step], step, 0) for step in steps]
    early_grads = [shift(early, "tp", step) for step in tp_steps]

    down = shared_down.T
    low = project_low(tokens, down, picked[:1])
    sent = rounded(low, [frozen_other])
    lows = [low] + [shift(sent, "tp", step) for step in tp_steps]

    part = project_back(away, offered, steps, grad_output, [low])
    parts = [part] + [shift(part, "tp", step) for step in tp_steps]

    near, late = head_term(lengths, lows, grad_output, scale, [part, *early_grads])
    late_grads = [shift(late, "tp", step) for step in tp_steps]
    back, keep, send = shared_terms(lengths, parts, tokens, scale, [near])
    pieces = [keep, shift(send, "sub", 1)]
    met = stack([near], [back], flops=middling)
    terms = [near] + [swap(met if step == 1 else near, step, 0) for step in steps[::-1]]

    bits = [1 << i for i in range(own_count.bit_length() - 1)]
    mark = back
    for bit in bits[:-1]:
        stays, leaves = halve(pieces, bit, [mark])
        pieces = [stays, swap(leaves, bit, 0)]
        mark = leaves
    cleaned, mark = clean((per_owner,) + near.shape[1:], [mark])
    near = stack(terms, [mark])
    far = shift(near, "sub", 1)
    total = add_up(pieces, [near], flops=busy)
    grad_heads, mark = place_terms(
        adapter_ids, near, far, [0] + steps[::-1], cleaned, [total]
    )
    kept = arrange(lengths, grad_output, list(zip(early_grads, late_grads)), [mark])
    sides = (frozen_value, frozen_other, back, down)
    blocks = features // width_of(features)
    cut = max(1, blocks * 2 // 5)
    input_gradient, mark = input_side(kept, *sides, 0, cut, None, [mark])
    if bits:
        total = add_up([total, swap(total, bits[-1], 0)], [mark])
    if blocks > cut:
        input_gradient, mark = input_side(
            kept, *sides, cut, blocks - cut, input_gradient, [total]
        )
    for bit in reversed(bits[:-1]):
        total = rejoin(total, swap(total, bit, 0), bit, [mark])
        mark = total
    shared_down_gradient = join_shares(total, shift(total, "sub", 1), [mark]).T
    return (input_gradient, shared_down_gradient, grad_heads)


def solution(mesh):
    placed = (
        P(("rep", "own", "sub"), "tp"),
        P(("rep", "own", "sub"), "tp"),
        P("tp", "sub"),
        P("tp", None),
        P("own", None, "tp"),
        P("rep"),
        P(("rep", "own", "sub")),
    )
    return jax.shard_map(
        on_device,
        mesh=mesh,
        in_specs=placed,
        out_specs=(
            P(("rep", "own", "sub"), "tp"),
            P(("rep", "tp"), None),
            P(("rep", "own"), None, "tp"),
        ),
        check_vma=False,
    )
```

```python
import jax
import jax.numpy as jnp
from jax import lax
from jax.experimental import pallas as pl
from jax.experimental.pallas import tpu as pltpu
from jax.sharding import PartitionSpec as P

adapter_scale = 2.0
f32 = jnp.float32
bf16 = jnp.bfloat16

early_part = 4

(busy, first_cost, middling, filling, brief, slight) = (
    10**10, 5 * 10**9, 5 * 10**9, 10**10, 3 * 10**9, 15 * 10**8
)

anywhere = pl.BlockSpec(memory_space=pl.ANY)
in_hbm = pl.BlockSpec(memory_space=pltpu.HBM)
in_vmem = pl.BlockSpec(memory_space=pltpu.VMEM)
in_smem = pl.BlockSpec(memory_space=pltpu.SMEM)


def shift(x, axis, step):
    count = lax.axis_size(axis)
    return lax.ppermute(x, axis, [(i, (i + step) % count) for i in range(count)])


def swap(x, own_bit, sub_bit):
    subs = lax.axis_size("sub")
    whole = lax.axis_size("own") * subs
    other = own_bit * subs + sub_bit
    return lax.ppermute(x, ("own", "sub"), [(i, i ^ other) for i in range(whole)])


def width_of(features):
    return next(width for width in (512, 256, 128) if features % width == 0)


def stay(x):
    return pltpu.with_memory_space_constraint(x, pltpu.HBM)


def shape_of(dims, kind):
    return jax.ShapeDtypeStruct(dims, kind)


def call(body, operands, specs, outs, out_specs=None, after=(), flops=0, **more):
    count, idle = len(operands), len(after)

    def kernel(*refs):
        body(*refs[:count], *refs[count + idle :])

    moved = sum(x.size * x.dtype.itemsize for x in list(operands) + list(outs))
    return pl.pallas_call(
        kernel,
        out_shape=outs,
        in_specs=list(specs) + [anywhere] * len(after),
        out_specs=[in_vmem] * len(outs) if out_specs is None else out_specs,
        compiler_params=pltpu.CompilerParams(vmem_limit_bytes=24 * 1024 * 1024),
        cost_estimate=pl.CostEstimate(flops=flops, bytes_accessed=moved, transcendentals=0),
        **more,
    )(*operands, *after)


def pick_heads(adapter_ids, head_up, grad):
    per_owner, rank, width = head_up.shape
    own_count, sub_count = lax.axis_size("own"), lax.axis_size("sub")
    first = grad.shape[0] // early_part

    def body(ids_far, head_up, grad, *refs):
        outs, early, away, ids, maps, sems = refs[:own_count], *refs[own_count:]
        own, sub = lax.axis_index("own"), lax.axis_index("sub")
        copies = [
            pltpu.make_async_copy(ids_far, ids, sems.at[0]),
            pltpu.make_async_copy(head_up, maps, sems.at[1]),
            pltpu.make_async_copy(grad.at[pl.ds(0, first)], early, sems.at[2]),
        ]
        for copy in copies:
            copy.start()
        copies[0].wait()
        copies[1].wait()
        for step in range(own_count):
            local = ids[(own ^ step) * sub_count + sub] - own * per_owner
            outs[step][...] = maps[jnp.clip(local, 0, per_owner - 1)]
        step = lax.div(ids[own * sub_count + sub], per_owner) ^ own
        away[...] = jnp.full(away.shape, step, jnp.int32)
        copies[2].wait()

    *picked, early, away = call(
        body,
        [stay(adapter_ids), stay(head_up), stay(grad)],
        [in_hbm] * 3,
        [shape_of((rank, width), bf16)] * own_count
        + [shape_of((first, grad.shape[1]), bf16), shape_of((8, 128), jnp.int32)],
        scratch_shapes=[
            pltpu.SMEM(adapter_ids.shape, jnp.int32),
            pltpu.VMEM(head_up.shape, bf16),
            pltpu.SemaphoreType.DMA((3,)),
        ],
        flops=first_cost,
    )
    return picked, early, away


def project_low(tokens, down, after):
    rows, features = tokens.shape
    rank = down.shape[0]

    def body(tokens, down, low):
        low[...] = lax.dot_general(
            down[...], tokens[...], (((1,), (1,)), ((), ())), preferred_element_type=f32
        )

    return call(
        body,
        [tokens, down],
        [in_vmem] * 2,
        [shape_of((rank, rows), f32)],
        after=after,
        flops=2 * rows * rank * features,
    )[0]


def rounded(x, after):
    def body(x, out):
        out[...] = x[...].astype(bf16)

    return call(body, [x], [in_vmem], [shape_of(x.shape, bf16)], after=after)[0]


def project_back(away, offered, steps, grad, after):
    rank, columns = offered[0].shape
    rows = grad.shape[0]

    def body(away, *refs):
        *offered, grad, part = refs
        step = jnp.broadcast_to(away[:1, :1], (rank, columns))
        head = offered[0][...].astype(f32)
        for at, block in zip(steps, offered[1:]):
            head = jnp.where(step == at, block[...].astype(f32), head)
        part[...] = lax.dot_general(
            head.astype(bf16), grad[...], (((1,), (1,)), ((), ())), preferred_element_type=f32
        )

    return call(
        body,
        [away, *offered, grad],
        [in_vmem] * (len(offered) + 2),
        [shape_of((rank, rows), f32)],
        after=after,
        flops=slight,
    )[0]


def head_term(lengths, lows, grad, scale, after):
    rank, rows = lows[0].shape
    columns = grad.shape[1]
    first = rows // early_part

    def body(lengths, *refs):
        *lows, grad, term, late = refs
        total = lows[0][...]
        for low in lows[1:]:
            total = total + low[...].astype(f32)
        live = lax.broadcasted_iota(jnp.int32, total.shape, 1) < lengths[0]
        total = jnp.where(live, total, 0.0)
        kept = total.astype(bf16)
        rest = (total - kept.astype(f32)).astype(bf16)
        product = jnp.dot(kept, grad[...], preferred_element_type=f32)
        product += jnp.dot(rest, grad[...], preferred_element_type=f32)
        term[0] = (scale * product).astype(bf16)
        late[...] = grad[first:, :]

    return call(
        body,
        [lengths, *lows, grad],
        [in_smem] + [in_vmem] * (len(lows) + 1),
        [shape_of((1, rank, columns), bf16), shape_of((rows - first, columns), bf16)],
        after=after,
        flops=brief,
    )


def shared_terms(lengths, parts, tokens, scale, after):
    rows, features = tokens.shape
    rank = parts[0].shape[0]
    share = rank // 4

    def body(lengths, *refs):
        parts, (tokens, back, *shares, total) = refs[:count], refs[count:]
        sub, bit = lax.axis_index("sub"), lax.rem(lax.axis_index("own"), 2)
        both = parts[0][...]
        for part in parts[1:]:
            both = both + part[...]
        live = lax.broadcasted_iota(jnp.int32, both.shape, 1) < lengths[0]
        back[...] = jnp.where(live, both, 0.0).astype(bf16)
        total[...] = scale * jnp.dot(back[...], tokens[...], preferred_element_type=f32)
        places = [(side, half) for side in (sub, 1 - sub) for half in (1 - bit, bit)]
        for (side, half), out in zip(places, shares):
            out[...] = total[pl.ds(pl.multiple_of((side * 2 + half) * share, share), share), :]

    count = len(parts)
    return call(
        body,
        [lengths, *parts, tokens],
        [in_smem] + [in_vmem] * (count + 1),
        [shape_of((rank, rows), bf16)] + [shape_of((share, features), f32)] * 4,
        after=after,
        scratch_shapes=[pltpu.VMEM((rank, features), f32)],
        flops=2 * rows * rank * features,
    )


def copied(x, after, flops):
    def body(x, out):
        out[...] = x[...]

    return call(body, [x], [in_vmem], [shape_of(x.shape, x.dtype)], after=after, flops=flops)[0]


def add_up(pieces, after=(), flops=0):
    def body(*refs):
        total = refs[0][...].astype(f32)
        for piece in refs[1:-1]:
            total = total + piece[...].astype(f32)
        refs[-1][...] = total.astype(bf16)

    return call(
        body,
        list(pieces),
        [in_vmem] * len(pieces),
        [shape_of(pieces[0].shape, bf16)],
        after=after,
        flops=flops,
    )[0]


def halve(pieces, bit, after=()):
    rows, features = pieces[0].shape
    half = rows // 2

    def body(*refs):
        total = refs[0][...].astype(f32)
        for piece in refs[1:-2]:
            total = total + piece[...].astype(f32)
        upper = lax.rem(lax.div(lax.axis_index("own"), bit), 2) == 1
        low, high = total[:half], total[half:]
        refs[-2][...] = jnp.where(upper, high, low)
        refs[-1][...] = jnp.where(upper, low, high).astype(bf16)

    return call(
        body,
        list(pieces),
        [in_vmem] * len(pieces),
        [shape_of((half, features), f32), shape_of((half, features), bf16)],
        after=after,
    )


def rejoin(mine, arrived, bit, after):
    rows, features = mine.shape

    def body(mine, arrived, out):
        upper = lax.rem(lax.div(lax.axis_index("own"), bit), 2) == 1
        one, two = mine[...].astype(f32), arrived[...].astype(f32)
        out[:rows] = jnp.where(upper, two, one).astype(bf16)
        out[rows:] = jnp.where(upper, one, two).astype(bf16)

    return call(
        body,
        [mine, arrived],
        [in_vmem] * 2,
        [shape_of((2 * rows, features), bf16)],
        after=after,
        flops=busy,
    )[0]


def lay_share(share, other, before, after):
    rows, features = share.shape
    held_in = [] if before is None else [before]

    def body(share, *refs):
        out, wide, sem = refs[len(held_in) :]
        sub = lax.axis_index("sub")
        side = 1 - sub if other else sub
        wide[...] = share[...].astype(f32)
        copy = pltpu.make_async_copy(
            wide, out.at[pl.ds(pl.multiple_of(side * rows, rows), rows)], sem
        )
        copy.start()
        copy.wait()

    return call(
        body,
        [share, *held_in],
        [in_vmem] + [in_hbm] * len(held_in),
        [shape_of((2 * rows, features), f32)],
        out_specs=[in_hbm],
        after=after,
        input_output_aliases={1: 0} if held_in else {},
        scratch_shapes=[pltpu.VMEM((rows, features), f32), pltpu.SemaphoreType.DMA],
    )[0]


def stack(pieces, after=(), flops=0):
    depths = [piece.shape[0] for piece in pieces]

    def body(*refs):
        at = 0
        for depth, piece in zip(depths, refs[:-1]):
            refs[-1][at : at + depth] = piece[...]
            at += depth

    return call(
        body,
        list(pieces),
        [in_vmem] * len(pieces),
        [shape_of((sum(depths),) + pieces[0].shape[1:], bf16)],
        after=after,
        flops=flops,
    )[0]


def clean(dims, after):
    def body(out, mark, held, sem):
        held[...] = jnp.zeros(held.shape, f32)
        mark[...] = jnp.zeros(mark.shape, f32)
        copies = [pltpu.make_async_copy(held, out.at[at], sem.at[at]) for at in range(dims[0])]
        for copy in copies:
            copy.start()
        for copy in copies:
            copy.wait()

    return call(
        body,
        [],
        [],
        [shape_of(dims, f32), shape_of((8, 128), f32)],
        out_specs=[in_hbm, in_vmem],
        after=after,
        scratch_shapes=[pltpu.VMEM(dims[1:], f32), pltpu.SemaphoreType.DMA((dims[0],))],
        flops=filling,
    )


def place_terms(adapter_ids, near, far, pattern, cleaned, after):
    per_owner, rank, columns = cleaned.shape
    sub_count = lax.axis_size("sub")

    def body(ids_far, near, far, cleaned, out, mark, held, ids, counts, sems):
        own, sub = lax.axis_index("own"), lax.axis_index("sub")
        fetch = pltpu.make_async_copy(ids_far, ids, sems.at[per_owner])
        fetch.start()
        mark[...] = jnp.zeros(mark.shape, f32)
        for local in range(per_owner):
            counts[local] = 0
        fetch.wait()
        for at, step in enumerate(pattern):
            for side in range(sub_count):
                local = ids[(own ^ step) * sub_count + side] - own * per_owner

                @pl.when(jnp.logical_and(local >= 0, local < per_owner))
                def _():
                    term = jnp.where(sub == side, near[at], far[at]).astype(f32)

                    @pl.when(counts[local] == 0)
                    def _():
                        held[local] = term

                    @pl.when(counts[local] > 0)
                    def _():
                        held[local] += term

                    counts[local] += 1

        copies = [
            pltpu.make_async_copy(held.at[local], out.at[local], sems.at[local])
            for local in range(per_owner)
        ]
        for local, copy in enumerate(copies):
            pl.when(counts[local] > 0)(copy.start)
        for local, copy in enumerate(copies):
            pl.when(counts[local] > 0)(copy.wait)

    return call(
        body,
        [stay(adapter_ids), near, far, cleaned],
        [in_hbm, in_vmem, in_vmem, in_hbm],
        [shape_of(cleaned.shape, f32), shape_of((8, 128), f32)],
        out_specs=[in_hbm, in_vmem],
        after=after,
        input_output_aliases={3: 0},
        scratch_shapes=[
            pltpu.VMEM(cleaned.shape, f32),
            pltpu.SMEM(adapter_ids.shape, jnp.int32),
            pltpu.SMEM((per_owner,), jnp.int32),
            pltpu.SemaphoreType.DMA((per_owner + 1,)),
        ],
    )


def arrange(lengths, grad, pieces, after):
    rows, columns = grad.shape
    count = 1 + len(pieces)
    first = rows // early_part

    def body(lengths, grad, *refs):
        pieces, kept = refs[:-1], refs[-1]
        at = lax.axis_index("tp")
        live = lax.broadcasted_iota(jnp.int32, (rows, columns), 0) < lengths[0]
        zero = jnp.zeros((rows, columns), bf16)
        place = pl.multiple_of(at * columns, 128)
        kept[:, pl.ds(place, columns)] = jnp.where(live, grad[...], zero)
        for step in range(1, count):
            place = pl.multiple_of(lax.rem(at + count - step, count) * columns, 128)
            early, late = pieces[2 * step - 2 : 2 * step]
            kept[:first, pl.ds(place, columns)] = jnp.where(live[:first], early[...], zero[:first])
            kept[first:, pl.ds(place, columns)] = jnp.where(live[first:], late[...], zero[first:])

    flat = [x for pair in pieces for x in pair]
    return call(
        body,
        [lengths, grad, *flat],
        [in_smem] + [in_vmem] * (1 + len(flat)),
        [shape_of((rows, count * columns), bf16)],
        after=after,
    )[0]


def input_side(kept, frozen, frozen_other, back, down, begin, count, before, after):
    rows = kept.shape[0]
    features, half = frozen.shape
    width = width_of(features)
    held_in = [] if before is None else [before]

    def body(kept, frozen, frozen_other, back, down, *refs):
        out, mark, held, sems = refs[len(held_in) :]
        mark[...] = jnp.zeros(mark.shape, f32)
        sub = lax.axis_index("sub")
        both = (((1,), (1,)), ((), ()))
        mine = kept[:, pl.ds(pl.multiple_of(sub * half, 128), half)]
        other = kept[:, pl.ds(pl.multiple_of((1 - sub) * half, 128), half)]
        twice = adapter_scale * back[...]
        copies = []
        for at in range(count):
            here = slice((begin + at) * width, (begin + at + 1) * width)
            total = lax.dot_general(mine, frozen[here, :], both, preferred_element_type=f32)
            total += lax.dot_general(other, frozen_other[here, :], both, preferred_element_type=f32)
            total += lax.dot_general(
                twice, down[:, here], (((0,), (0,)), ((), ())), preferred_element_type=f32
            )
            there = slice(at * width, (at + 1) * width)
            held[:, there] = total.astype(bf16)
            copies.append(
                pltpu.make_async_copy(held.at[:, there], out.at[:, here], sems.at[at])
            )
            copies[-1].start()
        for copy in copies:
            copy.wait()

    return call(
        body,
        [kept, frozen, frozen_other, back, down, *held_in],
        [in_vmem] * 5 + [in_hbm] * len(held_in),
        [shape_of((rows, features), bf16), shape_of((8, 128), f32)],
        out_specs=[in_hbm, in_vmem],
        after=after,
        input_output_aliases={5: 0} if held_in else {},
        scratch_shapes=[
            pltpu.VMEM((rows, count * width), bf16),
            pltpu.SemaphoreType.DMA((count,)),
        ],
        flops=2 * rows * width * count * (2 * half + back.shape[0]),
    )


def on_device(tokens, grad_output, frozen_value, shared_down, head_up, adapter_ids, lengths):
    rows, features = tokens.shape
    own_count = lax.axis_size("own")
    tp_count = lax.axis_size("tp")
    per_owner = head_up.shape[0]
    scale = adapter_scale / rows
    tp_steps, own_steps = range(1, tp_count), range(1, own_count)

    frozen_other = shift(frozen_value, "sub", 1)
    picked, early, away = pick_heads(adapter_ids, head_up, grad_output)
    steps = sorted(own_steps, key=lambda step: (-step.bit_length(), step))
    offered = [picked[0]] + [swap(picked[step], step, 0) for step in steps]
    early_grads = [shift(early, "tp", step) for step in tp_steps]

    down = shared_down.T
    low = project_low(tokens, down, picked[:1])
    sent = rounded(low, [frozen_other])
    lows = [low] + [shift(sent, "tp", step) for step in tp_steps]

    part = project_back(away, offered, steps, grad_output, [low])
    parts = [part] + [shift(part, "tp", step) for step in tp_steps]

    near, late = head_term(lengths, lows, grad_output, scale, [part, *early_grads])
    late_grads = [shift(late, "tp", step) for step in tp_steps]
    back, keep, keep_too, send, send_too = shared_terms(lengths, parts, tokens, scale, [near])
    met = stack([near], [back], flops=middling)
    terms = [near] + [swap(met if step == 1 else near, step, 0) for step in steps[::-1]]

    bits = [1 << i for i in range(own_count.bit_length() - 1)]
    leaves = add_up([keep, shift(send, "sub", 1)])
    later = copied(send_too, [leaves, terms[-1]], filling)
    pieces = [keep_too, shift(later, "sub", 1), swap(leaves, 1, 0)]
    mark = leaves
    for bit in bits[1:-1]:
        stays, leaves = halve(pieces, bit, [mark])
        pieces = [stays, swap(leaves, bit, 0)]
        mark = leaves
    cleaned, mark = clean((per_owner,) + near.shape[1:], [mark])
    near = stack(terms, [mark])
    far = shift(near, "sub", 1)
    total = add_up(pieces, [near], flops=busy)
    grad_heads, mark = place_terms(
        adapter_ids, near, far, [0] + steps[::-1], cleaned, [total]
    )
    kept = arrange(lengths, grad_output, list(zip(early_grads, late_grads)), [mark])
    sides = (frozen_value, frozen_other, back, down)
    blocks = features // width_of(features)
    cut = max(1, blocks * 2 // 5)
    input_gradient, mark = input_side(kept, *sides, 0, cut, None, [mark])
    if bits:
        total = add_up([total, swap(total, bits[-1], 0)], [mark])
    if blocks > cut:
        input_gradient, mark = input_side(
            kept, *sides, cut, blocks - cut, input_gradient, [total]
        )
    for bit in reversed(bits[:-1]):
        total = rejoin(total, swap(total, bit, 0), bit, [mark])
        mark = total
    laid = lay_share(total, False, None, [mark])
    shared_down_gradient = lay_share(shift(total, "sub", 1), True, laid, []).T
    return (input_gradient, shared_down_gradient, grad_heads)


def solution(mesh):
    placed = (
        P(("rep", "own", "sub"), "tp"),
        P(("rep", "own", "sub"), "tp"),
        P("tp", "sub"),
        P("tp", None),
        P("own", None, "tp"),
        P("rep"),
        P(("rep", "own", "sub")),
    )
    return jax.shard_map(
        on_device,
        mesh=mesh,
        in_specs=placed,
        out_specs=(
            P(("rep", "own", "sub"), "tp"),
            P(("rep", "tp"), None),
            P(("rep", "own"), None, "tp"),
        ),
        check_vma=False,
    )
```

```python
import jax
import jax.numpy as jnp
from jax import lax
from jax.experimental import pallas as pl
from jax.experimental.pallas import tpu as pltpu
from jax.sharding import PartitionSpec as P

adapter_scale = 2.0
f32 = jnp.float32
bf16 = jnp.bfloat16

early_part = 4

(busy, first_cost, middling, filling, brief, slight) = (
    10**10, 5 * 10**9, 5 * 10**9, 10**10, 3 * 10**9, 15 * 10**8
)

anywhere = pl.BlockSpec(memory_space=pl.ANY)
in_hbm = pl.BlockSpec(memory_space=pltpu.HBM)
in_vmem = pl.BlockSpec(memory_space=pltpu.VMEM)
in_smem = pl.BlockSpec(memory_space=pltpu.SMEM)


def shift(x, axis, step):
    count = lax.axis_size(axis)
    return lax.ppermute(x, axis, [(i, (i + step) % count) for i in range(count)])


def swap(x, own_bit, sub_bit):
    subs = lax.axis_size("sub")
    whole = lax.axis_size("own") * subs
    other = own_bit * subs + sub_bit
    return lax.ppermute(x, ("own", "sub"), [(i, i ^ other) for i in range(whole)])


def width_of(features):
    return next(width for width in (512, 256, 128) if features % width == 0)


def stay(x):
    return pltpu.with_memory_space_constraint(x, pltpu.HBM)


def shape_of(dims, kind):
    return jax.ShapeDtypeStruct(dims, kind)


def call(body, operands, specs, outs, out_specs=None, after=(), flops=0, **more):
    count, idle = len(operands), len(after)

    def kernel(*refs):
        body(*refs[:count], *refs[count + idle :])

    moved = sum(x.size * x.dtype.itemsize for x in list(operands) + list(outs))
    return pl.pallas_call(
        kernel,
        out_shape=outs,
        in_specs=list(specs) + [anywhere] * len(after),
        out_specs=[in_vmem] * len(outs) if out_specs is None else out_specs,
        compiler_params=pltpu.CompilerParams(vmem_limit_bytes=24 * 1024 * 1024),
        cost_estimate=pl.CostEstimate(flops=flops, bytes_accessed=moved, transcendentals=0),
        **more,
    )(*operands, *after)


def pick_heads(adapter_ids, head_up, grad):
    per_owner, rank, width = head_up.shape
    own_count, sub_count = lax.axis_size("own"), lax.axis_size("sub")
    first = grad.shape[0] // early_part

    def body(ids_far, head_up, grad, *refs):
        outs, early, away, ids, maps, sems = refs[:own_count], *refs[own_count:]
        own, sub = lax.axis_index("own"), lax.axis_index("sub")
        copies = [
            pltpu.make_async_copy(ids_far, ids, sems.at[0]),
            pltpu.make_async_copy(head_up, maps, sems.at[1]),
            pltpu.make_async_copy(grad.at[pl.ds(0, first)], early, sems.at[2]),
        ]
        for copy in copies:
            copy.start()
        copies[0].wait()
        copies[1].wait()
        for step in range(own_count):
            local = ids[(own ^ step) * sub_count + sub] - own * per_owner
            outs[step][...] = maps[jnp.clip(local, 0, per_owner - 1)]
        step = lax.div(ids[own * sub_count + sub], per_owner) ^ own
        away[...] = jnp.full(away.shape, step, jnp.int32)
        copies[2].wait()

    *picked, early, away = call(
        body,
        [stay(adapter_ids), stay(head_up), stay(grad)],
        [in_hbm] * 3,
        [shape_of((rank, width), bf16)] * own_count
        + [shape_of((first, grad.shape[1]), bf16), shape_of((8, 128), jnp.int32)],
        scratch_shapes=[
            pltpu.SMEM(adapter_ids.shape, jnp.int32),
            pltpu.VMEM(head_up.shape, bf16),
            pltpu.SemaphoreType.DMA((3,)),
        ],
        flops=first_cost,
    )
    return picked, early, away


def project_low(tokens, down, after):
    rows, features = tokens.shape
    rank = down.shape[0]

    def body(tokens, down, low):
        low[...] = lax.dot_general(
            down[...], tokens[...], (((1,), (1,)), ((), ())), preferred_element_type=f32
        )

    return call(
        body,
        [tokens, down],
        [in_vmem] * 2,
        [shape_of((rank, rows), f32)],
        after=after,
        flops=2 * rows * rank * features,
    )[0]


def rounded(x, after):
    def body(x, out):
        out[...] = x[...].astype(bf16)

    return call(body, [x], [in_vmem], [shape_of(x.shape, bf16)], after=after)[0]


def project_back(away, offered, steps, grad, after):
    rank, columns = offered[0].shape
    rows = grad.shape[0]

    def body(away, *refs):
        *offered, grad, part = refs
        step = jnp.broadcast_to(away[:1, :1], (rank, columns))
        head = offered[0][...].astype(f32)
        for at, block in zip(steps, offered[1:]):
            head = jnp.where(step == at, block[...].astype(f32), head)
        part[...] = lax.dot_general(
            head.astype(bf16), grad[...], (((1,), (1,)), ((), ())), preferred_element_type=f32
        )

    return call(
        body,
        [away, *offered, grad],
        [in_vmem] * (len(offered) + 2),
        [shape_of((rank, rows), f32)],
        after=after,
        flops=slight,
    )[0]


def head_term(lengths, lows, grad, scale, after):
    rank, rows = lows[0].shape
    columns = grad.shape[1]
    first = rows // early_part

    def body(lengths, *refs):
        *lows, grad, term, late = refs
        total = lows[0][...]
        for low in lows[1:]:
            total = total + low[...].astype(f32)
        live = lax.broadcasted_iota(jnp.int32, total.shape, 1) < lengths[0]
        total = jnp.where(live, total, 0.0)
        kept = total.astype(bf16)
        rest = (total - kept.astype(f32)).astype(bf16)
        product = jnp.dot(kept, grad[...], preferred_element_type=f32)
        product += jnp.dot(rest, grad[...], preferred_element_type=f32)
        term[0] = (scale * product).astype(bf16)
        late[...] = grad[first:, :]

    return call(
        body,
        [lengths, *lows, grad],
        [in_smem] + [in_vmem] * (len(lows) + 1),
        [shape_of((1, rank, columns), bf16), shape_of((rows - first, columns), bf16)],
        after=after,
        flops=brief,
    )


def shared_terms(lengths, parts, tokens, scale, after):
    rows, features = tokens.shape
    rank = parts[0].shape[0]
    share = rank // 2

    def body(lengths, *refs):
        parts, (tokens, back, keep, send, total) = refs[:count], refs[count:]
        sub = lax.axis_index("sub")
        both = parts[0][...]
        for part in parts[1:]:
            both = both + part[...]
        live = lax.broadcasted_iota(jnp.int32, both.shape, 1) < lengths[0]
        back[...] = jnp.where(live, both, 0.0).astype(bf16)
        total[...] = scale * jnp.dot(back[...], tokens[...], preferred_element_type=f32)
        keep[...] = total[pl.ds(pl.multiple_of(sub * share, share), share), :]
        send[...] = total[pl.ds(pl.multiple_of((1 - sub) * share, share), share), :]

    count = len(parts)
    return call(
        body,
        [lengths, *parts, tokens],
        [in_smem] + [in_vmem] * (count + 1),
        [shape_of((rank, rows), bf16)] + [shape_of((share, features), f32)] * 2,
        after=after,
        scratch_shapes=[pltpu.VMEM((rank, features), f32)],
        flops=2 * rows * rank * features,
    )


def add_up(pieces, after=(), flops=0):
    def body(*refs):
        total = refs[0][...].astype(f32)
        for piece in refs[1:-1]:
            total = total + piece[...].astype(f32)
        refs[-1][...] = total.astype(bf16)

    return call(
        body,
        list(pieces),
        [in_vmem] * len(pieces),
        [shape_of(pieces[0].shape, bf16)],
        after=after,
        flops=flops,
    )[0]


def halve(pieces, bit, after=()):
    rows, features = pieces[0].shape
    half = rows // 2

    def body(*refs):
        total = refs[0][...].astype(f32)
        for piece in refs[1:-2]:
            total = total + piece[...].astype(f32)
        upper = lax.rem(lax.div(lax.axis_index("own"), bit), 2) == 1
        low, high = total[:half], total[half:]
        refs[-2][...] = jnp.where(upper, high, low)
        refs[-1][...] = jnp.where(upper, low, high).astype(bf16)

    return call(
        body,
        list(pieces),
        [in_vmem] * len(pieces),
        [shape_of((half, features), f32), shape_of((half, features), bf16)],
        after=after,
    )


def rejoin(mine, arrived, bit, after):
    rows, features = mine.shape

    def body(mine, arrived, out):
        upper = lax.rem(lax.div(lax.axis_index("own"), bit), 2) == 1
        one, two = mine[...].astype(f32), arrived[...].astype(f32)
        out[:rows] = jnp.where(upper, two, one).astype(bf16)
        out[rows:] = jnp.where(upper, one, two).astype(bf16)

    return call(
        body,
        [mine, arrived],
        [in_vmem] * 2,
        [shape_of((2 * rows, features), bf16)],
        after=after,
        flops=busy,
    )[0]


def join_shares(mine, other, after):
    share, features = mine.shape

    def body(mine, other, out):
        sub = lax.axis_index("sub")
        for side, piece in ((sub, mine), (1 - sub, other)):
            out[pl.ds(pl.multiple_of(side * share, share), share), :] = piece[...].astype(f32)

    return call(
        body,
        [mine, other],
        [in_vmem] * 2,
        [shape_of((2 * share, features), f32)],
        after=after,
    )[0]


def stack(pieces, after=(), flops=0):
    depths = [piece.shape[0] for piece in pieces]

    def body(*refs):
        at = 0
        for depth, piece in zip(depths, refs[:-1]):
            refs[-1][at : at + depth] = piece[...]
            at += depth

    return call(
        body,
        list(pieces),
        [in_vmem] * len(pieces),
        [shape_of((sum(depths),) + pieces[0].shape[1:], bf16)],
        after=after,
        flops=flops,
    )[0]


def clean(dims, after):
    def body(out, mark, held, sem):
        held[...] = jnp.zeros(held.shape, f32)
        mark[...] = jnp.zeros(mark.shape, f32)
        copies = [pltpu.make_async_copy(held, out.at[at], sem.at[at]) for at in range(dims[0])]
        for copy in copies:
            copy.start()
        for copy in copies:
            copy.wait()

    return call(
        body,
        [],
        [],
        [shape_of(dims, f32), shape_of((8, 128), f32)],
        out_specs=[in_hbm, in_vmem],
        after=after,
        scratch_shapes=[pltpu.VMEM(dims[1:], f32), pltpu.SemaphoreType.DMA((dims[0],))],
        flops=filling,
    )


def place_terms(adapter_ids, near, far, pattern, cleaned, after):
    per_owner, rank, columns = cleaned.shape
    sub_count = lax.axis_size("sub")

    def body(ids_far, near, far, cleaned, out, mark, held, ids, counts, sems):
        own, sub = lax.axis_index("own"), lax.axis_index("sub")
        fetch = pltpu.make_async_copy(ids_far, ids, sems.at[per_owner])
        fetch.start()
        mark[...] = jnp.zeros(mark.shape, f32)
        for local in range(per_owner):
            counts[local] = 0
        fetch.wait()
        for at, step in enumerate(pattern):
            for side in range(sub_count):
                local = ids[(own ^ step) * sub_count + side] - own * per_owner

                @pl.when(jnp.logical_and(local >= 0, local < per_owner))
                def _():
                    term = jnp.where(sub == side, near[at], far[at]).astype(f32)

                    @pl.when(counts[local] == 0)
                    def _():
                        held[local] = term

                    @pl.when(counts[local] > 0)
                    def _():
                        held[local] += term

                    counts[local] += 1

        copies = [
            pltpu.make_async_copy(held.at[local], out.at[local], sems.at[local])
            for local in range(per_owner)
        ]
        for local, copy in enumerate(copies):
            pl.when(counts[local] > 0)(copy.start)
        for local, copy in enumerate(copies):
            pl.when(counts[local] > 0)(copy.wait)

    return call(
        body,
        [stay(adapter_ids), near, far, cleaned],
        [in_hbm, in_vmem, in_vmem, in_hbm],
        [shape_of(cleaned.shape, f32), shape_of((8, 128), f32)],
        out_specs=[in_hbm, in_vmem],
        after=after,
        input_output_aliases={3: 0},
        scratch_shapes=[
            pltpu.VMEM(cleaned.shape, f32),
            pltpu.SMEM(adapter_ids.shape, jnp.int32),
            pltpu.SMEM((per_owner,), jnp.int32),
            pltpu.SemaphoreType.DMA((per_owner + 1,)),
        ],
    )


def arrange(lengths, grad, pieces, after):
    rows, columns = grad.shape
    count = 1 + len(pieces)
    first = rows // early_part

    def body(lengths, grad, *refs):
        pieces, kept = refs[:-1], refs[-1]
        at = lax.axis_index("tp")
        live = lax.broadcasted_iota(jnp.int32, (rows, columns), 0) < lengths[0]
        zero = jnp.zeros((rows, columns), bf16)
        place = pl.multiple_of(at * columns, 128)
        kept[:, pl.ds(place, columns)] = jnp.where(live, grad[...], zero)
        for step in range(1, count):
            place = pl.multiple_of(lax.rem(at + count - step, count) * columns, 128)
            early, late = pieces[2 * step - 2 : 2 * step]
            kept[:first, pl.ds(place, columns)] = jnp.where(live[:first], early[...], zero[:first])
            kept[first:, pl.ds(place, columns)] = jnp.where(live[first:], late[...], zero[first:])

    flat = [x for pair in pieces for x in pair]
    return call(
        body,
        [lengths, grad, *flat],
        [in_smem] + [in_vmem] * (1 + len(flat)),
        [shape_of((rows, count * columns), bf16)],
        after=after,
    )[0]


def input_side(kept, frozen, frozen_other, back, down, begin, count, before, after):
    rows = kept.shape[0]
    features, half = frozen.shape
    width = width_of(features)
    held_in = [] if before is None else [before]

    def body(kept, frozen, frozen_other, back, down, *refs):
        out, mark, held, sems = refs[len(held_in) :]
        mark[...] = jnp.zeros(mark.shape, f32)
        sub = lax.axis_index("sub")
        both = (((1,), (1,)), ((), ()))
        mine = kept[:, pl.ds(pl.multiple_of(sub * half, 128), half)]
        other = kept[:, pl.ds(pl.multiple_of((1 - sub) * half, 128), half)]
        twice = adapter_scale * back[...]
        copies = []
        for at in range(count):
            here = slice((begin + at) * width, (begin + at + 1) * width)
            total = lax.dot_general(mine, frozen[here, :], both, preferred_element_type=f32)
            total += lax.dot_general(other, frozen_other[here, :], both, preferred_element_type=f32)
            total += lax.dot_general(
                twice, down[:, here], (((0,), (0,)), ((), ())), preferred_element_type=f32
            )
            there = slice(at * width, (at + 1) * width)
            held[:, there] = total.astype(bf16)
            copies.append(
                pltpu.make_async_copy(held.at[:, there], out.at[:, here], sems.at[at])
            )
            copies[-1].start()
        for copy in copies:
            copy.wait()

    return call(
        body,
        [kept, frozen, frozen_other, back, down, *held_in],
        [in_vmem] * 5 + [in_hbm] * len(held_in),
        [shape_of((rows, features), bf16), shape_of((8, 128), f32)],
        out_specs=[in_hbm, in_vmem],
        after=after,
        input_output_aliases={5: 0} if held_in else {},
        scratch_shapes=[
            pltpu.VMEM((rows, count * width), bf16),
            pltpu.SemaphoreType.DMA((count,)),
        ],
        flops=2 * rows * width * count * (2 * half + back.shape[0]),
    )


def on_device(tokens, grad_output, frozen_value, shared_down, head_up, adapter_ids, lengths):
    rows, features = tokens.shape
    own_count = lax.axis_size("own")
    tp_count = lax.axis_size("tp")
    per_owner = head_up.shape[0]
    scale = adapter_scale / rows
    tp_steps, own_steps = range(1, tp_count), range(1, own_count)

    frozen_other = shift(frozen_value, "sub", 1)
    picked, early, away = pick_heads(adapter_ids, head_up, grad_output)
    steps = sorted(own_steps, key=lambda step: -step)
    offered = [picked[0]] + [swap(picked[step], step, 0) for step in steps]
    early_grads = [shift(early, "tp", step) for step in tp_steps]

    down = shared_down.T
    low = project_low(tokens, down, picked[:1])
    sent = rounded(low, [frozen_other])
    lows = [low] + [shift(sent, "tp", step) for step in tp_steps]

    part = project_back(away, offered, steps, grad_output, [low])
    parts = [part] + [shift(part, "tp", step) for step in tp_steps]

    near, late = head_term(lengths, lows, grad_output, scale, [part, *early_grads])
    late_grads = [shift(late, "tp", step) for step in tp_steps]
    back, keep, send = shared_terms(lengths, parts, tokens, scale, [near])
    pieces = [keep, shift(send, "sub", 1)]
    met = stack([near], [back], flops=middling)
    terms = [near] + [swap(met if step == 1 else near, step, 0) for step in steps[::-1]]

    bits = [1 << i for i in range(own_count.bit_length() - 1)]
    mark = back
    for bit in bits[:-1]:
        stays, leaves = halve(pieces, bit, [mark])
        pieces = [stays, swap(leaves, bit, 0)]
        mark = leaves
    cleaned, mark = clean((per_owner,) + near.shape[1:], [mark])
    near = stack(terms, [mark])
    far = shift(near, "sub", 1)
    total = add_up(pieces, [near], flops=busy)
    grad_heads, mark = place_terms(
        adapter_ids, near, far, [0] + steps[::-1], cleaned, [total]
    )
    kept = arrange(lengths, grad_output, list(zip(early_grads, late_grads)), [mark])
    sides = (frozen_value, frozen_other, back, down)
    blocks = features // width_of(features)
    cut = max(1, blocks * 2 // 5)
    input_gradient, mark = input_side(kept, *sides, 0, cut, None, [mark])
    if bits:
        total = add_up([total, swap(total, bits[-1], 0)], [mark])
    if blocks > cut:
        input_gradient, mark = input_side(
            kept, *sides, cut, blocks - cut, input_gradient, [total]
        )
    for bit in reversed(bits[:-1]):
        total = rejoin(total, swap(total, bit, 0), bit, [mark])
        mark = total
    shared_down_gradient = join_shares(total, shift(total, "sub", 1), [mark]).T
    return (input_gradient, shared_down_gradient, grad_heads)


def solution(mesh):
    placed = (
        P(("rep", "own", "sub"), "tp"),
        P(("rep", "own", "sub"), "tp"),
        P("tp", "sub"),
        P("tp", None),
        P("own", None, "tp"),
        P("rep"),
        P(("rep", "own", "sub")),
    )
    return jax.shard_map(
        on_device,
        mesh=mesh,
        in_specs=placed,
        out_specs=(
            P(("rep", "own", "sub"), "tp"),
            P(("rep", "tp"), None),
            P(("rep", "own"), None, "tp"),
        ),
        check_vma=False,
    )
```

```python
import jax
import jax.numpy as jnp
from jax import lax
from jax.experimental import pallas as pl
from jax.experimental.pallas import tpu as pltpu
from jax.sharding import PartitionSpec as P

adapter_scale = 2.0
f32 = jnp.float32
bf16 = jnp.bfloat16

early_part = 4

(busy, first_cost, middling, filling, brief, slight) = (
    10**10, 5 * 10**9, 5 * 10**9, 10**10, 3 * 10**9, 15 * 10**8
)

anywhere = pl.BlockSpec(memory_space=pl.ANY)
in_hbm = pl.BlockSpec(memory_space=pltpu.HBM)
in_vmem = pl.BlockSpec(memory_space=pltpu.VMEM)
in_smem = pl.BlockSpec(memory_space=pltpu.SMEM)


def shift(x, axis, step):
    count = lax.axis_size(axis)
    return lax.ppermute(x, axis, [(i, (i + step) % count) for i in range(count)])


def swap(x, own_bit, sub_bit):
    subs = lax.axis_size("sub")
    whole = lax.axis_size("own") * subs
    other = own_bit * subs + sub_bit
    return lax.ppermute(x, ("own", "sub"), [(i, i ^ other) for i in range(whole)])


def width_of(features):
    return next(width for width in (512, 256, 128) if features % width == 0)


def stay(x):
    return pltpu.with_memory_space_constraint(x, pltpu.HBM)


def shape_of(dims, kind):
    return jax.ShapeDtypeStruct(dims, kind)


def call(body, operands, specs, outs, out_specs=None, after=(), flops=0, **more):
    count, idle = len(operands), len(after)

    def kernel(*refs):
        body(*refs[:count], *refs[count + idle :])

    moved = sum(x.size * x.dtype.itemsize for x in list(operands) + list(outs))
    return pl.pallas_call(
        kernel,
        out_shape=outs,
        in_specs=list(specs) + [anywhere] * len(after),
        out_specs=[in_vmem] * len(outs) if out_specs is None else out_specs,
        compiler_params=pltpu.CompilerParams(vmem_limit_bytes=24 * 1024 * 1024),
        cost_estimate=pl.CostEstimate(flops=flops, bytes_accessed=moved, transcendentals=0),
        **more,
    )(*operands, *after)


def pick_heads(adapter_ids, head_up, grad):
    per_owner, rank, width = head_up.shape
    own_count, sub_count = lax.axis_size("own"), lax.axis_size("sub")
    first = grad.shape[0] // early_part

    def body(ids_far, head_up, grad, *refs):
        outs, early, away, ids, maps, sems = refs[:own_count], *refs[own_count:]
        own, sub = lax.axis_index("own"), lax.axis_index("sub")
        copies = [
            pltpu.make_async_copy(ids_far, ids, sems.at[0]),
            pltpu.make_async_copy(head_up, maps, sems.at[1]),
            pltpu.make_async_copy(grad.at[pl.ds(0, first)], early, sems.at[2]),
        ]
        for copy in copies:
            copy.start()
        copies[0].wait()
        copies[1].wait()
        for step in range(own_count):
            local = ids[(own ^ step) * sub_count + sub] - own * per_owner
            outs[step][...] = maps[jnp.clip(local, 0, per_owner - 1)]
        step = lax.div(ids[own * sub_count + sub], per_owner) ^ own
        away[...] = jnp.full(away.shape, step, jnp.int32)
        copies[2].wait()

    *picked, early, away = call(
        body,
        [stay(adapter_ids), stay(head_up), stay(grad)],
        [in_hbm] * 3,
        [shape_of((rank, width), bf16)] * own_count
        + [shape_of((first, grad.shape[1]), bf16), shape_of((8, 128), jnp.int32)],
        scratch_shapes=[
            pltpu.SMEM(adapter_ids.shape, jnp.int32),
            pltpu.VMEM(head_up.shape, bf16),
            pltpu.SemaphoreType.DMA((3,)),
        ],
        flops=first_cost,
    )
    return picked, early, away


def project_low(tokens, down, after):
    rows, features = tokens.shape
    rank = down.shape[0]

    def body(tokens, down, low):
        low[...] = lax.dot_general(
            down[...], tokens[...], (((1,), (1,)), ((), ())), preferred_element_type=f32
        )

    return call(
        body,
        [tokens, down],
        [in_vmem] * 2,
        [shape_of((rank, rows), f32)],
        after=after,
        flops=2 * rows * rank * features,
    )[0]


def rounded(x, after):
    def body(x, out):
        out[...] = x[...].astype(bf16)

    return call(body, [x], [in_vmem], [shape_of(x.shape, bf16)], after=after)[0]


def project_back(away, offered, steps, grad, after):
    rank, columns = offered[0].shape
    rows = grad.shape[0]

    def body(away, *refs):
        *offered, grad, part = refs
        step = jnp.broadcast_to(away[:1, :1], (rank, columns))
        head = offered[0][...].astype(f32)
        for at, block in zip(steps, offered[1:]):
            head = jnp.where(step == at, block[...].astype(f32), head)
        part[...] = lax.dot_general(
            head.astype(bf16), grad[...], (((1,), (1,)), ((), ())), preferred_element_type=f32
        )

    return call(
        body,
        [away, *offered, grad],
        [in_vmem] * (len(offered) + 2),
        [shape_of((rank, rows), f32)],
        after=after,
        flops=slight,
    )[0]


def head_term(lengths, lows, grad, scale, after):
    rank, rows = lows[0].shape
    columns = grad.shape[1]
    first = rows // early_part

    def body(lengths, *refs):
        *lows, grad, term, late = refs
        total = lows[0][...]
        for low in lows[1:]:
            total = total + low[...].astype(f32)
        live = lax.broadcasted_iota(jnp.int32, total.shape, 1) < lengths[0]
        total = jnp.where(live, total, 0.0)
        kept = total.astype(bf16)
        rest = (total - kept.astype(f32)).astype(bf16)
        product = jnp.dot(kept, grad[...], preferred_element_type=f32)
        product += jnp.dot(rest, grad[...], preferred_element_type=f32)
        term[0] = (scale * product).astype(bf16)
        late[...] = grad[first:, :]

    return call(
        body,
        [lengths, *lows, grad],
        [in_smem] + [in_vmem] * (len(lows) + 1),
        [shape_of((1, rank, columns), bf16), shape_of((rows - first, columns), bf16)],
        after=after,
        flops=brief,
    )


def shared_terms(lengths, parts, tokens, scale, after):
    rows, features = tokens.shape
    rank = parts[0].shape[0]
    share = rank // 2

    def body(lengths, *refs):
        parts, (tokens, back, keep, send, total) = refs[:count], refs[count:]
        sub = lax.axis_index("sub")
        both = parts[0][...]
        for part in parts[1:]:
            both = both + part[...]
        live = lax.broadcasted_iota(jnp.int32, both.shape, 1) < lengths[0]
        back[...] = jnp.where(live, both, 0.0).astype(bf16)
        total[...] = scale * jnp.dot(back[...], tokens[...], preferred_element_type=f32)
        keep[...] = total[pl.ds(pl.multiple_of(sub * share, share), share), :]
        send[...] = total[pl.ds(pl.multiple_of((1 - sub) * share, share), share), :]

    count = len(parts)
    return call(
        body,
        [lengths, *parts, tokens],
        [in_smem] + [in_vmem] * (count + 1),
        [shape_of((rank, rows), bf16)] + [shape_of((share, features), f32)] * 2,
        after=after,
        scratch_shapes=[pltpu.VMEM((rank, features), f32)],
        flops=2 * rows * rank * features,
    )


def add_up(pieces, after=(), flops=0):
    def body(*refs):
        total = refs[0][...].astype(f32)
        for piece in refs[1:-1]:
            total = total + piece[...].astype(f32)
        refs[-1][...] = total.astype(bf16)

    return call(
        body,
        list(pieces),
        [in_vmem] * len(pieces),
        [shape_of(pieces[0].shape, bf16)],
        after=after,
        flops=flops,
    )[0]


def halve(pieces, bit, after=()):
    rows, features = pieces[0].shape
    half = rows // 2

    def body(*refs):
        total = refs[0][...].astype(f32)
        for piece in refs[1:-2]:
            total = total + piece[...].astype(f32)
        upper = lax.rem(lax.div(lax.axis_index("own"), bit), 2) == 1
        low, high = total[:half], total[half:]
        refs[-2][...] = jnp.where(upper, high, low)
        refs[-1][...] = jnp.where(upper, low, high).astype(bf16)

    return call(
        body,
        list(pieces),
        [in_vmem] * len(pieces),
        [shape_of((half, features), f32), shape_of((half, features), bf16)],
        after=after,
    )


def rejoin(mine, arrived, bit, after):
    rows, features = mine.shape

    def body(mine, arrived, out):
        upper = lax.rem(lax.div(lax.axis_index("own"), bit), 2) == 1
        one, two = mine[...].astype(f32), arrived[...].astype(f32)
        out[:rows] = jnp.where(upper, two, one).astype(bf16)
        out[rows:] = jnp.where(upper, one, two).astype(bf16)

    return call(
        body,
        [mine, arrived],
        [in_vmem] * 2,
        [shape_of((2 * rows, features), bf16)],
        after=after,
        flops=busy,
    )[0]


def join_shares(mine, other, after):
    share, features = mine.shape

    def body(mine, other, out):
        sub = lax.axis_index("sub")
        for side, piece in ((sub, mine), (1 - sub, other)):
            out[pl.ds(pl.multiple_of(side * share, share), share), :] = piece[...].astype(f32)

    return call(
        body,
        [mine, other],
        [in_vmem] * 2,
        [shape_of((2 * share, features), f32)],
        after=after,
    )[0]


def stack(pieces, after=(), flops=0):
    depths = [piece.shape[0] for piece in pieces]

    def body(*refs):
        at = 0
        for depth, piece in zip(depths, refs[:-1]):
            refs[-1][at : at + depth] = piece[...]
            at += depth

    return call(
        body,
        list(pieces),
        [in_vmem] * len(pieces),
        [shape_of((sum(depths),) + pieces[0].shape[1:], bf16)],
        after=after,
        flops=flops,
    )[0]


def clean(dims, after):
    def body(out, mark, held, sem):
        held[...] = jnp.zeros(held.shape, f32)
        mark[...] = jnp.zeros(mark.shape, f32)
        copies = [pltpu.make_async_copy(held, out.at[at], sem.at[at]) for at in range(dims[0])]
        for copy in copies:
            copy.start()
        for copy in copies:
            copy.wait()

    return call(
        body,
        [],
        [],
        [shape_of(dims, f32), shape_of((8, 128), f32)],
        out_specs=[in_hbm, in_vmem],
        after=after,
        scratch_shapes=[pltpu.VMEM(dims[1:], f32), pltpu.SemaphoreType.DMA((dims[0],))],
        flops=filling,
    )


def place_terms(adapter_ids, near, far, pattern, cleaned, after):
    per_owner, rank, columns = cleaned.shape
    sub_count = lax.axis_size("sub")

    def body(ids_far, near, far, cleaned, out, mark, held, ids, counts, sems):
        own, sub = lax.axis_index("own"), lax.axis_index("sub")
        fetch = pltpu.make_async_copy(ids_far, ids, sems.at[per_owner])
        fetch.start()
        mark[...] = jnp.zeros(mark.shape, f32)
        for local in range(per_owner):
            counts[local] = 0
        fetch.wait()
        for at, step in enumerate(pattern):
            for side in range(sub_count):
                local = ids[(own ^ step) * sub_count + side] - own * per_owner

                @pl.when(jnp.logical_and(local >= 0, local < per_owner))
                def _():
                    term = jnp.where(sub == side, near[at], far[at]).astype(f32)

                    @pl.when(counts[local] == 0)
                    def _():
                        held[local] = term

                    @pl.when(counts[local] > 0)
                    def _():
                        held[local] += term

                    counts[local] += 1

        copies = [
            pltpu.make_async_copy(held.at[local], out.at[local], sems.at[local])
            for local in range(per_owner)
        ]
        for local, copy in enumerate(copies):
            pl.when(counts[local] > 0)(copy.start)
        for local, copy in enumerate(copies):
            pl.when(counts[local] > 0)(copy.wait)

    return call(
        body,
        [stay(adapter_ids), near, far, cleaned],
        [in_hbm, in_vmem, in_vmem, in_hbm],
        [shape_of(cleaned.shape, f32), shape_of((8, 128), f32)],
        out_specs=[in_hbm, in_vmem],
        after=after,
        input_output_aliases={3: 0},
        scratch_shapes=[
            pltpu.VMEM(cleaned.shape, f32),
            pltpu.SMEM(adapter_ids.shape, jnp.int32),
            pltpu.SMEM((per_owner,), jnp.int32),
            pltpu.SemaphoreType.DMA((per_owner + 1,)),
        ],
    )


def arrange(lengths, grad, pieces, after):
    rows, columns = grad.shape
    count = 1 + len(pieces)
    first = rows // early_part

    def body(lengths, grad, *refs):
        pieces, kept = refs[:-1], refs[-1]
        at = lax.axis_index("tp")
        live = lax.broadcasted_iota(jnp.int32, (rows, columns), 0) < lengths[0]
        zero = jnp.zeros((rows, columns), bf16)
        place = pl.multiple_of(at * columns, 128)
        kept[:, pl.ds(place, columns)] = jnp.where(live, grad[...], zero)
        for step in range(1, count):
            place = pl.multiple_of(lax.rem(at + count - step, count) * columns, 128)
            early, late = pieces[2 * step - 2 : 2 * step]
            kept[:first, pl.ds(place, columns)] = jnp.where(live[:first], early[...], zero[:first])
            kept[first:, pl.ds(place, columns)] = jnp.where(live[first:], late[...], zero[first:])

    flat = [x for pair in pieces for x in pair]
    return call(
        body,
        [lengths, grad, *flat],
        [in_smem] + [in_vmem] * (1 + len(flat)),
        [shape_of((rows, count * columns), bf16)],
        after=after,
    )[0]


def input_side(kept, frozen, frozen_other, back, down, begin, count, before, after):
    rows = kept.shape[0]
    features, half = frozen.shape
    width = width_of(features)
    held_in = [] if before is None else [before]

    def body(kept, frozen, frozen_other, back, down, *refs):
        out, mark, held, sems = refs[len(held_in) :]
        mark[...] = jnp.zeros(mark.shape, f32)
        sub = lax.axis_index("sub")
        both = (((1,), (1,)), ((), ()))
        mine = kept[:, pl.ds(pl.multiple_of(sub * half, 128), half)]
        other = kept[:, pl.ds(pl.multiple_of((1 - sub) * half, 128), half)]
        twice = adapter_scale * back[...]
        copies = []
        for at in range(count):
            here = slice((begin + at) * width, (begin + at + 1) * width)
            total = lax.dot_general(mine, frozen[here, :], both, preferred_element_type=f32)
            total += lax.dot_general(other, frozen_other[here, :], both, preferred_element_type=f32)
            total += lax.dot_general(
                twice, down[:, here], (((0,), (0,)), ((), ())), preferred_element_type=f32
            )
            there = slice(at * width, (at + 1) * width)
            held[:, there] = total.astype(bf16)
            copies.append(
                pltpu.make_async_copy(held.at[:, there], out.at[:, here], sems.at[at])
            )
            copies[-1].start()
        for copy in copies:
            copy.wait()

    return call(
        body,
        [kept, frozen, frozen_other, back, down, *held_in],
        [in_vmem] * 5 + [in_hbm] * len(held_in),
        [shape_of((rows, features), bf16), shape_of((8, 128), f32)],
        out_specs=[in_hbm, in_vmem],
        after=after,
        input_output_aliases={5: 0} if held_in else {},
        scratch_shapes=[
            pltpu.VMEM((rows, count * width), bf16),
            pltpu.SemaphoreType.DMA((count,)),
        ],
        flops=2 * rows * width * count * (2 * half + back.shape[0]),
    )


def on_device(tokens, grad_output, frozen_value, shared_down, head_up, adapter_ids, lengths):
    rows, features = tokens.shape
    own_count = lax.axis_size("own")
    tp_count = lax.axis_size("tp")
    per_owner = head_up.shape[0]
    scale = adapter_scale / rows
    tp_steps, own_steps = range(1, tp_count), range(1, own_count)

    frozen_other = shift(frozen_value, "sub", 1)
    picked, early, away = pick_heads(adapter_ids, head_up, grad_output)
    steps = sorted(own_steps, key=lambda step: (-step.bit_length(), step))
    offered = [picked[0]] + [swap(picked[step], step, 0) for step in steps]
    early_grads = [shift(early, "tp", step) for step in tp_steps]

    down = shared_down.T
    low = project_low(tokens, down, picked[:1])
    sent = rounded(low, [frozen_other])
    lows = [low] + [shift(sent, "tp", step) for step in tp_steps]

    part = project_back(away, offered, steps, grad_output, [low])
    parts = [part] + [shift(part, "tp", step) for step in tp_steps]

    near, late = head_term(lengths, lows, grad_output, scale, [part, *early_grads])
    late_grads = [shift(late, "tp", step) for step in tp_steps]
    back, keep, send = shared_terms(lengths, parts, tokens, scale, [near])
    pieces = [keep, shift(send, "sub", 1)]
    met = stack([near], [back], flops=middling)
    terms = [near] + [swap(met if step == own_count - 1 else near, step, 0) for step in steps[::-1]]

    bits = [1 << i for i in range(own_count.bit_length() - 1)]
    mark = back
    for bit in bits[:-1]:
        stays, leaves = halve(pieces, bit, [mark])
        pieces = [stays, swap(leaves, bit, 0)]
        mark = leaves
    cleaned, mark = clean((per_owner,) + near.shape[1:], [mark])
    near = stack(terms, [mark])
    far = shift(near, "sub", 1)
    total = add_up(pieces, [near], flops=busy)
    grad_heads, mark = place_terms(
        adapter_ids, near, far, [0] + steps[::-1], cleaned, [total]
    )
    kept = arrange(lengths, grad_output, list(zip(early_grads, late_grads)), [mark])
    sides = (frozen_value, frozen_other, back, down)
    blocks = features // width_of(features)
    cut = max(1, blocks * 2 // 5)
    input_gradient, mark = input_side(kept, *sides, 0, cut, None, [mark])
    if bits:
        total = add_up([total, swap(total, bits[-1], 0)], [mark])
    if blocks > cut:
        input_gradient, mark = input_side(
            kept, *sides, cut, blocks - cut, input_gradient, [total]
        )
    for bit in reversed(bits[:-1]):
        total = rejoin(total, swap(total, bit, 0), bit, [mark])
        mark = total
    shared_down_gradient = join_shares(total, shift(total, "sub", 1), [mark]).T
    return (input_gradient, shared_down_gradient, grad_heads)


def solution(mesh):
    placed = (
        P(("rep", "own", "sub"), "tp"),
        P(("rep", "own", "sub"), "tp"),
        P("tp", "sub"),
        P("tp", None),
        P("own", None, "tp"),
        P("rep"),
        P(("rep", "own", "sub")),
    )
    return jax.shard_map(
        on_device,
        mesh=mesh,
        in_specs=placed,
        out_specs=(
            P(("rep", "own", "sub"), "tp"),
            P(("rep", "tp"), None),
            P(("rep", "own"), None, "tp"),
        ),
        check_vma=False,
    )
```

```python
import jax
import jax.numpy as jnp
from jax import lax
from jax.experimental import pallas as pl
from jax.experimental.pallas import tpu as pltpu
from jax.sharding import PartitionSpec as P

adapter_scale = 2.0
f32 = jnp.float32
bf16 = jnp.bfloat16

early_part = 3

(busy, first_cost, middling, filling, brief, slight) = (
    10**10, 5 * 10**9, 5 * 10**9, 10**10, 3 * 10**9, 15 * 10**8
)

anywhere = pl.BlockSpec(memory_space=pl.ANY)
in_hbm = pl.BlockSpec(memory_space=pltpu.HBM)
in_vmem = pl.BlockSpec(memory_space=pltpu.VMEM)
in_smem = pl.BlockSpec(memory_space=pltpu.SMEM)


def shift(x, axis, step):
    count = lax.axis_size(axis)
    return lax.ppermute(x, axis, [(i, (i + step) % count) for i in range(count)])


def swap(x, own_bit, sub_bit):
    subs = lax.axis_size("sub")
    whole = lax.axis_size("own") * subs
    other = own_bit * subs + sub_bit
    return lax.ppermute(x, ("own", "sub"), [(i, i ^ other) for i in range(whole)])


def width_of(features):
    return next(width for width in (512, 256, 128) if features % width == 0)


def stay(x):
    return pltpu.with_memory_space_constraint(x, pltpu.HBM)


def shape_of(dims, kind):
    return jax.ShapeDtypeStruct(dims, kind)


def call(body, operands, specs, outs, out_specs=None, after=(), flops=0, **more):
    count, idle = len(operands), len(after)

    def kernel(*refs):
        body(*refs[:count], *refs[count + idle :])

    moved = sum(x.size * x.dtype.itemsize for x in list(operands) + list(outs))
    return pl.pallas_call(
        kernel,
        out_shape=outs,
        in_specs=list(specs) + [anywhere] * len(after),
        out_specs=[in_vmem] * len(outs) if out_specs is None else out_specs,
        compiler_params=pltpu.CompilerParams(vmem_limit_bytes=24 * 1024 * 1024),
        cost_estimate=pl.CostEstimate(flops=flops, bytes_accessed=moved, transcendentals=0),
        **more,
    )(*operands, *after)


def pick_heads(adapter_ids, head_up, grad):
    per_owner, rank, width = head_up.shape
    own_count, sub_count = lax.axis_size("own"), lax.axis_size("sub")
    first = grad.shape[0] * early_part // 16

    def body(ids_far, head_up, grad, *refs):
        outs, early, away, ids, maps, sems = refs[:own_count], *refs[own_count:]
        own, sub = lax.axis_index("own"), lax.axis_index("sub")
        copies = [
            pltpu.make_async_copy(ids_far, ids, sems.at[0]),
            pltpu.make_async_copy(head_up, maps, sems.at[1]),
            pltpu.make_async_copy(grad.at[pl.ds(0, first)], early, sems.at[2]),
        ]
        for copy in copies:
            copy.start()
        copies[0].wait()
        copies[1].wait()
        for step in range(own_count):
            local = ids[(own ^ step) * sub_count + sub] - own * per_owner
            outs[step][...] = maps[jnp.clip(local, 0, per_owner - 1)]
        step = lax.div(ids[own * sub_count + sub], per_owner) ^ own
        away[...] = jnp.full(away.shape, step, jnp.int32)
        copies[2].wait()

    *picked, early, away = call(
        body,
        [stay(adapter_ids), stay(head_up), stay(grad)],
        [in_hbm] * 3,
        [shape_of((rank, width), bf16)] * own_count
        + [shape_of((first, grad.shape[1]), bf16), shape_of((8, 128), jnp.int32)],
        scratch_shapes=[
            pltpu.SMEM(adapter_ids.shape, jnp.int32),
            pltpu.VMEM(head_up.shape, bf16),
            pltpu.SemaphoreType.DMA((3,)),
        ],
        flops=first_cost,
    )
    return picked, early, away


def project_low(tokens, down, after):
    rows, features = tokens.shape
    rank = down.shape[0]

    def body(tokens, down, low):
        low[...] = lax.dot_general(
            down[...], tokens[...], (((1,), (1,)), ((), ())), preferred_element_type=f32
        )

    return call(
        body,
        [tokens, down],
        [in_vmem] * 2,
        [shape_of((rank, rows), f32)],
        after=after,
        flops=2 * rows * rank * features,
    )[0]


def rounded(x, after):
    def body(x, out):
        out[...] = x[...].astype(bf16)

    return call(body, [x], [in_vmem], [shape_of(x.shape, bf16)], after=after)[0]


def project_back(away, offered, steps, grad, after):
    rank, columns = offered[0].shape
    rows = grad.shape[0]

    def body(away, *refs):
        *offered, grad, part = refs
        step = jnp.broadcast_to(away[:1, :1], (rank, columns))
        head = offered[0][...].astype(f32)
        for at, block in zip(steps, offered[1:]):
            head = jnp.where(step == at, block[...].astype(f32), head)
        part[...] = lax.dot_general(
            head.astype(bf16), grad[...], (((1,), (1,)), ((), ())), preferred_element_type=f32
        )

    return call(
        body,
        [away, *offered, grad],
        [in_vmem] * (len(offered) + 2),
        [shape_of((rank, rows), f32)],
        after=after,
        flops=slight,
    )[0]


def head_term(lengths, lows, grad, scale, after):
    rank, rows = lows[0].shape
    columns = grad.shape[1]
    first = rows * early_part // 16

    def body(lengths, *refs):
        *lows, grad, term, late = refs
        total = lows[0][...]
        for low in lows[1:]:
            total = total + low[...].astype(f32)
        live = lax.broadcasted_iota(jnp.int32, total.shape, 1) < lengths[0]
        total = jnp.where(live, total, 0.0)
        kept = total.astype(bf16)
        rest = (total - kept.astype(f32)).astype(bf16)
        product = jnp.dot(kept, grad[...], preferred_element_type=f32)
        product += jnp.dot(rest, grad[...], preferred_element_type=f32)
        term[0] = (scale * product).astype(bf16)
        late[...] = grad[first:, :]

    return call(
        body,
        [lengths, *lows, grad],
        [in_smem] + [in_vmem] * (len(lows) + 1),
        [shape_of((1, rank, columns), bf16), shape_of((rows - first, columns), bf16)],
        after=after,
        flops=brief,
    )


def shared_terms(lengths, parts, tokens, scale, after):
    rows, features = tokens.shape
    rank = parts[0].shape[0]
    share = rank // 2

    def body(lengths, *refs):
        parts, (tokens, back, keep, send, total) = refs[:count], refs[count:]
        sub = lax.axis_index("sub")
        both = parts[0][...]
        for part in parts[1:]:
            both = both + part[...]
        live = lax.broadcasted_iota(jnp.int32, both.shape, 1) < lengths[0]
        back[...] = jnp.where(live, both, 0.0).astype(bf16)
        total[...] = scale * jnp.dot(back[...], tokens[...], preferred_element_type=f32)
        keep[...] = total[pl.ds(pl.multiple_of(sub * share, share), share), :]
        send[...] = total[pl.ds(pl.multiple_of((1 - sub) * share, share), share), :]

    count = len(parts)
    return call(
        body,
        [lengths, *parts, tokens],
        [in_smem] + [in_vmem] * (count + 1),
        [shape_of((rank, rows), bf16)] + [shape_of((share, features), f32)] * 2,
        after=after,
        scratch_shapes=[pltpu.VMEM((rank, features), f32)],
        flops=2 * rows * rank * features,
    )


def add_up(pieces, after=(), flops=0):
    def body(*refs):
        total = refs[0][...].astype(f32)
        for piece in refs[1:-1]:
            total = total + piece[...].astype(f32)
        refs[-1][...] = total.astype(bf16)

    return call(
        body,
        list(pieces),
        [in_vmem] * len(pieces),
        [shape_of(pieces[0].shape, bf16)],
        after=after,
        flops=flops,
    )[0]


def halve(pieces, bit, after=()):
    rows, features = pieces[0].shape
    half = rows // 2

    def body(*refs):
        total = refs[0][...].astype(f32)
        for piece in refs[1:-2]:
            total = total + piece[...].astype(f32)
        upper = lax.rem(lax.div(lax.axis_index("own"), bit), 2) == 1
        low, high = total[:half], total[half:]
        refs[-2][...] = jnp.where(upper, high, low)
        refs[-1][...] = jnp.where(upper, low, high).astype(bf16)

    return call(
        body,
        list(pieces),
        [in_vmem] * len(pieces),
        [shape_of((half, features), f32), shape_of((half, features), bf16)],
        after=after,
    )


def rejoin(mine, arrived, bit, after):
    rows, features = mine.shape

    def body(mine, arrived, out):
        upper = lax.rem(lax.div(lax.axis_index("own"), bit), 2) == 1
        one, two = mine[...].astype(f32), arrived[...].astype(f32)
        out[:rows] = jnp.where(upper, two, one).astype(bf16)
        out[rows:] = jnp.where(upper, one, two).astype(bf16)

    return call(
        body,
        [mine, arrived],
        [in_vmem] * 2,
        [shape_of((2 * rows, features), bf16)],
        after=after,
        flops=busy,
    )[0]


def join_shares(mine, other, after):
    share, features = mine.shape

    def body(mine, other, out):
        sub = lax.axis_index("sub")
        for side, piece in ((sub, mine), (1 - sub, other)):
            out[pl.ds(pl.multiple_of(side * share, share), share), :] = piece[...].astype(f32)

    return call(
        body,
        [mine, other],
        [in_vmem] * 2,
        [shape_of((2 * share, features), f32)],
        after=after,
    )[0]


def stack(pieces, after=(), flops=0):
    depths = [piece.shape[0] for piece in pieces]

    def body(*refs):
        at = 0
        for depth, piece in zip(depths, refs[:-1]):
            refs[-1][at : at + depth] = piece[...]
            at += depth

    return call(
        body,
        list(pieces),
        [in_vmem] * len(pieces),
        [shape_of((sum(depths),) + pieces[0].shape[1:], bf16)],
        after=after,
        flops=flops,
    )[0]


def clean(dims, after):
    def body(out, mark, held, sem):
        held[...] = jnp.zeros(held.shape, f32)
        mark[...] = jnp.zeros(mark.shape, f32)
        copies = [pltpu.make_async_copy(held, out.at[at], sem.at[at]) for at in range(dims[0])]
        for copy in copies:
            copy.start()
        for copy in copies:
            copy.wait()

    return call(
        body,
        [],
        [],
        [shape_of(dims, f32), shape_of((8, 128), f32)],
        out_specs=[in_hbm, in_vmem],
        after=after,
        scratch_shapes=[pltpu.VMEM(dims[1:], f32), pltpu.SemaphoreType.DMA((dims[0],))],
        flops=filling,
    )


def place_terms(adapter_ids, near, far, pattern, cleaned, after):
    per_owner, rank, columns = cleaned.shape
    sub_count = lax.axis_size("sub")

    def body(ids_far, near, far, cleaned, out, mark, held, ids, counts, sems):
        own, sub = lax.axis_index("own"), lax.axis_index("sub")
        fetch = pltpu.make_async_copy(ids_far, ids, sems.at[per_owner])
        fetch.start()
        mark[...] = jnp.zeros(mark.shape, f32)
        for local in range(per_owner):
            counts[local] = 0
        fetch.wait()
        for at, step in enumerate(pattern):
            for side in range(sub_count):
                local = ids[(own ^ step) * sub_count + side] - own * per_owner

                @pl.when(jnp.logical_and(local >= 0, local < per_owner))
                def _():
                    term = jnp.where(sub == side, near[at], far[at]).astype(f32)

                    @pl.when(counts[local] == 0)
                    def _():
                        held[local] = term

                    @pl.when(counts[local] > 0)
                    def _():
                        held[local] += term

                    counts[local] += 1

        copies = [
            pltpu.make_async_copy(held.at[local], out.at[local], sems.at[local])
            for local in range(per_owner)
        ]
        for local, copy in enumerate(copies):
            pl.when(counts[local] > 0)(copy.start)
        for local, copy in enumerate(copies):
            pl.when(counts[local] > 0)(copy.wait)

    return call(
        body,
        [stay(adapter_ids), near, far, cleaned],
        [in_hbm, in_vmem, in_vmem, in_hbm],
        [shape_of(cleaned.shape, f32), shape_of((8, 128), f32)],
        out_specs=[in_hbm, in_vmem],
        after=after,
        input_output_aliases={3: 0},
        scratch_shapes=[
            pltpu.VMEM(cleaned.shape, f32),
            pltpu.SMEM(adapter_ids.shape, jnp.int32),
            pltpu.SMEM((per_owner,), jnp.int32),
            pltpu.SemaphoreType.DMA((per_owner + 1,)),
        ],
    )


def arrange(lengths, grad, pieces, after):
    rows, columns = grad.shape
    count = 1 + len(pieces)
    first = rows * early_part // 16

    def body(lengths, grad, *refs):
        pieces, kept = refs[:-1], refs[-1]
        at = lax.axis_index("tp")
        live = lax.broadcasted_iota(jnp.int32, (rows, columns), 0) < lengths[0]
        zero = jnp.zeros((rows, columns), bf16)
        place = pl.multiple_of(at * columns, 128)
        kept[:, pl.ds(place, columns)] = jnp.where(live, grad[...], zero)
        for step in range(1, count):
            place = pl.multiple_of(lax.rem(at + count - step, count) * columns, 128)
            early, late = pieces[2 * step - 2 : 2 * step]
            kept[:first, pl.ds(place, columns)] = jnp.where(live[:first], early[...], zero[:first])
            kept[first:, pl.ds(place, columns)] = jnp.where(live[first:], late[...], zero[first:])

    flat = [x for pair in pieces for x in pair]
    return call(
        body,
        [lengths, grad, *flat],
        [in_smem] + [in_vmem] * (1 + len(flat)),
        [shape_of((rows, count * columns), bf16)],
        after=after,
    )[0]


def input_side(kept, frozen, frozen_other, back, down, begin, count, before, after):
    rows = kept.shape[0]
    features, half = frozen.shape
    width = width_of(features)
    held_in = [] if before is None else [before]

    def body(kept, frozen, frozen_other, back, down, *refs):
        out, mark, held, sems = refs[len(held_in) :]
        mark[...] = jnp.zeros(mark.shape, f32)
        sub = lax.axis_index("sub")
        both = (((1,), (1,)), ((), ()))
        mine = kept[:, pl.ds(pl.multiple_of(sub * half, 128), half)]
        other = kept[:, pl.ds(pl.multiple_of((1 - sub) * half, 128), half)]
        twice = adapter_scale * back[...]
        copies = []
        for at in range(count):
            here = slice((begin + at) * width, (begin + at + 1) * width)
            total = lax.dot_general(mine, frozen[here, :], both, preferred_element_type=f32)
            total += lax.dot_general(other, frozen_other[here, :], both, preferred_element_type=f32)
            total += lax.dot_general(
                twice, down[:, here], (((0,), (0,)), ((), ())), preferred_element_type=f32
            )
            there = slice(at * width, (at + 1) * width)
            held[:, there] = total.astype(bf16)
            copies.append(
                pltpu.make_async_copy(held.at[:, there], out.at[:, here], sems.at[at])
            )
            copies[-1].start()
        for copy in copies:
            copy.wait()

    return call(
        body,
        [kept, frozen, frozen_other, back, down, *held_in],
        [in_vmem] * 5 + [in_hbm] * len(held_in),
        [shape_of((rows, features), bf16), shape_of((8, 128), f32)],
        out_specs=[in_hbm, in_vmem],
        after=after,
        input_output_aliases={5: 0} if held_in else {},
        scratch_shapes=[
            pltpu.VMEM((rows, count * width), bf16),
            pltpu.SemaphoreType.DMA((count,)),
        ],
        flops=2 * rows * width * count * (2 * half + back.shape[0]),
    )


def on_device(tokens, grad_output, frozen_value, shared_down, head_up, adapter_ids, lengths):
    rows, features = tokens.shape
    own_count = lax.axis_size("own")
    tp_count = lax.axis_size("tp")
    per_owner = head_up.shape[0]
    scale = adapter_scale / rows
    tp_steps, own_steps = range(1, tp_count), range(1, own_count)

    frozen_other = shift(frozen_value, "sub", 1)
    picked, early, away = pick_heads(adapter_ids, head_up, grad_output)
    steps = sorted(own_steps, key=lambda step: (-step.bit_length(), step))
    offered = [picked[0]] + [swap(picked[step], step, 0) for step in steps]
    early_grads = [shift(early, "tp", step) for step in tp_steps]

    down = shared_down.T
    low = project_low(tokens, down, picked[:1])
    sent = rounded(low, [frozen_other])
    lows = [low] + [shift(sent, "tp", step) for step in tp_steps]

    part = project_back(away, offered, steps, grad_output, [low])
    parts = [part] + [shift(part, "tp", step) for step in tp_steps]

    near, late = head_term(lengths, lows, grad_output, scale, [part, *early_grads])
    late_grads = [shift(late, "tp", step) for step in tp_steps]
    back, keep, send = shared_terms(lengths, parts, tokens, scale, [near])
    pieces = [keep, shift(send, "sub", 1)]
    met = stack([near], [back], flops=middling)
    terms = [near] + [swap(met if step == 1 else near, step, 0) for step in steps[::-1]]

    bits = [1 << i for i in range(own_count.bit_length() - 1)]
    mark = back
    for bit in bits[:-1]:
        stays, leaves = halve(pieces, bit, [mark])
        pieces = [stays, swap(leaves, bit, 0)]
        mark = leaves
    cleaned, mark = clean((per_owner,) + near.shape[1:], [mark])
    near = stack(terms, [mark])
    far = shift(near, "sub", 1)
    total = add_up(pieces, [near], flops=busy)
    grad_heads, mark = place_terms(
        adapter_ids, near, far, [0] + steps[::-1], cleaned, [total]
    )
    kept = arrange(lengths, grad_output, list(zip(early_grads, late_grads)), [mark])
    sides = (frozen_value, frozen_other, back, down)
    blocks = features // width_of(features)
    cut = max(1, blocks * 2 // 5)
    input_gradient, mark = input_side(kept, *sides, 0, cut, None, [mark])
    if bits:
        total = add_up([total, swap(total, bits[-1], 0)], [mark])
    if blocks > cut:
        input_gradient, mark = input_side(
            kept, *sides, cut, blocks - cut, input_gradient, [total]
        )
    for bit in reversed(bits[:-1]):
        total = rejoin(total, swap(total, bit, 0), bit, [mark])
        mark = total
    shared_down_gradient = join_shares(total, shift(total, "sub", 1), [mark]).T
    return (input_gradient, shared_down_gradient, grad_heads)


def solution(mesh):
    placed = (
        P(("rep", "own", "sub"), "tp"),
        P(("rep", "own", "sub"), "tp"),
        P("tp", "sub"),
        P("tp", None),
        P("own", None, "tp"),
        P("rep"),
        P(("rep", "own", "sub")),
    )
    return jax.shard_map(
        on_device,
        mesh=mesh,
        in_specs=placed,
        out_specs=(
            P(("rep", "own", "sub"), "tp"),
            P(("rep", "tp"), None),
            P(("rep", "own"), None, "tp"),
        ),
        check_vma=False,
    )
```

```python
import jax
import jax.numpy as jnp
from jax import lax
from jax.experimental import pallas as pl
from jax.experimental.pallas import tpu as pltpu
from jax.sharding import PartitionSpec as P

adapter_scale = 2.0
f32 = jnp.float32
bf16 = jnp.bfloat16

early_part = 3

(busy, first_cost, middling, filling, brief, slight) = (
    10**10, 5 * 10**9, 5 * 10**9, 10**10, 3 * 10**9, 15 * 10**8
)

anywhere = pl.BlockSpec(memory_space=pl.ANY)
in_hbm = pl.BlockSpec(memory_space=pltpu.HBM)
in_vmem = pl.BlockSpec(memory_space=pltpu.VMEM)
in_smem = pl.BlockSpec(memory_space=pltpu.SMEM)


def shift(x, axis, step):
    count = lax.axis_size(axis)
    return lax.ppermute(x, axis, [(i, (i + step) % count) for i in range(count)])


def swap(x, own_bit, sub_bit):
    subs = lax.axis_size("sub")
    whole = lax.axis_size("own") * subs
    other = own_bit * subs + sub_bit
    return lax.ppermute(x, ("own", "sub"), [(i, i ^ other) for i in range(whole)])


def width_of(features):
    return next(width for width in (512, 256, 128) if features % width == 0)


def stay(x):
    return pltpu.with_memory_space_constraint(x, pltpu.HBM)


def shape_of(dims, kind):
    return jax.ShapeDtypeStruct(dims, kind)


def call(body, operands, specs, outs, out_specs=None, after=(), flops=0, **more):
    count, idle = len(operands), len(after)

    def kernel(*refs):
        body(*refs[:count], *refs[count + idle :])

    moved = sum(x.size * x.dtype.itemsize for x in list(operands) + list(outs))
    return pl.pallas_call(
        kernel,
        out_shape=outs,
        in_specs=list(specs) + [anywhere] * len(after),
        out_specs=[in_vmem] * len(outs) if out_specs is None else out_specs,
        compiler_params=pltpu.CompilerParams(vmem_limit_bytes=24 * 1024 * 1024),
        cost_estimate=pl.CostEstimate(flops=flops, bytes_accessed=moved, transcendentals=0),
        **more,
    )(*operands, *after)


def pick_heads(adapter_ids, head_up, grad):
    per_owner, rank, width = head_up.shape
    own_count, sub_count = lax.axis_size("own"), lax.axis_size("sub")
    first = grad.shape[0] * early_part // 16

    def body(ids_far, head_up, grad, *refs):
        outs, early, away, ids, maps, sems = refs[:own_count], *refs[own_count:]
        own, sub = lax.axis_index("own"), lax.axis_index("sub")
        copies = [
            pltpu.make_async_copy(ids_far, ids, sems.at[0]),
            pltpu.make_async_copy(head_up, maps, sems.at[1]),
            pltpu.make_async_copy(grad.at[pl.ds(0, first)], early, sems.at[2]),
        ]
        for copy in copies:
            copy.start()
        copies[0].wait()
        copies[1].wait()
        for step in range(own_count):
            local = ids[(own ^ step) * sub_count + sub] - own * per_owner
            outs[step][...] = maps[jnp.clip(local, 0, per_owner - 1)]
        step = lax.div(ids[own * sub_count + sub], per_owner) ^ own
        away[...] = jnp.full(away.shape, step, jnp.int32)
        copies[2].wait()

    *picked, early, away = call(
        body,
        [stay(adapter_ids), stay(head_up), stay(grad)],
        [in_hbm] * 3,
        [shape_of((rank, width), bf16)] * own_count
        + [shape_of((first, grad.shape[1]), bf16), shape_of((8, 128), jnp.int32)],
        scratch_shapes=[
            pltpu.SMEM(adapter_ids.shape, jnp.int32),
            pltpu.VMEM(head_up.shape, bf16),
            pltpu.SemaphoreType.DMA((3,)),
        ],
        flops=first_cost,
    )
    return picked, early, away


def project_low(tokens, down, after):
    rows, features = tokens.shape
    rank = down.shape[0]

    def body(tokens, down, low):
        low[...] = lax.dot_general(
            down[...], tokens[...], (((1,), (1,)), ((), ())), preferred_element_type=f32
        )

    return call(
        body,
        [tokens, down],
        [in_vmem] * 2,
        [shape_of((rank, rows), f32)],
        after=after,
        flops=2 * rows * rank * features,
    )[0]


def rounded(x, after):
    def body(x, out):
        out[...] = x[...].astype(bf16)

    return call(body, [x], [in_vmem], [shape_of(x.shape, bf16)], after=after)[0]


def project_back(away, offered, steps, grad, after):
    rank, columns = offered[0].shape
    rows = grad.shape[0]

    def body(away, *refs):
        *offered, grad, part = refs
        step = jnp.broadcast_to(away[:1, :1], (rank, columns))
        head = offered[0][...].astype(f32)
        for at, block in zip(steps, offered[1:]):
            head = jnp.where(step == at, block[...].astype(f32), head)
        part[...] = lax.dot_general(
            head.astype(bf16), grad[...], (((1,), (1,)), ((), ())), preferred_element_type=f32
        )

    return call(
        body,
        [away, *offered, grad],
        [in_vmem] * (len(offered) + 2),
        [shape_of((rank, rows), f32)],
        after=after,
        flops=slight,
    )[0]


def head_term(lengths, lows, grad, scale, after):
    rank, rows = lows[0].shape
    columns = grad.shape[1]
    first = rows * early_part // 16

    def body(lengths, *refs):
        *lows, grad, term, late = refs
        total = lows[0][...]
        for low in lows[1:]:
            total = total + low[...].astype(f32)
        live = lax.broadcasted_iota(jnp.int32, total.shape, 1) < lengths[0]
        total = jnp.where(live, total, 0.0)
        kept = total.astype(bf16)
        rest = (total - kept.astype(f32)).astype(bf16)
        product = jnp.dot(kept, grad[...], preferred_element_type=f32)
        product += jnp.dot(rest, grad[...], preferred_element_type=f32)
        term[0] = (scale * product).astype(bf16)
        late[...] = grad[first:, :]

    return call(
        body,
        [lengths, *lows, grad],
        [in_smem] + [in_vmem] * (len(lows) + 1),
        [shape_of((1, rank, columns), bf16), shape_of((rows - first, columns), bf16)],
        after=after,
        flops=brief,
    )


def shared_terms(lengths, parts, tokens, scale, after):
    rows, features = tokens.shape
    rank = parts[0].shape[0]
    share = rank // 2

    def body(lengths, *refs):
        parts, (tokens, back, keep, send, total) = refs[:count], refs[count:]
        sub = lax.axis_index("sub")
        both = parts[0][...]
        for part in parts[1:]:
            both = both + part[...]
        live = lax.broadcasted_iota(jnp.int32, both.shape, 1) < lengths[0]
        back[...] = jnp.where(live, both, 0.0).astype(bf16)
        total[...] = scale * jnp.dot(back[...], tokens[...], preferred_element_type=f32)
        keep[...] = total[pl.ds(pl.multiple_of(sub * share, share), share), :]
        send[...] = total[pl.ds(pl.multiple_of((1 - sub) * share, share), share), :]

    count = len(parts)
    return call(
        body,
        [lengths, *parts, tokens],
        [in_smem] + [in_vmem] * (count + 1),
        [shape_of((rank, rows), bf16)] + [shape_of((share, features), f32)] * 2,
        after=after,
        scratch_shapes=[pltpu.VMEM((rank, features), f32)],
        flops=2 * rows * rank * features,
    )


def add_up(pieces, after=(), flops=0):
    def body(*refs):
        total = refs[0][...].astype(f32)
        for piece in refs[1:-1]:
            total = total + piece[...].astype(f32)
        refs[-1][...] = total.astype(bf16)

    return call(
        body,
        list(pieces),
        [in_vmem] * len(pieces),
        [shape_of(pieces[0].shape, bf16)],
        after=after,
        flops=flops,
    )[0]


def halve(pieces, bit, after=()):
    rows, features = pieces[0].shape
    half = rows // 2

    def body(*refs):
        total = refs[0][...].astype(f32)
        for piece in refs[1:-2]:
            total = total + piece[...].astype(f32)
        upper = lax.rem(lax.div(lax.axis_index("own"), bit), 2) == 1
        low, high = total[:half], total[half:]
        refs[-2][...] = jnp.where(upper, high, low)
        refs[-1][...] = jnp.where(upper, low, high).astype(bf16)

    return call(
        body,
        list(pieces),
        [in_vmem] * len(pieces),
        [shape_of((half, features), f32), shape_of((half, features), bf16)],
        after=after,
    )


def rejoin(mine, arrived, bit, after):
    rows, features = mine.shape

    def body(mine, arrived, out):
        upper = lax.rem(lax.div(lax.axis_index("own"), bit), 2) == 1
        one, two = mine[...].astype(f32), arrived[...].astype(f32)
        out[:rows] = jnp.where(upper, two, one).astype(bf16)
        out[rows:] = jnp.where(upper, one, two).astype(bf16)

    return call(
        body,
        [mine, arrived],
        [in_vmem] * 2,
        [shape_of((2 * rows, features), bf16)],
        after=after,
        flops=busy,
    )[0]


def lay_share(share, other, before, after):
    rows, features = share.shape
    held_in = [] if before is None else [before]

    def body(share, *refs):
        out, wide, sem = refs[len(held_in) :]
        sub = lax.axis_index("sub")
        side = 1 - sub if other else sub
        wide[...] = share[...].astype(f32)
        copy = pltpu.make_async_copy(
            wide, out.at[pl.ds(pl.multiple_of(side * rows, rows), rows)], sem
        )
        copy.start()
        copy.wait()

    return call(
        body,
        [share, *held_in],
        [in_vmem] + [in_hbm] * len(held_in),
        [shape_of((2 * rows, features), f32)],
        out_specs=[in_hbm],
        after=after,
        input_output_aliases={1: 0} if held_in else {},
        scratch_shapes=[pltpu.VMEM((rows, features), f32), pltpu.SemaphoreType.DMA],
    )[0]


def stack(pieces, after=(), flops=0):
    depths = [piece.shape[0] for piece in pieces]

    def body(*refs):
        at = 0
        for depth, piece in zip(depths, refs[:-1]):
            refs[-1][at : at + depth] = piece[...]
            at += depth

    return call(
        body,
        list(pieces),
        [in_vmem] * len(pieces),
        [shape_of((sum(depths),) + pieces[0].shape[1:], bf16)],
        after=after,
        flops=flops,
    )[0]


def clean(dims, after):
    def body(out, mark, held, sem):
        held[...] = jnp.zeros(held.shape, f32)
        mark[...] = jnp.zeros(mark.shape, f32)
        copies = [pltpu.make_async_copy(held, out.at[at], sem.at[at]) for at in range(dims[0])]
        for copy in copies:
            copy.start()
        for copy in copies:
            copy.wait()

    return call(
        body,
        [],
        [],
        [shape_of(dims, f32), shape_of((8, 128), f32)],
        out_specs=[in_hbm, in_vmem],
        after=after,
        scratch_shapes=[pltpu.VMEM(dims[1:], f32), pltpu.SemaphoreType.DMA((dims[0],))],
        flops=filling,
    )


def place_terms(adapter_ids, near, far, pattern, cleaned, after):
    per_owner, rank, columns = cleaned.shape
    sub_count = lax.axis_size("sub")

    def body(ids_far, near, far, cleaned, out, mark, held, ids, counts, sems):
        own, sub = lax.axis_index("own"), lax.axis_index("sub")
        fetch = pltpu.make_async_copy(ids_far, ids, sems.at[per_owner])
        fetch.start()
        mark[...] = jnp.zeros(mark.shape, f32)
        for local in range(per_owner):
            counts[local] = 0
        fetch.wait()
        for at, step in enumerate(pattern):
            for side in range(sub_count):
                local = ids[(own ^ step) * sub_count + side] - own * per_owner

                @pl.when(jnp.logical_and(local >= 0, local < per_owner))
                def _():
                    term = jnp.where(sub == side, near[at], far[at]).astype(f32)

                    @pl.when(counts[local] == 0)
                    def _():
                        held[local] = term

                    @pl.when(counts[local] > 0)
                    def _():
                        held[local] += term

                    counts[local] += 1

        copies = [
            pltpu.make_async_copy(held.at[local], out.at[local], sems.at[local])
            for local in range(per_owner)
        ]
        for local, copy in enumerate(copies):
            pl.when(counts[local] > 0)(copy.start)
        for local, copy in enumerate(copies):
            pl.when(counts[local] > 0)(copy.wait)

    return call(
        body,
        [stay(adapter_ids), near, far, cleaned],
        [in_hbm, in_vmem, in_vmem, in_hbm],
        [shape_of(cleaned.shape, f32), shape_of((8, 128), f32)],
        out_specs=[in_hbm, in_vmem],
        after=after,
        input_output_aliases={3: 0},
        scratch_shapes=[
            pltpu.VMEM(cleaned.shape, f32),
            pltpu.SMEM(adapter_ids.shape, jnp.int32),
            pltpu.SMEM((per_owner,), jnp.int32),
            pltpu.SemaphoreType.DMA((per_owner + 1,)),
        ],
    )


def arrange(lengths, grad, pieces, after):
    rows, columns = grad.shape
    count = 1 + len(pieces)
    first = rows * early_part // 16

    def body(lengths, grad, *refs):
        pieces, kept = refs[:-1], refs[-1]
        at = lax.axis_index("tp")
        live = lax.broadcasted_iota(jnp.int32, (rows, columns), 0) < lengths[0]
        zero = jnp.zeros((rows, columns), bf16)
        place = pl.multiple_of(at * columns, 128)
        kept[:, pl.ds(place, columns)] = jnp.where(live, grad[...], zero)
        for step in range(1, count):
            place = pl.multiple_of(lax.rem(at + count - step, count) * columns, 128)
            early, late = pieces[2 * step - 2 : 2 * step]
            kept[:first, pl.ds(place, columns)] = jnp.where(live[:first], early[...], zero[:first])
            kept[first:, pl.ds(place, columns)] = jnp.where(live[first:], late[...], zero[first:])

    flat = [x for pair in pieces for x in pair]
    return call(
        body,
        [lengths, grad, *flat],
        [in_smem] + [in_vmem] * (1 + len(flat)),
        [shape_of((rows, count * columns), bf16)],
        after=after,
    )[0]


def input_side(kept, frozen, frozen_other, back, down, begin, count, before, after):
    rows = kept.shape[0]
    features, half = frozen.shape
    width = width_of(features)
    held_in = [] if before is None else [before]

    def body(kept, frozen, frozen_other, back, down, *refs):
        out, mark, held, sems = refs[len(held_in) :]
        mark[...] = jnp.zeros(mark.shape, f32)
        sub = lax.axis_index("sub")
        both = (((1,), (1,)), ((), ()))
        mine = kept[:, pl.ds(pl.multiple_of(sub * half, 128), half)]
        other = kept[:, pl.ds(pl.multiple_of((1 - sub) * half, 128), half)]
        twice = adapter_scale * back[...]
        copies = []
        for at in range(count):
            here = slice((begin + at) * width, (begin + at + 1) * width)
            total = lax.dot_general(mine, frozen[here, :], both, preferred_element_type=f32)
            total += lax.dot_general(other, frozen_other[here, :], both, preferred_element_type=f32)
            total += lax.dot_general(
                twice, down[:, here], (((0,), (0,)), ((), ())), preferred_element_type=f32
            )
            there = slice(at * width, (at + 1) * width)
            held[:, there] = total.astype(bf16)
            copies.append(
                pltpu.make_async_copy(held.at[:, there], out.at[:, here], sems.at[at])
            )
            copies[-1].start()
        for copy in copies:
            copy.wait()

    return call(
        body,
        [kept, frozen, frozen_other, back, down, *held_in],
        [in_vmem] * 5 + [in_hbm] * len(held_in),
        [shape_of((rows, features), bf16), shape_of((8, 128), f32)],
        out_specs=[in_hbm, in_vmem],
        after=after,
        input_output_aliases={5: 0} if held_in else {},
        scratch_shapes=[
            pltpu.VMEM((rows, count * width), bf16),
            pltpu.SemaphoreType.DMA((count,)),
        ],
        flops=2 * rows * width * count * (2 * half + back.shape[0]),
    )


def on_device(tokens, grad_output, frozen_value, shared_down, head_up, adapter_ids, lengths):
    rows, features = tokens.shape
    own_count = lax.axis_size("own")
    tp_count = lax.axis_size("tp")
    per_owner = head_up.shape[0]
    scale = adapter_scale / rows
    tp_steps, own_steps = range(1, tp_count), range(1, own_count)

    frozen_other = shift(frozen_value, "sub", 1)
    picked, early, away = pick_heads(adapter_ids, head_up, grad_output)
    steps = sorted(own_steps, key=lambda step: (-step.bit_length(), step))
    offered = [picked[0]] + [swap(picked[step], step, 0) for step in steps]
    early_grads = [shift(early, "tp", step) for step in tp_steps]

    down = shared_down.T
    low = project_low(tokens, down, picked[:1])
    sent = rounded(low, [frozen_other])
    lows = [low] + [shift(sent, "tp", step) for step in tp_steps]

    part = project_back(away, offered, steps, grad_output, [low])
    parts = [part] + [shift(part, "tp", step) for step in tp_steps]

    near, late = head_term(lengths, lows, grad_output, scale, [part, *early_grads])
    late_grads = [shift(late, "tp", step) for step in tp_steps]
    back, keep, send = shared_terms(lengths, parts, tokens, scale, [near])
    pieces = [keep, shift(send, "sub", 1)]
    met = stack([near], [back], flops=middling)
    terms = [near] + [swap(met if step == 1 else near, step, 0) for step in steps[::-1]]

    bits = [1 << i for i in range(own_count.bit_length() - 1)]
    mark = back
    for bit in bits[:-1]:
        stays, leaves = halve(pieces, bit, [mark])
        pieces = [stays, swap(leaves, bit, 0)]
        mark = leaves
    cleaned, mark = clean((per_owner,) + near.shape[1:], [mark])
    near = stack(terms, [mark])
    far = shift(near, "sub", 1)
    total = add_up(pieces, [near], flops=busy)
    grad_heads, mark = place_terms(
        adapter_ids, near, far, [0] + steps[::-1], cleaned, [total]
    )
    kept = arrange(lengths, grad_output, list(zip(early_grads, late_grads)), [mark])
    sides = (frozen_value, frozen_other, back, down)
    blocks = features // width_of(features)
    cut = max(1, blocks * 2 // 5)
    input_gradient, mark = input_side(kept, *sides, 0, cut, None, [mark])
    if bits:
        total = add_up([total, swap(total, bits[-1], 0)], [mark])
    if blocks > cut:
        input_gradient, mark = input_side(
            kept, *sides, cut, blocks - cut, input_gradient, [total]
        )
    for bit in reversed(bits[:-1]):
        total = rejoin(total, swap(total, bit, 0), bit, [mark])
        mark = total
    laid = lay_share(total, False, None, [mark])
    shared_down_gradient = lay_share(shift(total, "sub", 1), True, laid, []).T
    return (input_gradient, shared_down_gradient, grad_heads)


def solution(mesh):
    placed = (
        P(("rep", "own", "sub"), "tp"),
        P(("rep", "own", "sub"), "tp"),
        P("tp", "sub"),
        P("tp", None),
        P("own", None, "tp"),
        P("rep"),
        P(("rep", "own", "sub")),
    )
    return jax.shard_map(
        on_device,
        mesh=mesh,
        in_specs=placed,
        out_specs=(
            P(("rep", "own", "sub"), "tp"),
            P(("rep", "tp"), None),
            P(("rep", "own"), None, "tp"),
        ),
        check_vma=False,
    )
```

```python
import jax
import jax.numpy as jnp
from jax import lax
from jax.experimental import pallas as pl
from jax.experimental.pallas import tpu as pltpu
from jax.sharding import PartitionSpec as P

adapter_scale = 2.0
f32 = jnp.float32
bf16 = jnp.bfloat16

early_part = 2

(busy, first_cost, middling, filling, brief, slight) = (
    10**10, 5 * 10**9, 5 * 10**9, 10**10, 3 * 10**9, 15 * 10**8
)

anywhere = pl.BlockSpec(memory_space=pl.ANY)
in_hbm = pl.BlockSpec(memory_space=pltpu.HBM)
in_vmem = pl.BlockSpec(memory_space=pltpu.VMEM)
in_smem = pl.BlockSpec(memory_space=pltpu.SMEM)


def shift(x, axis, step):
    count = lax.axis_size(axis)
    return lax.ppermute(x, axis, [(i, (i + step) % count) for i in range(count)])


def swap(x, own_bit, sub_bit):
    subs = lax.axis_size("sub")
    whole = lax.axis_size("own") * subs
    other = own_bit * subs + sub_bit
    return lax.ppermute(x, ("own", "sub"), [(i, i ^ other) for i in range(whole)])


def width_of(features):
    return next(width for width in (512, 256, 128) if features % width == 0)


def stay(x):
    return pltpu.with_memory_space_constraint(x, pltpu.HBM)


def shape_of(dims, kind):
    return jax.ShapeDtypeStruct(dims, kind)


def call(body, operands, specs, outs, out_specs=None, after=(), flops=0, **more):
    count, idle = len(operands), len(after)

    def kernel(*refs):
        body(*refs[:count], *refs[count + idle :])

    moved = sum(x.size * x.dtype.itemsize for x in list(operands) + list(outs))
    return pl.pallas_call(
        kernel,
        out_shape=outs,
        in_specs=list(specs) + [anywhere] * len(after),
        out_specs=[in_vmem] * len(outs) if out_specs is None else out_specs,
        compiler_params=pltpu.CompilerParams(vmem_limit_bytes=24 * 1024 * 1024),
        cost_estimate=pl.CostEstimate(flops=flops, bytes_accessed=moved, transcendentals=0),
        **more,
    )(*operands, *after)


def pick_heads(adapter_ids, head_up, grad):
    per_owner, rank, width = head_up.shape
    own_count, sub_count = lax.axis_size("own"), lax.axis_size("sub")
    first = grad.shape[0] * early_part // 16

    def body(ids_far, head_up, grad, *refs):
        outs, early, away, ids, maps, sems = refs[:own_count], *refs[own_count:]
        own, sub = lax.axis_index("own"), lax.axis_index("sub")
        copies = [
            pltpu.make_async_copy(ids_far, ids, sems.at[0]),
            pltpu.make_async_copy(head_up, maps, sems.at[1]),
            pltpu.make_async_copy(grad.at[pl.ds(0, first)], early, sems.at[2]),
        ]
        for copy in copies:
            copy.start()
        copies[0].wait()
        copies[1].wait()
        for step in range(own_count):
            local = ids[(own ^ step) * sub_count + sub] - own * per_owner
            outs[step][...] = maps[jnp.clip(local, 0, per_owner - 1)]
        step = lax.div(ids[own * sub_count + sub], per_owner) ^ own
        away[...] = jnp.full(away.shape, step, jnp.int32)
        copies[2].wait()

    *picked, early, away = call(
        body,
        [stay(adapter_ids), stay(head_up), stay(grad)],
        [in_hbm] * 3,
        [shape_of((rank, width), bf16)] * own_count
        + [shape_of((first, grad.shape[1]), bf16), shape_of((8, 128), jnp.int32)],
        scratch_shapes=[
            pltpu.SMEM(adapter_ids.shape, jnp.int32),
            pltpu.VMEM(head_up.shape, bf16),
            pltpu.SemaphoreType.DMA((3,)),
        ],
        flops=first_cost,
    )
    return picked, early, away


def project_low(tokens, down, after):
    rows, features = tokens.shape
    rank = down.shape[0]

    def body(tokens, down, low):
        low[...] = lax.dot_general(
            down[...], tokens[...], (((1,), (1,)), ((), ())), preferred_element_type=f32
        )

    return call(
        body,
        [tokens, down],
        [in_vmem] * 2,
        [shape_of((rank, rows), f32)],
        after=after,
        flops=2 * rows * rank * features,
    )[0]


def rounded(x, after):
    def body(x, out):
        out[...] = x[...].astype(bf16)

    return call(body, [x], [in_vmem], [shape_of(x.shape, bf16)], after=after)[0]


def project_back(away, offered, steps, grad, after):
    rank, columns = offered[0].shape
    rows = grad.shape[0]

    def body(away, *refs):
        *offered, grad, part = refs
        step = jnp.broadcast_to(away[:1, :1], (rank, columns))
        head = offered[0][...].astype(f32)
        for at, block in zip(steps, offered[1:]):
            head = jnp.where(step == at, block[...].astype(f32), head)
        part[...] = lax.dot_general(
            head.astype(bf16), grad[...], (((1,), (1,)), ((), ())), preferred_element_type=f32
        )

    return call(
        body,
        [away, *offered, grad],
        [in_vmem] * (len(offered) + 2),
        [shape_of((rank, rows), f32)],
        after=after,
        flops=slight,
    )[0]


def head_term(lengths, lows, grad, scale, after):
    rank, rows = lows[0].shape
    columns = grad.shape[1]
    first = rows * early_part // 16

    def body(lengths, *refs):
        *lows, grad, term, late = refs
        total = lows[0][...]
        for low in lows[1:]:
            total = total + low[...].astype(f32)
        live = lax.broadcasted_iota(jnp.int32, total.shape, 1) < lengths[0]
        total = jnp.where(live, total, 0.0)
        kept = total.astype(bf16)
        rest = (total - kept.astype(f32)).astype(bf16)
        product = jnp.dot(kept, grad[...], preferred_element_type=f32)
        product += jnp.dot(rest, grad[...], preferred_element_type=f32)
        term[0] = (scale * product).astype(bf16)
        late[...] = grad[first:, :]

    return call(
        body,
        [lengths, *lows, grad],
        [in_smem] + [in_vmem] * (len(lows) + 1),
        [shape_of((1, rank, columns), bf16), shape_of((rows - first, columns), bf16)],
        after=after,
        flops=brief,
    )


def shared_terms(lengths, parts, tokens, scale, after):
    rows, features = tokens.shape
    rank = parts[0].shape[0]
    share = rank // 2

    def body(lengths, *refs):
        parts, (tokens, back, keep, send, total) = refs[:count], refs[count:]
        sub = lax.axis_index("sub")
        both = parts[0][...]
        for part in parts[1:]:
            both = both + part[...]
        live = lax.broadcasted_iota(jnp.int32, both.shape, 1) < lengths[0]
        back[...] = jnp.where(live, both, 0.0).astype(bf16)
        total[...] = scale * jnp.dot(back[...], tokens[...], preferred_element_type=f32)
        keep[...] = total[pl.ds(pl.multiple_of(sub * share, share), share), :]
        send[...] = total[pl.ds(pl.multiple_of((1 - sub) * share, share), share), :]

    count = len(parts)
    return call(
        body,
        [lengths, *parts, tokens],
        [in_smem] + [in_vmem] * (count + 1),
        [shape_of((rank, rows), bf16)] + [shape_of((share, features), f32)] * 2,
        after=after,
        scratch_shapes=[pltpu.VMEM((rank, features), f32)],
        flops=2 * rows * rank * features,
    )


def add_up(pieces, after=(), flops=0):
    def body(*refs):
        total = refs[0][...].astype(f32)
        for piece in refs[1:-1]:
            total = total + piece[...].astype(f32)
        refs[-1][...] = total.astype(bf16)

    return call(
        body,
        list(pieces),
        [in_vmem] * len(pieces),
        [shape_of(pieces[0].shape, bf16)],
        after=after,
        flops=flops,
    )[0]


def halve(pieces, bit, after=()):
    rows, features = pieces[0].shape
    half = rows // 2

    def body(*refs):
        total = refs[0][...].astype(f32)
        for piece in refs[1:-2]:
            total = total + piece[...].astype(f32)
        upper = lax.rem(lax.div(lax.axis_index("own"), bit), 2) == 1
        low, high = total[:half], total[half:]
        refs[-2][...] = jnp.where(upper, high, low)
        refs[-1][...] = jnp.where(upper, low, high).astype(bf16)

    return call(
        body,
        list(pieces),
        [in_vmem] * len(pieces),
        [shape_of((half, features), f32), shape_of((half, features), bf16)],
        after=after,
    )


def rejoin(mine, arrived, bit, after):
    rows, features = mine.shape

    def body(mine, arrived, out):
        upper = lax.rem(lax.div(lax.axis_index("own"), bit), 2) == 1
        one, two = mine[...].astype(f32), arrived[...].astype(f32)
        out[:rows] = jnp.where(upper, two, one).astype(bf16)
        out[rows:] = jnp.where(upper, one, two).astype(bf16)

    return call(
        body,
        [mine, arrived],
        [in_vmem] * 2,
        [shape_of((2 * rows, features), bf16)],
        after=after,
        flops=busy,
    )[0]


def lay_share(share, other, before, after):
    rows, features = share.shape
    held_in = [] if before is None else [before]

    def body(share, *refs):
        out, wide, sem = refs[len(held_in) :]
        sub = lax.axis_index("sub")
        side = 1 - sub if other else sub
        wide[...] = share[...].astype(f32)
        copy = pltpu.make_async_copy(
            wide, out.at[pl.ds(pl.multiple_of(side * rows, rows), rows)], sem
        )
        copy.start()
        copy.wait()

    return call(
        body,
        [share, *held_in],
        [in_vmem] + [in_hbm] * len(held_in),
        [shape_of((2 * rows, features), f32)],
        out_specs=[in_hbm],
        after=after,
        input_output_aliases={1: 0} if held_in else {},
        scratch_shapes=[pltpu.VMEM((rows, features), f32), pltpu.SemaphoreType.DMA],
    )[0]


def stack(pieces, after=(), flops=0):
    depths = [piece.shape[0] for piece in pieces]

    def body(*refs):
        at = 0
        for depth, piece in zip(depths, refs[:-1]):
            refs[-1][at : at + depth] = piece[...]
            at += depth

    return call(
        body,
        list(pieces),
        [in_vmem] * len(pieces),
        [shape_of((sum(depths),) + pieces[0].shape[1:], bf16)],
        after=after,
        flops=flops,
    )[0]


def clean(dims, after):
    def body(out, mark, held, sem):
        held[...] = jnp.zeros(held.shape, f32)
        mark[...] = jnp.zeros(mark.shape, f32)
        copies = [pltpu.make_async_copy(held, out.at[at], sem.at[at]) for at in range(dims[0])]
        for copy in copies:
            copy.start()
        for copy in copies:
            copy.wait()

    return call(
        body,
        [],
        [],
        [shape_of(dims, f32), shape_of((8, 128), f32)],
        out_specs=[in_hbm, in_vmem],
        after=after,
        scratch_shapes=[pltpu.VMEM(dims[1:], f32), pltpu.SemaphoreType.DMA((dims[0],))],
        flops=filling,
    )


def place_terms(adapter_ids, near, far, pattern, cleaned, after):
    per_owner, rank, columns = cleaned.shape
    sub_count = lax.axis_size("sub")

    def body(ids_far, near, far, cleaned, out, mark, held, ids, counts, sems):
        own, sub = lax.axis_index("own"), lax.axis_index("sub")
        fetch = pltpu.make_async_copy(ids_far, ids, sems.at[per_owner])
        fetch.start()
        mark[...] = jnp.zeros(mark.shape, f32)
        for local in range(per_owner):
            counts[local] = 0
        fetch.wait()
        for at, step in enumerate(pattern):
            for side in range(sub_count):
                local = ids[(own ^ step) * sub_count + side] - own * per_owner

                @pl.when(jnp.logical_and(local >= 0, local < per_owner))
                def _():
                    term = jnp.where(sub == side, near[at], far[at]).astype(f32)

                    @pl.when(counts[local] == 0)
                    def _():
                        held[local] = term

                    @pl.when(counts[local] > 0)
                    def _():
                        held[local] += term

                    counts[local] += 1

        copies = [
            pltpu.make_async_copy(held.at[local], out.at[local], sems.at[local])
            for local in range(per_owner)
        ]
        for local, copy in enumerate(copies):
            pl.when(counts[local] > 0)(copy.start)
        for local, copy in enumerate(copies):
            pl.when(counts[local] > 0)(copy.wait)

    return call(
        body,
        [stay(adapter_ids), near, far, cleaned],
        [in_hbm, in_vmem, in_vmem, in_hbm],
        [shape_of(cleaned.shape, f32), shape_of((8, 128), f32)],
        out_specs=[in_hbm, in_vmem],
        after=after,
        input_output_aliases={3: 0},
        scratch_shapes=[
            pltpu.VMEM(cleaned.shape, f32),
            pltpu.SMEM(adapter_ids.shape, jnp.int32),
            pltpu.SMEM((per_owner,), jnp.int32),
            pltpu.SemaphoreType.DMA((per_owner + 1,)),
        ],
    )


def arrange(lengths, grad, pieces, after):
    rows, columns = grad.shape
    count = 1 + len(pieces)
    first = rows * early_part // 16

    def body(lengths, grad, *refs):
        pieces, kept = refs[:-1], refs[-1]
        at = lax.axis_index("tp")
        live = lax.broadcasted_iota(jnp.int32, (rows, columns), 0) < lengths[0]
        zero = jnp.zeros((rows, columns), bf16)
        place = pl.multiple_of(at * columns, 128)
        kept[:, pl.ds(place, columns)] = jnp.where(live, grad[...], zero)
        for step in range(1, count):
            place = pl.multiple_of(lax.rem(at + count - step, count) * columns, 128)
            early, late = pieces[2 * step - 2 : 2 * step]
            kept[:first, pl.ds(place, columns)] = jnp.where(live[:first], early[...], zero[:first])
            kept[first:, pl.ds(place, columns)] = jnp.where(live[first:], late[...], zero[first:])

    flat = [x for pair in pieces for x in pair]
    return call(
        body,
        [lengths, grad, *flat],
        [in_smem] + [in_vmem] * (1 + len(flat)),
        [shape_of((rows, count * columns), bf16)],
        after=after,
    )[0]


def input_side(kept, frozen, frozen_other, back, down, begin, count, before, after):
    rows = kept.shape[0]
    features, half = frozen.shape
    width = width_of(features)
    held_in = [] if before is None else [before]

    def body(kept, frozen, frozen_other, back, down, *refs):
        out, mark, held, sems = refs[len(held_in) :]
        mark[...] = jnp.zeros(mark.shape, f32)
        sub = lax.axis_index("sub")
        both = (((1,), (1,)), ((), ()))
        mine = kept[:, pl.ds(pl.multiple_of(sub * half, 128), half)]
        other = kept[:, pl.ds(pl.multiple_of((1 - sub) * half, 128), half)]
        twice = adapter_scale * back[...]
        copies = []
        for at in range(count):
            here = slice((begin + at) * width, (begin + at + 1) * width)
            total = lax.dot_general(mine, frozen[here, :], both, preferred_element_type=f32)
            total += lax.dot_general(other, frozen_other[here, :], both, preferred_element_type=f32)
            total += lax.dot_general(
                twice, down[:, here], (((0,), (0,)), ((), ())), preferred_element_type=f32
            )
            there = slice(at * width, (at + 1) * width)
            held[:, there] = total.astype(bf16)
            copies.append(
                pltpu.make_async_copy(held.at[:, there], out.at[:, here], sems.at[at])
            )
            copies[-1].start()
        for copy in copies:
            copy.wait()

    return call(
        body,
        [kept, frozen, frozen_other, back, down, *held_in],
        [in_vmem] * 5 + [in_hbm] * len(held_in),
        [shape_of((rows, features), bf16), shape_of((8, 128), f32)],
        out_specs=[in_hbm, in_vmem],
        after=after,
        input_output_aliases={5: 0} if held_in else {},
        scratch_shapes=[
            pltpu.VMEM((rows, count * width), bf16),
            pltpu.SemaphoreType.DMA((count,)),
        ],
        flops=2 * rows * width * count * (2 * half + back.shape[0]),
    )


def on_device(tokens, grad_output, frozen_value, shared_down, head_up, adapter_ids, lengths):
    rows, features = tokens.shape
    own_count = lax.axis_size("own")
    tp_count = lax.axis_size("tp")
    per_owner = head_up.shape[0]
    scale = adapter_scale / rows
    tp_steps, own_steps = range(1, tp_count), range(1, own_count)

    frozen_other = shift(frozen_value, "sub", 1)
    picked, early, away = pick_heads(adapter_ids, head_up, grad_output)
    steps = sorted(own_steps, key=lambda step: (-step.bit_length(), step))
    offered = [picked[0]] + [swap(picked[step], step, 0) for step in steps]
    early_grads = [shift(early, "tp", step) for step in tp_steps]

    down = shared_down.T
    low = project_low(tokens, down, picked[:1])
    sent = rounded(low, [frozen_other])
    lows = [low] + [shift(sent, "tp", step) for step in tp_steps]

    part = project_back(away, offered, steps, grad_output, [low])
    parts = [part] + [shift(part, "tp", step) for step in tp_steps]

    near, late = head_term(lengths, lows, grad_output, scale, [part, *early_grads])
    late_grads = [shift(late, "tp", step) for step in tp_steps]
    back, keep, send = shared_terms(lengths, parts, tokens, scale, [near])
    pieces = [keep, shift(send, "sub", 1)]
    met = stack([near], [back], flops=middling)
    terms = [near] + [swap(met if step == 1 else near, step, 0) for step in steps[::-1]]

    bits = [1 << i for i in range(own_count.bit_length() - 1)]
    mark = back
    for bit in bits[:-1]:
        stays, leaves = halve(pieces, bit, [mark])
        pieces = [stays, swap(leaves, bit, 0)]
        mark = leaves
    cleaned, mark = clean((per_owner,) + near.shape[1:], [mark])
    near = stack(terms, [mark])
    far = shift(near, "sub", 1)
    total = add_up(pieces, [near], flops=busy)
    grad_heads, mark = place_terms(
        adapter_ids, near, far, [0] + steps[::-1], cleaned, [total]
    )
    kept = arrange(lengths, grad_output, list(zip(early_grads, late_grads)), [mark])
    sides = (frozen_value, frozen_other, back, down)
    blocks = features // width_of(features)
    cut = max(1, blocks * 2 // 5)
    input_gradient, mark = input_side(kept, *sides, 0, cut, None, [mark])
    if bits:
        total = add_up([total, swap(total, bits[-1], 0)], [mark])
    if blocks > cut:
        input_gradient, mark = input_side(
            kept, *sides, cut, blocks - cut, input_gradient, [total]
        )
    for bit in reversed(bits[:-1]):
        total = rejoin(total, swap(total, bit, 0), bit, [mark])
        mark = total
    laid = lay_share(total, False, None, [mark])
    shared_down_gradient = lay_share(shift(total, "sub", 1), True, laid, []).T
    return (input_gradient, shared_down_gradient, grad_heads)


def solution(mesh):
    placed = (
        P(("rep", "own", "sub"), "tp"),
        P(("rep", "own", "sub"), "tp"),
        P("tp", "sub"),
        P("tp", None),
        P("own", None, "tp"),
        P("rep"),
        P(("rep", "own", "sub")),
    )
    return jax.shard_map(
        on_device,
        mesh=mesh,
        in_specs=placed,
        out_specs=(
            P(("rep", "own", "sub"), "tp"),
            P(("rep", "tp"), None),
            P(("rep", "own"), None, "tp"),
        ),
        check_vma=False,
    )
```
